512 devices in a mesh: dp: 8 (over z_hi, core), expert: 64 (over x, y, z_lo).
Axes of the slice: x: 4, y: 8, z: 8 (z_hi: 4, z_lo: 2; z = z_hi * 2 + z_lo), core: 2. Of those that a mesh axis runs over, the one named last changes fastest.
Arguments:
- tokens: bfloat16 [2048, 3584], P('expert', 'dp'), may hold values from -6 to 6
- cotangent: bfloat16 [2048, 3584], P('expert', 'dp'), may hold values from -6 to 6
- expert_ids: int32 [2048, 8], P('expert'), may hold values from 0 to 63, all different within a row; in each aligned block of 32 rows (0 to 31, 32 to 63, ...) at most 10 rows name the same one
- route_weight: float32 [2048, 8], P('expert'), may hold values from 0.05 to 0.4
- replaced: int32 [1], replicated, may hold values from 0 to 63
- gate_weight: bfloat16 [64, 3584, 1024], P('expert', 'dp'), may hold values from -0.09375 to 0.09375
- up_weight: bfloat16 [64, 3584, 1024], P('expert', 'dp'), may hold values from -0.09375 to 0.09375
- down_weight: bfloat16 [64, 1024, 3584], P('expert', None, 'dp'), may hold values from -0.1875 to 0.1875
- backup: bfloat16 [3, 3584, 1024], P(None, 'dp', 'expert'), may hold values from -0.09375 to 0.09375
Outputs:
- combined: bfloat16 [2048, 3584], P('expert', 'dp')
- token_grad: bfloat16 [2048, 3584], P('expert', 'dp')
- gate_grad: bfloat16 [64, 3584, 1024], P('expert', 'dp')
- up_grad: bfloat16 [64, 3584, 1024], P('expert', 'dp')
The draws below stay inside these ranges and needn't reach their ends.
Inputs may be any that keep to these rules, and one draw needn't show every extreme that they name: `expert_ids`: each row names 8 different experts. In each aligned block of 32 rows (the tokens of one expert-parallel rank) no expert is named by more than 10 rows, a bound that some block reaches.
All inputs are finite; a program needn't handle non-finite values.
Results may differ from the reference program's by a relative error of at most 0.029.
Values may be sent and summed in bfloat16 or wider, within the bound.
No kernel may reach another device: no remote copies, remote signals or barrier semaphores. Data moves between devices by JAX's collectives and lax.ppermute only.
A program may use at most 64 MiB of HBM per device.

```python
import math
import jax
import jax.numpy as jnp
import numpy as np
from jax import lax

D = 3584
FF = 1024
TOPK = 8
TOK_DEV = 32
EXPERTS = 64
TOKENS = 2048
CAP = 10
N_DP = 8


def steps_of(rng, dims, cuts, least, high):
    def one(axis_at, parts):
        heights = jax.random.uniform(jax.random.fold_in(jax.random.fold_in(rng, 6), axis_at), (parts,), jnp.float32, least / len(cuts), high / len(cuts))
        return jnp.repeat(jnp.exp(heights), dims[axis_at] // parts).reshape((-1,) + (1,) * (len(dims) - axis_at - 1))

    level = one(*cuts[0])
    for cut in cuts[1:]:
        level = level * one(*cut)
    return level


def shared_out(key, own, number, rows, amount, top, reach, lean):
    sequence = jax.random.permutation(key, amount)
    crowded, ordinary = load_shares(amount, rows * top, reach, lean, True), load_shares(amount, rows * top, reach, lean, False)
    places = jnp.arange(amount)

    def named(sizes, rotation):
        used = int((sizes > 0).sum())
        fixed = max(1, used // 4)
        passed = fixed + (places - fixed + rotation * (used - fixed)) % max(1, amount - fixed)
        return jnp.zeros((amount,), jnp.int32).at[sequence[jnp.where(places < fixed, places, passed)]].set(jnp.asarray(sizes, jnp.int32))

    sizes = jnp.where(number % 4 == 0, named(crowded, number // 4), named(ordinary, number - number // 4 - 1))
    mixed = jax.random.permutation(jax.random.fold_in(own, 3), amount)
    source_of, receiver = mixed[0:amount // 2 * 2:2], mixed[1:amount // 2 * 2:2]
    room = jnp.minimum(sizes[source_of] - 1, reach - sizes[receiver]) // 2
    room = jnp.where((source_of == sequence[0]) | (receiver == sequence[0]) | (sizes[receiver] == 0), 0, jnp.maximum(room, 0))
    passed = jax.random.randint(jax.random.fold_in(own, 4), (amount // 2,), 0, 1 << 20) % (room + 1)
    sizes = sizes.at[source_of].add(-passed).at[receiver].add(passed)
    labels = jnp.searchsorted(jnp.cumsum(sizes), jnp.arange(rows * top), side="right").astype(jnp.int32)
    table = labels.reshape(top, rows).T
    table = table[jax.random.permutation(jax.random.fold_in(own, 1), rows)]
    rotation = jax.random.randint(jax.random.fold_in(own, 2), (rows, 1), 0, top)
    return jnp.take_along_axis(table, (jnp.arange(top)[None, :] + rotation) % top, axis=1)


def load_shares(count, total, most, skew, full):
    weights = [(1 << 20) // math.isqrt(rank ** skew) + 1 for rank in range(1, count + 1)]
    largest = most if full else min(most, max(-(-total // count), total * weights[0] // sum(weights)))
    least = 1 if total - largest >= count - 1 else 0
    holding, rest = [largest] + [least] * (count - 1), total - largest - least * (count - 1)
    while rest > 0:
        free = [i for i in range(1, count) if holding[i] < largest] or [i for i in range(1, count) if holding[i] < most]
        mass, budget = sum([weights[i] for i in free]), rest
        for i in free:
            extra = min(most - holding[i], max(1, budget * weights[i] // mass), rest)
            holding[i] = holding[i] + extra
            rest = rest - extra
    return np.array(holding)


def scatter_about(own_key, extent, deviation, most, split=(), kind=jnp.bfloat16):
    entries = deviation * jax.random.normal(own_key, extent, jnp.float32)
    if split:
        entries = entries * steps_of(own_key, extent, split, -0.22, 0.18)
    return jnp.clip(entries, -most, most).astype(kind)


def setup_inputs(seed: int = 0) -> dict:
    key_of = jax.random.split(jax.random.key(seed), 10)
    tokens = scatter_about(key_of[0], (TOKENS, D), 1.0, 6.0, ((0, 64), (1, 8)))
    cotangent = scatter_about(key_of[1], (TOKENS, D), 1.0, 6.0, ((0, 64), (1, 8)))
    expert_ids_keys = jax.random.split(jax.random.fold_in(key_of[2], 1), TOKENS // TOK_DEV)
    expert_ids_turns = jax.random.permutation(jax.random.fold_in(key_of[2], 3), TOKENS // TOK_DEV)
    expert_ids = jax.vmap(lambda own, number: shared_out(jax.random.fold_in(key_of[2], 2), own, number, TOK_DEV, EXPERTS, TOPK, CAP, 2))(expert_ids_keys, expert_ids_turns).reshape((TOKENS, TOPK))
    route_weight = jnp.clip(jnp.exp(math.log(0.4) - 2.0794415 * jax.random.uniform(key_of[3], (TOKENS, TOPK), jnp.float32) ** steps_of(key_of[3], (TOKENS, TOPK), ((0, 64),), -0.2, 0.2)), 0.05, 0.4)
    replaced = jax.random.randint(key_of[4], (1,), 0, EXPERTS).astype(jnp.int32)
    gate_weight = scatter_about(key_of[5], (EXPERTS, D, FF), D ** -0.5, 0.09375, ((0, 64), (1, 8)))
    up_weight = scatter_about(key_of[6], (EXPERTS, D, FF), D ** -0.5, 0.09375, ((0, 64), (1, 8)))
    down_weight = scatter_about(key_of[7], (EXPERTS, FF, D), FF ** -0.5, 0.1875, ((0, 64), (2, 8)))
    backup = scatter_about(key_of[8], (3, D, FF), D ** -0.5, 0.09375, ((1, 8), (2, 64)))
    return dict(tokens=tokens, cotangent=cotangent, expert_ids=expert_ids, route_weight=route_weight, replaced=replaced, gate_weight=gate_weight, up_weight=up_weight, down_weight=down_weight, backup=backup)


def block_sum(left, right, pattern):
    terms = jnp.einsum(pattern, left, right)
    terms = lax.optimization_barrier(terms.astype(jnp.bfloat16))
    return jnp.sum(terms.astype(jnp.float32), axis=0)


def reference(tokens, cotangent, expert_ids, route_weight, replaced, gate_weight, up_weight, down_weight, backup):
    slots = EXPERTS * CAP
    part = D // N_DP
    target = replaced[0]

    def one_expert(carry, expert):
        out_acc, grad_acc = carry
        chosen = expert_ids == expert
        member = jnp.any(chosen, axis=1)
        share = jnp.sum(jnp.where(chosen, route_weight, jnp.float32(0.0)), axis=1)
        count = jnp.sum(member.astype(jnp.int32))
        index = jnp.nonzero(member, size=slots, fill_value=0)[0].astype(jnp.int32)
        valid = jnp.arange(slots, dtype=jnp.int32) < count
        rows = jnp.where(valid[:, None], tokens[index], jnp.zeros((), jnp.bfloat16))
        scale = jnp.where(valid, share[index], jnp.float32(0.0))
        is_target = expert == target
        w_gate = jnp.where(is_target, backup[0], gate_weight[expert])
        w_up = jnp.where(is_target, backup[1], up_weight[expert])
        w_down = jnp.where(is_target, jnp.transpose(backup[2]), down_weight[expert])
        blocks = rows.astype(jnp.float32).reshape(slots, N_DP, part)
        gate = block_sum(blocks, w_gate.astype(jnp.float32).reshape(N_DP, part, FF), "snc,ncf->nsf")
        up = block_sum(blocks, w_up.astype(jnp.float32).reshape(N_DP, part, FF), "snc,ncf->nsf")
        sig = jax.nn.sigmoid(gate)
        hidden = (gate * sig * up).astype(jnp.bfloat16)
        result = jnp.dot(hidden, w_down, preferred_element_type=jnp.float32).astype(jnp.bfloat16)
        dout = (scale[:, None] * cotangent[index].astype(jnp.float32)).astype(jnp.bfloat16)
        dh = block_sum(dout.astype(jnp.float32).reshape(slots, N_DP, part),
                       w_down.astype(jnp.float32).reshape(FF, N_DP, part), "snc,fnc->nsf")
        d_gate = (dh * up * sig * (1.0 + gate * (1.0 - sig))).astype(jnp.bfloat16)
        d_up = (dh * gate * sig).astype(jnp.bfloat16)
        back_dims = (((1,), (1,)), ((), ()))
        d_rows = (lax.dot_general(d_gate, w_gate, back_dims, preferred_element_type=jnp.float32)
                  + lax.dot_general(d_up, w_up, back_dims, preferred_element_type=jnp.float32)).astype(jnp.bfloat16)
        row_dims = (((0,), (0,)), ((), ()))
        gate_grad = lax.dot_general(rows, d_gate, row_dims, preferred_element_type=jnp.float32).astype(jnp.bfloat16)
        up_grad = lax.dot_general(rows, d_up, row_dims, preferred_element_type=jnp.float32).astype(jnp.bfloat16)
        out_acc = out_acc.at[index].add(scale[:, None] * result.astype(jnp.float32))
        grad_acc = grad_acc.at[index].add(jnp.where(valid[:, None], d_rows.astype(jnp.float32), jnp.float32(0.0)))
        return (out_acc, grad_acc), (gate_grad, up_grad)

    start = (jnp.zeros((TOKENS, D), jnp.float32), jnp.zeros((TOKENS, D), jnp.float32))
    (out_acc, grad_acc), (gate_grads, up_grads) = lax.scan(one_expert, start, jnp.arange(EXPERTS, dtype=jnp.int32))
    return out_acc.astype(jnp.bfloat16), grad_acc.astype(jnp.bfloat16), gate_grads, up_grads
```

```python
import jax
import jax.numpy as jnp
from jax import lax
from jax.sharding import PartitionSpec as P

BF = jnp.bfloat16
F32 = jnp.float32
GRID = {64: (4, 8, 2), 8: (2, 2, 2)}


def dot(a, b, dims=(((1,), (0,)), ((), ()))):
    return lax.dot_general(a, b, dims, preferred_element_type=F32)


def activate(gate, up):
    return (gate * jax.nn.sigmoid(gate) * up).astype(BF)


def derive(gate, up, dh):
    sig = jax.nn.sigmoid(gate)
    d_gate = (dh * up * sig * (1.0 + gate * (1.0 - sig))).astype(BF)
    d_up = (dh * gate * sig).astype(BF)
    return (d_gate, d_up)


def core_swap(x):
    return lax.ppermute(x, "dp", [(i, i ^ 1) for i in range(8)])


def shift(x, k):
    return lax.ppermute(
        x, "dp", [(2 * h + c, 2 * ((h + k) % 4) + c) for h in range(4) for c in range(2)]
    )


def add(a, b):
    return (a.astype(F32) + b.astype(F32)).astype(BF)


def part_of(x, index, size):
    return lax.dynamic_slice_in_dim(x, index * size, size, 0)


def sum_scatter(x):
    me = lax.axis_index("dp")
    h, c = me // 2, me % 2
    half, chunk = x.shape[0] // 2, x.shape[0] // 8
    mid = chunk // 2
    other = core_swap(part_of(x, 1 - c, half))
    s = add(part_of(x, c, half), other)
    far = part_of(s, (h + 2) % 4, chunk)
    from_left = shift(far[:mid], 1)
    from_right = shift(far[mid:], -1)
    right = part_of(s, (h + 1) % 4, chunk)
    left = part_of(s, (h + 3) % 4, chunk)
    right = jnp.concatenate([add(right[:mid], from_left), right[mid:]], axis=0)
    left = jnp.concatenate([left[:mid], add(left[mid:], from_right)], axis=0)
    a = shift(right, 1)
    b = shift(left, -1)
    return part_of(s, h, chunk).astype(F32) + a.astype(F32) + b.astype(F32)


def gather_rows(v):
    me = lax.axis_index("dp")
    h, c = me // 2, me % 2
    chunk, width = v.shape
    mid = chunk // 2
    left = shift(v, 1)
    right = shift(v, -1)
    far = jnp.concatenate([shift(left[:mid], 1), shift(right[mid:], -1)], axis=0)
    half = jnp.zeros((4 * chunk, width), v.dtype)
    for k, block in ((0, v), (3, left), (1, right), (2, far)):
        half = lax.dynamic_update_slice_in_dim(half, block, ((h + k) % 4) * chunk, 0)
    other = core_swap(half)
    low = jnp.where(c == 0, half, other)
    high = jnp.where(c == 0, other, half)
    return jnp.concatenate([low, high], axis=0)


def body(
    tokens,
    cotangent,
    expert_ids,
    route_weight,
    replaced,
    gate_weight,
    up_weight,
    down_weight,
    backup,
):
    ranks = lax.axis_size("expert")
    nx, ny, nz = GRID[ranks]
    nxz = nx * nz
    along_y = [
        [(x * ny + y) * nz + z for y in range(ny)] for x in range(nx) for z in range(nz)
    ]
    along_xz = [
        [(x * ny + y) * nz + z for x in range(nx) for z in range(nz)] for y in range(ny)
    ]

    def over_y(v):
        return lax.all_to_all(v, "expert", 0, 0, axis_index_groups=along_y, tiled=True)

    def over_xz(v):
        return lax.all_to_all(v, "expert", 0, 0, axis_index_groups=along_xz, tiled=True)

    local_tok, topk = expert_ids.shape
    feat = tokens.shape[1]
    ff = gate_weight.shape[2]
    ffr = ff // ranks
    capacity = min(local_tok, 5 * local_tok * topk // (2 * ranks))
    is_target = lax.axis_index("expert") == replaced[0]

    experts = jnp.arange(ranks, dtype=jnp.int32)
    chosen = expert_ids[:, :, None] == experts
    member = jnp.sum(chosen.astype(jnp.int32), axis=1)
    share = jnp.sum(jnp.where(chosen, route_weight[:, :, None], 0.0), axis=1)
    place = jnp.where(member == 1, jnp.cumsum(member, axis=0) - 1, -1)
    share_hi = lax.reduce_precision(share, 8, 7)
    share_lo = share - share_hi
    meta = jnp.stack([place.astype(F32), share_hi, share_lo], axis=0).astype(BF)
    meta = meta.reshape(3, local_tok, nx, ny, nz)
    meta = jnp.transpose(meta, (3, 1, 0, 2, 4)).reshape(ny, local_tok, 3 * nxz)

    saved = jnp.transpose(backup, (0, 2, 1))
    width = 2 * feat + 128
    top = jnp.concatenate(
        [
            jnp.broadcast_to(jnp.concatenate([tokens, cotangent], axis=1), (ny, local_tok, 2 * feat)),
            jnp.pad(meta, ((0, 0), (0, 0), (0, 128 - 3 * nxz))),
        ],
        axis=2,
    )
    low = jnp.concatenate([saved[2, : ffr // 2], saved[2, ffr // 2 :]], axis=1)
    low = jnp.broadcast_to(jnp.pad(low, ((0, 0), (0, 128))), (ny, ffr // 2, width))
    first = jnp.concatenate([top, low], axis=1)
    first = over_y(first.reshape(-1, width)).reshape(ny, local_tok + ffr // 2, width)
    saved_gu = saved[:2].reshape(2 * ffr, feat)
    saved_gu = over_y(jnp.broadcast_to(saved_gu, (ny, 2 * ffr, feat)).reshape(-1, feat))

    seen = first[:, :local_tok].reshape(ny * local_tok, width)
    saved_d = first[:, local_tok:]
    saved_d = jnp.concatenate([saved_d[:, :, :feat], saved_d[:, :, feat : 2 * feat]], axis=1)
    saved_d = saved_d.reshape(ny * ffr, feat)
    tok_y, cot_y = seen[:, :feat], seen[:, feat : 2 * feat]
    meta_y = jnp.transpose(seen[:, 2 * feat : 2 * feat + 3 * nxz].astype(F32)).reshape(
        3, nxz, 1, ny * local_tok
    )

    rows_out = ny * capacity
    row = jnp.arange(rows_out, dtype=jnp.int32)[:, None]
    col = jnp.arange(ny * local_tok, dtype=jnp.int32)[None, :]
    want = jnp.where(row // capacity == col // local_tok, row % capacity, -2).astype(F32)
    hit = meta_y[0] == want[None]
    pick = hit.astype(BF).reshape(nxz * rows_out, -1)
    pick_hi = jnp.where(hit, meta_y[1], 0.0).astype(BF).reshape(nxz * rows_out, -1)
    pick_lo = jnp.where(hit, meta_y[2], 0.0).astype(BF).reshape(nxz * rows_out, -1)
    send_grad = (dot(pick_hi, cot_y) + dot(pick_lo, cot_y)).astype(BF)
    send_rows = dot(pick, tok_y).astype(BF)

    def exchange(rows, saved_rows):
        n = saved_rows.shape[0]
        both = jnp.concatenate(
            [rows.reshape(nxz, rows_out, feat), jnp.broadcast_to(saved_rows, (nxz, n, feat))],
            axis=1,
        )
        both = over_xz(both.reshape(-1, feat)).reshape(nxz, rows_out + n, feat)
        return both[:, :rows_out].reshape(nxz * rows_out, feat), both[:, rows_out:]

    douts, all_d = exchange(send_grad, saved_d)
    rows, all_gu = exchange(send_rows, saved_gu)

    def in_order(blocks, count):
        blocks = blocks.reshape(nx, nz, ny, count, ffr, feat)
        return jnp.transpose(blocks, (3, 0, 2, 1, 4, 5)).reshape(count, ff, feat)

    restored_d = in_order(all_d, 1)
    restored_gu = in_order(all_gu, 2)
    w_down = jnp.where(is_target, restored_d[0], down_weight[0])
    w_gate = jnp.where(is_target, jnp.transpose(restored_gu[0]), gate_weight[0])
    w_up = jnp.where(is_target, jnp.transpose(restored_gu[1]), up_weight[0])

    back_dims = (((1,), (1,)), ((), ()))
    row_dims = (((0,), (0,)), ((), ()))
    dh = sum_scatter(dot(douts, w_down, back_dims).astype(BF))
    gate_up = sum_scatter(
        jnp.concatenate([dot(rows, w_gate).astype(BF), dot(rows, w_up).astype(BF)], axis=1)
    )
    gate, up = gate_up[:, :ff], gate_up[:, ff:]
    hidden = activate(gate, up)
    d_gate, d_up = derive(gate, up, dh)
    d_both = gather_rows(jnp.concatenate([d_gate, d_up], axis=1))
    d_gate, d_up = d_both[:, :ff], d_both[:, ff:]
    hidden = gather_rows(hidden)

    d_rows = (dot(d_gate, w_gate, back_dims) + dot(d_up, w_up, back_dims)).astype(BF)
    back_dx = over_xz(d_rows)
    sum_dx = dot(pick, back_dx, row_dims).astype(BF)
    token_grad = jnp.sum(
        over_y(sum_dx).reshape(ny, local_tok, feat).astype(F32), axis=0
    ).astype(BF)

    result = dot(hidden, w_down).astype(BF)
    back_out = over_xz(result)
    sum_out = (dot(pick_hi, back_out, row_dims) + dot(pick_lo, back_out, row_dims)).astype(BF)
    combined = jnp.sum(
        over_y(sum_out).reshape(ny, local_tok, feat).astype(F32), axis=0
    ).astype(BF)

    gate_grad = dot(rows, d_gate, row_dims).astype(BF)
    up_grad = dot(rows, d_up, row_dims).astype(BF)
    return (combined, token_grad, gate_grad[None], up_grad[None])


def solution(mesh):
    placed = (
        P("expert", "dp"),
        P("expert", "dp"),
        P("expert", None),
        P("expert", None),
        P(),
        P("expert", "dp", None),
        P("expert", "dp", None),
        P("expert", None, "dp"),
        P(None, "dp", "expert"),
    )
    return jax.shard_map(
        body,
        mesh=mesh,
        in_specs=placed,
        out_specs=(
            P("expert", "dp"),
            P("expert", "dp"),
            P("expert", "dp", None),
            P("expert", "dp", None),
        ),
        check_vma=False,
    )
```

```python
import functools

import jax
import jax.numpy as jnp
import numpy as np
from jax import lax
from jax.experimental import pallas as pl
from jax.experimental.pallas import tpu as pltpu
from jax.sharding import PartitionSpec as P

BF = jnp.bfloat16
F32 = jnp.float32
GRID = {64: (4, 8, 2), 8: (2, 2, 2)}
NN = (((1,), (0,)), ((), ()))
NT = (((1,), (1,)), ((), ()))
TN = (((0,), (0,)), ((), ()))
LANES = 1152
TILE = 256


def dot(a, b, dims=NN):
    return lax.dot_general(a, b, dims, preferred_element_type=F32)


def call(kernel, outs, scratch=(), scalars=0, operands=0, megabytes=32):
    def of(shape, dtype=BF):
        return jax.ShapeDtypeStruct(shape, dtype)

    specs = [pl.BlockSpec(memory_space=pltpu.SMEM)] * scalars
    specs += [pl.BlockSpec(memory_space=pltpu.VMEM)] * operands
    return pl.pallas_call(
        kernel,
        out_shape=[of(*s) if isinstance(s[0], tuple) else of(s) for s in outs],
        in_specs=specs,
        out_specs=[pl.BlockSpec(memory_space=pltpu.VMEM)] * len(outs),
        scratch_shapes=list(scratch),
        compiler_params=pltpu.CompilerParams(vmem_limit_bytes=megabytes << 20),
    )


def pack_kernel(grid, ids_ref, weight_ref, tok_ref, cot_ref, saved_ref, out_ref):
    nx, ny, nz = grid
    nxz, ranks = nx * nz, nx * ny * nz
    tok, topk = ids_ref.shape
    ids = ids_ref[...]
    x, y, z = lax.div(ids, ny * nz), lax.rem(lax.div(ids, nz), ny), lax.rem(ids, nz)
    column = y * nxz + x * nz + z
    lane = lax.broadcasted_iota(jnp.int32, (tok, ranks), 1)
    member = jnp.zeros((tok, ranks), F32)
    share = jnp.zeros((tok, ranks), F32)
    for k in range(topk):
        same = column[:, k : k + 1] == lane
        member = member + jnp.where(same, 1.0, 0.0)
        share = share + jnp.where(same, weight_ref[:, k : k + 1], 0.0)
    row = lax.broadcasted_iota(jnp.int32, (tok, tok), 0)
    col = lax.broadcasted_iota(jnp.int32, (tok, tok), 1)
    before = dot(jnp.where(col <= row, 1.0, 0.0).astype(BF), member.astype(BF))
    place = jnp.where(member > 0.5, before - 1.0, -1.0).astype(BF)
    hi = share.astype(BF)
    lo = (share - hi.astype(F32)).astype(BF)
    source = lax.broadcasted_iota(jnp.int32, (ranks, ny * 128), 0)
    target = lax.broadcasted_iota(jnp.int32, (ranks, ny * 128), 1)
    base = lax.div(source, nxz) * 128 + lax.rem(source, nxz) + 64
    meta = jnp.zeros((tok, ny * 128), F32)
    for k, part in enumerate((place, hi, lo)):
        meta = meta + dot(part, jnp.where(target == base + k * nxz, 1.0, 0.0).astype(BF))
    feat = tok_ref.shape[1]
    assert feat == 448
    last = jnp.concatenate([tok_ref[:, 384:448].astype(F32), jnp.zeros((tok, 64), F32)], axis=1)
    n = saved_ref.shape[1]
    for i in range(ny):
        out_ref[i, 0:tok, 0:384] = tok_ref[:, 0:384]
        out_ref[i, 0:tok, 384:512] = (meta[:, i * 128 : (i + 1) * 128] + last).astype(BF)
        out_ref[i, 0:tok, 512 : 512 + feat] = cot_ref[...]
        out_ref[i, tok : tok + n, 0:feat] = saved_ref[0]
        out_ref[i, tok : tok + n, 512 : 512 + feat] = saved_ref[1]
        for k in range(3):
            out_ref[i, k * n : (k + 1) * n, 1024:1152] = saved_ref[2, :, k * 128 : (k + 1) * 128]
        out_ref[i, 2 * n : 3 * n, 960:1024] = saved_ref[2, :, 384:448]


def select_kernel(first_ref, want_ref, out_ref, pick_ref, hi_ref, lo_ref):
    nxz, _, width = out_ref.shape
    feat = width // 2
    ny, rows, _ = first_ref.shape
    n = 16
    tok = rows - n
    seen = ny * tok
    out_rows = want_ref.shape[0]
    tokens = first_ref[:, 0:tok, 0:feat].reshape(seen, feat)
    cots = first_ref[:, 0:tok, 512 : 512 + feat].reshape(seen, feat)
    meta = jnp.transpose(first_ref[:, 0:tok, 384:512].reshape(seen, 128).astype(F32))
    want = want_ref[...]
    both = jnp.concatenate([cots, cots], axis=0)
    gate = first_ref[:, tok : tok + n, 0:feat].reshape(ny * n, feat)
    up = first_ref[:, tok : tok + n, 512 : 512 + feat].reshape(ny * n, feat)
    half = ny // 2
    for q in range(nxz):
        hit = meta[64 + q : 65 + q] == want
        pick = jnp.where(hit, 1.0, 0.0).astype(BF)
        hi = jnp.where(hit, meta[64 + nxz + q : 65 + nxz + q], 0.0).astype(BF)
        lo = jnp.where(hit, meta[64 + 2 * nxz + q : 65 + 2 * nxz + q], 0.0).astype(BF)
        span = pl.ds(q * out_rows, out_rows)
        pick_ref[span, :] = pick
        hi_ref[span, :] = hi
        lo_ref[span, :] = lo
        out_ref[q, 0:out_rows, 0:feat] = dot(pick, tokens).astype(BF)
        weighted = dot(jnp.concatenate([hi, lo], axis=1), both)
        out_ref[q, 0:out_rows, feat:width] = weighted.astype(BF)
        r = out_rows
        out_ref[q, r : r + ny * n, 0:feat] = gate
        out_ref[q, r : r + ny * n, feat:width] = up
        r += ny * n
        for k in range(3):
            piece = first_ref[:, k * n : (k + 1) * n, 1024:1152]
            at = k * 128
            out_ref[q, r : r + half * n, at : at + 128] = piece[:half].reshape(half * n, 128)
            out_ref[q, r : r + half * n, feat + at : feat + at + 128] = piece[half:].reshape(half * n, 128)
        piece = first_ref[:, 2 * n : 3 * n, 960:1024]
        out_ref[q, r : r + half * n, 384:448] = piece[:half].reshape(half * n, 64)
        out_ref[q, r : r + half * n, feat + 384 : feat + 448] = piece[half:].reshape(half * n, 64)


def chunk_at(h, c, p):
    half = c if p < 4 else 1 - c
    return half * 4 + lax.rem(h + (2, 0, 1, 3)[p % 4], 4)


def products_kernel(
    grid, who_ref, recv_ref, gate_ref, up_ref, down_ref,
    rows_ref, far_ref, rest_ref, far_out_ref, rest_out_ref, restored_ref, grads_ref,
):
    nx, ny, nz = grid
    feat, ff = gate_ref.shape
    chunk = far_ref.shape[0]
    n = 16
    target, h, c = who_ref[0], who_ref[1], who_ref[2]
    for p in range(8):
        g = chunk_at(h, c, p)
        rows_ref[p * chunk : (p + 1) * chunk, :] = recv_ref[g, 0:chunk, 0:feat]
        grads_ref[p * chunk : (p + 1) * chunk, :] = recv_ref[g, 0:chunk, feat : 2 * feat]

    def store(k, j, value):
        at = pl.ds(pl.multiple_of(k * ff + j * TILE, TILE), TILE)
        value = value.astype(BF)
        far_ref[:, at] = value[0:chunk]
        rest_ref[:, at] = value[chunk : 4 * chunk]
        far_out_ref[:, at] = value[4 * chunk : 5 * chunk]
        rest_out_ref[:, at] = value[5 * chunk :]

    tiles = ff // TILE

    @pl.when(target == 0)
    def _():
        @pl.loop(0, tiles)
        def _(j):
            at = pl.ds(pl.multiple_of(j * TILE, TILE), TILE)
            store(0, j, dot(rows_ref[...], gate_ref[:, at]))
            store(1, j, dot(rows_ref[...], up_ref[:, at]))
            store(2, j, dot(grads_ref[...], down_ref[:, at]))

    @pl.when(target == 1)
    def _():
        for x in range(nx):
            for z in range(nz):
                q = x * nz + z
                for y in range(ny):
                    to = pl.ds(((x * ny + y) * nz + z) * n, n)
                    r = chunk + y * n
                    restored_ref[0, to, :] = recv_ref[q, r : r + n, 0:feat]
                    restored_ref[1, to, :] = recv_ref[q, r : r + n, feat : 2 * feat]
                    r = chunk + ny * n + (y % (ny // 2)) * n
                    s = 0 if y < ny // 2 else feat
                    restored_ref[2, to, :] = recv_ref[q, r : r + n, s : s + feat]

        @pl.loop(0, tiles)
        def _(j):
            at = pl.ds(pl.multiple_of(j * TILE, TILE), TILE)
            store(0, j, dot(rows_ref[...], restored_ref[0, at, :], NT))
            store(1, j, dot(rows_ref[...], restored_ref[1, at, :], NT))
            store(2, j, dot(grads_ref[...], restored_ref[2, at, :], NT))


def activate_kernel(own_ref, other_ref, left_ref, right_ref, out_ref):
    ff = out_ref.shape[1] // 3
    rows = out_ref.shape[0]

    @pl.loop(0, ff // TILE)
    def _(j):
        def total(k):
            at = pl.ds(pl.multiple_of(k * ff + j * TILE, TILE), TILE)
            near = own_ref[0:rows, at].astype(F32) + other_ref[0:rows, at].astype(F32)
            return near + (left_ref[:, at].astype(F32) + right_ref[:, at].astype(F32))

        gate, up, dh = total(0), total(1), total(2)
        sig = jax.nn.sigmoid(gate)
        values = (
            gate * sig * up,
            dh * up * sig * (1.0 + gate * (1.0 - sig)),
            dh * gate * sig,
        )
        for k, value in enumerate(values):
            at = pl.ds(pl.multiple_of(k * ff + j * TILE, TILE), TILE)
            out_ref[:, at] = value.astype(BF)


def back_kernel(*refs):
    who_ref, parts = refs[0], refs[1:9]
    gate_ref, up_ref, down_ref, restored_ref, out_ref, grads_ref, hidden_ref, y_ref, dx_ref = refs[9:]
    feat, ff = gate_ref.shape
    chunk = out_ref.shape[1]
    target, h, c = who_ref[0], who_ref[1], who_ref[2]
    for p in range(8):
        span = slice(p * chunk, (p + 1) * chunk)
        hidden_ref[span, :] = parts[p][:, 0:ff]
        grads_ref[span, :] = parts[p][:, ff : 3 * ff]

    @pl.when(target == 0)
    def _():
        y_ref[...] = dot(hidden_ref[...], down_ref[...], NT).astype(BF)
        dx_ref[...] = (
            dot(grads_ref[:, 0:ff], gate_ref[...], NT) + dot(grads_ref[:, ff : 2 * ff], up_ref[...], NT)
        ).astype(BF)

    @pl.when(target == 1)
    def _():
        y_ref[...] = dot(hidden_ref[...], restored_ref[2]).astype(BF)
        dx_ref[...] = (
            dot(grads_ref[:, 0:ff], restored_ref[0]) + dot(grads_ref[:, ff : 2 * ff], restored_ref[1])
        ).astype(BF)

    for p in range(8):
        g = chunk_at(h, c, p)
        span = slice(p * chunk, (p + 1) * chunk)
        out_ref[g, :, 0:feat] = y_ref[span, :]
        out_ref[g, :, feat : 2 * feat] = dx_ref[span, :]


def combine_kernel(recv_ref, pick_ref, hi_ref, lo_ref, out_ref):
    nxz, out_rows, width = recv_ref.shape
    feat = width // 2
    rows = recv_ref[...].reshape(nxz * out_rows, width)
    y = dot(hi_ref[...], rows[:, 0:feat], TN) + dot(lo_ref[...], rows[:, 0:feat], TN)
    out_ref[:, 0:feat] = y.astype(BF)
    out_ref[:, feat:width] = dot(pick_ref[...], rows[:, feat:width], TN).astype(BF)


def finish_kernel(recv_ref, out_ref, grad_ref):
    feat = out_ref.shape[1]
    total = jnp.sum(recv_ref[...].astype(F32), axis=0)
    out_ref[...] = total[:, 0:feat].astype(BF)
    grad_ref[...] = total[:, feat : 2 * feat].astype(BF)


def core_swap(x):
    return lax.ppermute(x, "dp", [(i, i ^ 1) for i in range(8)])


def shift(x, k):
    return lax.ppermute(
        x, "dp", [(2 * h + c, 2 * ((h + k) % 4) + c) for h in range(4) for c in range(2)]
    )


def add(a, b):
    return (a.astype(F32) + b.astype(F32)).astype(BF)


def body(
    tokens,
    cotangent,
    expert_ids,
    route_weight,
    replaced,
    gate_weight,
    up_weight,
    down_weight,
    backup,
):
    ranks = lax.axis_size("expert")
    grid = nx, ny, nz = GRID[ranks]
    nxz = nx * nz
    along_y = [
        [(x * ny + y) * nz + z for y in range(ny)] for x in range(nx) for z in range(nz)
    ]
    along_xz = [
        [(x * ny + y) * nz + z for x in range(nx) for z in range(nz)] for y in range(ny)
    ]

    def exchange(v, groups):
        flat = v.reshape(-1, v.shape[-1])
        flat = lax.all_to_all(flat, "expert", 0, 0, axis_index_groups=groups, tiled=True)
        return flat.reshape(v.shape)

    tok, topk = expert_ids.shape
    feat = tokens.shape[1]
    ff = gate_weight.shape[2]
    ffr = ff // ranks
    capacity = min(tok, 5 * tok * topk // (2 * ranks))
    chunk = ranks * capacity // 8
    me = lax.axis_index("dp")
    who = jnp.stack(
        [(lax.axis_index("expert") == replaced[0]).astype(jnp.int32), me // 2, me % 2]
    ).astype(jnp.int32)

    saved = jnp.transpose(backup, (0, 2, 1))
    (first,) = call(
        functools.partial(pack_kernel, grid), [(ny, tok + ffr, LANES)], operands=5
    )(expert_ids, route_weight, tokens, cotangent, saved)
    first = exchange(first, along_y)

    out_rows, seen = ny * capacity, ny * tok
    row, col = np.arange(out_rows)[:, None], np.arange(seen)[None, :]
    want = np.where(row // capacity == col // tok, row % capacity, -2).astype(np.float32)
    table = (nxz * out_rows, seen)
    send, pick, pick_hi, pick_lo = call(
        select_kernel,
        [(nxz, out_rows + ny * ffr * 3 // 2, 2 * feat), table, table, table],
        operands=2,
    )(first, want)
    recv = exchange(send, along_xz)

    w_gate, w_up, w_down = gate_weight[0], up_weight[0], jnp.transpose(down_weight[0])
    wide = 3 * ff
    rows, far, rest, far_out, rest_out, restored = call(
        functools.partial(products_kernel, grid),
        [
            (8 * chunk, feat), (chunk, wide), (3 * chunk, wide),
            (chunk, wide), (3 * chunk, wide), (3, ff, feat),
        ],
        scratch=[pltpu.VMEM((8 * chunk, feat), BF)],
        scalars=1,
        operands=4,
        megabytes=40,
    )(who, recv, w_gate, w_up, w_down)

    mid = chunk // 2
    far = add(far, core_swap(far_out))
    rest_in = core_swap(rest_out)
    from_left, from_right = shift(far[:mid], 1), shift(far[mid:], -1)
    sides = add(rest[chunk:], rest_in[chunk:])
    right, left = sides[:chunk], sides[chunk:]
    right = jnp.concatenate([add(right[:mid], from_left), right[mid:]], axis=0)
    left = jnp.concatenate([left[:mid], add(left[mid:], from_right)], axis=0)
    from_left, from_right = shift(right, 1), shift(left, -1)
    (own,) = call(activate_kernel, [(chunk, wide)], operands=4)(
        rest, rest_in, from_left, from_right
    )

    left, right = shift(own, 1), shift(own, -1)
    far = jnp.concatenate([shift(left[:mid], 1), shift(right[mid:], -1)], axis=0)
    mine = (far, own, right, left)
    other = tuple(core_swap(v) for v in mine)

    out, grads = call(
        back_kernel,
        [(8, chunk, 2 * feat), (8 * chunk, 2 * ff)],
        scratch=[
            pltpu.VMEM((8 * chunk, ff), BF),
            pltpu.VMEM((8 * chunk, feat), BF),
            pltpu.VMEM((8 * chunk, feat), BF),
        ],
        scalars=1,
        operands=12,
        megabytes=40,
    )(who, *mine, *other, w_gate, w_up, w_down, restored)

    out = exchange(out.reshape(nxz, out_rows, 2 * feat), along_xz)
    gate_grad = dot(rows, grads[:, :ff], TN).astype(BF)
    up_grad = dot(rows, grads[:, ff:], TN).astype(BF)
    (part,) = call(combine_kernel, [(seen, 2 * feat)], operands=4)(out, pick, pick_hi, pick_lo)
    part = exchange(part.reshape(ny, tok, 2 * feat), along_y)
    combined, token_grad = call(finish_kernel, [(tok, feat), (tok, feat)], operands=1)(part)
    return (combined, token_grad, gate_grad[None], up_grad[None])


def solution(mesh):
    placed = (
        P("expert", "dp"),
        P("expert", "dp"),
        P("expert", None),
        P("expert", None),
        P(),
        P("expert", "dp", None),
        P("expert", "dp", None),
        P("expert", None, "dp"),
        P(None, "dp", "expert"),
    )
    return jax.shard_map(
        body,
        mesh=mesh,
        in_specs=placed,
        out_specs=(
            P("expert", "dp"),
            P("expert", "dp"),
            P("expert", "dp", None),
            P("expert", "dp", None),
        ),
        check_vma=False,
    )
```

```python
import functools

import jax
import jax.numpy as jnp
import numpy as np
from jax import lax
from jax.experimental import pallas as pl
from jax.experimental.pallas import tpu as pltpu
from jax.sharding import PartitionSpec as P

BF = jnp.bfloat16
F32 = jnp.float32
GRID = {64: (4, 8, 2), 8: (2, 2, 2)}
NN = (((1,), (0,)), ((), ()))
NT = (((1,), (1,)), ((), ()))
TN = (((0,), (0,)), ((), ()))
LANES = 1280
TILE = 256


def dot(a, b, dims=NN):
    return lax.dot_general(a, b, dims, preferred_element_type=F32)


def call(kernel, outs, scratch=(), scalars=0, operands=0, megabytes=32):
    def of(shape, dtype=BF):
        return jax.ShapeDtypeStruct(shape, dtype)

    specs = [pl.BlockSpec(memory_space=pltpu.SMEM)] * scalars
    specs += [pl.BlockSpec(memory_space=pltpu.VMEM)] * operands
    return pl.pallas_call(
        kernel,
        out_shape=[of(*s) if isinstance(s[0], tuple) else of(s) for s in outs],
        in_specs=specs,
        out_specs=[pl.BlockSpec(memory_space=pltpu.VMEM)] * len(outs),
        scratch_shapes=list(scratch),
        compiler_params=pltpu.CompilerParams(vmem_limit_bytes=megabytes << 20),
    )


def pack_kernel(grid, ids_ref, weight_ref, tok_ref, cot_ref, saved_ref, out_ref):
    nx, ny, nz = grid
    nxz, ranks = nx * nz, nx * ny * nz
    tok, topk = ids_ref.shape
    ids = ids_ref[...]
    x, y, z = lax.div(ids, ny * nz), lax.rem(lax.div(ids, nz), ny), lax.rem(ids, nz)
    column = y * nxz + x * nz + z
    lane = lax.broadcasted_iota(jnp.int32, (tok, ranks), 1)
    member = jnp.zeros((tok, ranks), F32)
    share = jnp.zeros((tok, ranks), F32)
    for k in range(topk):
        same = column[:, k : k + 1] == lane
        member = member + jnp.where(same, 1.0, 0.0)
        share = share + jnp.where(same, weight_ref[:, k : k + 1], 0.0)
    row = lax.broadcasted_iota(jnp.int32, (tok, tok), 0)
    col = lax.broadcasted_iota(jnp.int32, (tok, tok), 1)
    before = dot(jnp.where(col <= row, 1.0, 0.0).astype(BF), member.astype(BF))
    place = jnp.where(member > 0.5, before - 1.0, -1.0).astype(BF)
    hi = share.astype(BF)
    lo = (share - hi.astype(F32)).astype(BF)
    source = lax.broadcasted_iota(jnp.int32, (ranks, ny * 128), 0)
    target = lax.broadcasted_iota(jnp.int32, (ranks, ny * 128), 1)
    base = lax.div(source, nxz) * 128 + lax.rem(source, nxz) + 64
    meta = jnp.zeros((tok, ny * 128), F32)
    for k, part in enumerate((place, hi, lo)):
        meta = meta + dot(part, jnp.where(target == base + k * nxz, 1.0, 0.0).astype(BF))
    feat = tok_ref.shape[1]
    assert feat == 448
    last = jnp.concatenate([tok_ref[:, 384:448].astype(F32), jnp.zeros((tok, 64), F32)], axis=1)
    n = saved_ref.shape[0]
    for i in range(ny):
        out_ref[i, :, 0:384] = tok_ref[:, 0:384]
        out_ref[i, :, 384:512] = (meta[:, i * 128 : (i + 1) * 128] + last).astype(BF)
        out_ref[i, :, 512 : 512 + feat] = cot_ref[...]
        for k in range(4):
            at, wide = 1024 + 128 * (k // 2), min(128, feat - 128 * k)
            out_ref[i, (k % 2) * n : (k % 2 + 1) * n, at : at + wide] = saved_ref[:, 128 * k : 128 * k + wide]


def select_kernel(first_ref, want_ref, out_ref, pick_ref, hi_ref, lo_ref):
    nxz = out_ref.shape[0]
    ny, tok, _ = first_ref.shape
    n = tok // 2
    seen = ny * tok
    rows = want_ref.shape[0]
    saved = ny * n
    cots = first_ref[:, :, 512:960].reshape(seen, 448)
    meta = jnp.transpose(first_ref[:, :, 384:512].reshape(seen, 128).astype(F32))
    want = want_ref[...]
    both = jnp.concatenate([cots, cots], axis=0)
    split = saved - rows
    for q in range(nxz):
        hit = meta[64 + q : 65 + q] == want
        hi = jnp.where(hit, meta[64 + nxz + q : 65 + nxz + q], 0.0).astype(BF)
        lo = jnp.where(hit, meta[64 + 2 * nxz + q : 65 + 2 * nxz + q], 0.0).astype(BF)
        span = pl.ds(q * rows, rows)
        pick_ref[span, :] = jnp.where(hit, 1.0, 0.0).astype(BF)
        hi_ref[span, :] = hi
        lo_ref[span, :] = lo
        value = dot(jnp.concatenate([hi, lo], axis=1), both).astype(BF)
        out_ref[q, 0:rows, 512:640] = value[:, 0:128]
        out_ref[q, 0:rows, 640:768] = value[:, 128:256]
        out_ref[q, rows : rows + split, 512:640] = value[0:split, 256:384]
        out_ref[q, rows : 2 * rows - split, 640:768] = value[split:, 256:384]
        out_ref[q, 0:rows, 448:512] = value[:, 384:448]
        for k in range(4):
            at, wide = 1024 + 128 * (k // 2), min(128, 448 - 128 * k)
            piece = first_ref[:, (k % 2) * n : (k % 2 + 1) * n, at : at + wide]
            out_ref[q, 0:saved, 128 * k : 128 * k + wide] = piece.reshape(saved, wide)


def pick_kernel(first_ref, pick_ref, out_ref):
    ny, tok, _ = first_ref.shape
    nxz, rows, feat = out_ref.shape
    tokens = first_ref[:, :, 0:feat].reshape(ny * tok, feat)
    out_ref[...] = dot(pick_ref[...], tokens).astype(BF).reshape(nxz, rows, feat)


def chunk_at(h, c, p):
    half = c if p < 4 else 1 - c
    return half * 4 + lax.rem(h + (2, 0, 1, 3)[p % 4], 4)


def store(outs, chunk, at, value):
    value = value.astype(BF)
    outs[0][:, at] = value[0:chunk]
    outs[1][:, at] = value[chunk : 4 * chunk]
    outs[2][:, at] = value[4 * chunk : 5 * chunk]
    outs[3][:, at] = value[5 * chunk :]


def down_kernel(grid, who_ref, recv_ref, down_ref, o0, o1, o2, o3, restored_ref, grads_ref):
    nx, ny, nz = grid
    ff = down_ref.shape[1]
    chunk = o0.shape[0]
    outs = (o0, o1, o2, o3)
    saved = recv_ref.shape[1]
    n = saved // ny
    split = saved - chunk
    target, h, c = who_ref[0], who_ref[1], who_ref[2]
    for p in range(8):
        g = chunk_at(h, c, p)
        at = p * chunk
        grads_ref[at : at + chunk, 0:128] = recv_ref[g, 0:chunk, 512:640]
        grads_ref[at : at + chunk, 128:256] = recv_ref[g, 0:chunk, 640:768]
        grads_ref[at : at + split, 256:384] = recv_ref[g, chunk : chunk + split, 512:640]
        grads_ref[at + split : at + chunk, 256:384] = recv_ref[g, chunk : 2 * chunk - split, 640:768]
        grads_ref[at : at + chunk, 384:448] = recv_ref[g, 0:chunk, 448:512]

    @pl.when(target == 0)
    def _():
        @pl.loop(0, ff // TILE)
        def _(j):
            at = pl.ds(pl.multiple_of(j * TILE, TILE), TILE)
            store(outs, chunk, at, dot(grads_ref[...], down_ref[:, at]))

    @pl.when(target == 1)
    def _():
        for x in range(nx):
            for z in range(nz):
                for y in range(ny):
                    to = pl.ds(((x * ny + y) * nz + z) * n, n)
                    restored_ref[to, :] = recv_ref[x * nz + z, y * n : (y + 1) * n, 0:448]

        @pl.loop(0, ff // TILE)
        def _(j):
            at = pl.ds(pl.multiple_of(j * TILE, TILE), TILE)
            store(outs, chunk, at, dot(grads_ref[...], restored_ref[at, :], NT))


def gate_up_kernel(
    grid, who_ref, recv_ref, saved_ref, gate_ref, up_ref, rows_ref, o0, o1, o2, o3, restored_ref
):
    nx, ny, nz = grid
    feat, ff = gate_ref.shape
    chunk = o0.shape[0]
    outs = (o0, o1, o2, o3)
    n = saved_ref.shape[0] // (nx * ny * nz)
    target, h, c, my_x, my_z = (who_ref[i] for i in range(5))
    for p in range(8):
        rows_ref[p * chunk : (p + 1) * chunk, :] = recv_ref[chunk_at(h, c, p)]

    def tile(k, j):
        return pl.ds(pl.multiple_of(k * ff + j * TILE, TILE), TILE)

    @pl.when(target == 0)
    def _():
        @pl.loop(0, ff // TILE)
        def _(j):
            store(outs, chunk, tile(0, j), dot(rows_ref[...], gate_ref[:, tile(0, j)]))
            store(outs, chunk, tile(1, j), dot(rows_ref[...], up_ref[:, tile(0, j)]))

    @pl.when(target == 1)
    def _():
        for y in range(ny):
            for k in range(nx):
                for other in range(nz):
                    x = lax.rem(my_x - k + nx, nx)
                    z = 1 - my_z if other else my_z
                    to = pl.ds(pl.multiple_of(((x * ny + y) * nz + z) * n, n), n)
                    r = ((y * nx + k) * nz + other) * n
                    restored_ref[0, to, :] = saved_ref[r : r + n, 0:feat]
                    restored_ref[1, to, :] = saved_ref[r : r + n, feat : 2 * feat]

        @pl.loop(0, ff // TILE)
        def _(j):
            store(outs, chunk, tile(0, j), dot(rows_ref[...], restored_ref[0, tile(0, j), :], NT))
            store(outs, chunk, tile(1, j), dot(rows_ref[...], restored_ref[1, tile(0, j), :], NT))


def activate_kernel(*refs):
    gate_up, grads, out_ref = refs[0:4], refs[4:8], refs[8]
    ff = out_ref.shape[1] // 3
    rows = out_ref.shape[0]

    @pl.loop(0, ff // TILE)
    def _(j):
        def total(parts, k):
            at = pl.ds(pl.multiple_of(k * ff + j * TILE, TILE), TILE)
            near = parts[0][0:rows, at].astype(F32) + parts[1][0:rows, at].astype(F32)
            return near + (parts[2][:, at].astype(F32) + parts[3][:, at].astype(F32))

        gate, up, dh = total(gate_up, 0), total(gate_up, 1), total(grads, 0)
        sig = jax.nn.sigmoid(gate)
        values = (
            gate * sig * up,
            dh * up * sig * (1.0 + gate * (1.0 - sig)),
            dh * gate * sig,
        )
        for k, value in enumerate(values):
            at = pl.ds(pl.multiple_of(k * ff + j * TILE, TILE), TILE)
            out_ref[:, at] = value.astype(BF)


def back_kernel(*refs):
    who_ref, parts = refs[0], refs[1:9]
    gate_ref, up_ref, down_ref, restored_ref, restored_down_ref = refs[9:14]
    out_ref, grads_ref, hidden_ref, y_ref, dx_ref = refs[14:]
    feat, ff = gate_ref.shape
    chunk = out_ref.shape[1]
    target, h, c = who_ref[0], who_ref[1], who_ref[2]
    for p in range(8):
        span = slice(p * chunk, (p + 1) * chunk)
        hidden_ref[span, :] = parts[p][:, 0:ff]
        grads_ref[span, :] = parts[p][:, ff : 3 * ff]

    @pl.when(target == 0)
    def _():
        y_ref[...] = dot(hidden_ref[...], down_ref[...], NT).astype(BF)
        dx_ref[...] = (
            dot(grads_ref[:, 0:ff], gate_ref[...], NT) + dot(grads_ref[:, ff : 2 * ff], up_ref[...], NT)
        ).astype(BF)

    @pl.when(target == 1)
    def _():
        y_ref[...] = dot(hidden_ref[...], restored_down_ref[...]).astype(BF)
        dx_ref[...] = (
            dot(grads_ref[:, 0:ff], restored_ref[0]) + dot(grads_ref[:, ff : 2 * ff], restored_ref[1])
        ).astype(BF)

    for p in range(8):
        g = chunk_at(h, c, p)
        span = slice(p * chunk, (p + 1) * chunk)
        out_ref[g, :, 0:feat] = y_ref[span, :]
        out_ref[g, :, feat : 2 * feat] = dx_ref[span, :]


def combine_kernel(recv_ref, pick_ref, hi_ref, lo_ref, out_ref):
    nxz, out_rows, width = recv_ref.shape
    feat = width // 2
    rows = recv_ref[...].reshape(nxz * out_rows, width)
    y = dot(hi_ref[...], rows[:, 0:feat], TN) + dot(lo_ref[...], rows[:, 0:feat], TN)
    out_ref[:, 0:feat] = y.astype(BF)
    out_ref[:, feat:width] = dot(pick_ref[...], rows[:, feat:width], TN).astype(BF)


def finish_kernel(recv_ref, out_ref, grad_ref):
    feat = out_ref.shape[1]
    total = jnp.sum(recv_ref[...].astype(F32), axis=0)
    out_ref[...] = total[:, 0:feat].astype(BF)
    grad_ref[...] = total[:, feat : 2 * feat].astype(BF)


def core_swap(x):
    return lax.ppermute(x, "dp", [(i, i ^ 1) for i in range(8)])


def shift(x, k):
    return lax.ppermute(
        x, "dp", [(2 * h + c, 2 * ((h + k) % 4) + c) for h in range(4) for c in range(2)]
    )


def add(a, b):
    return (a.astype(F32) + b.astype(F32)).astype(BF)


def body(
    tokens,
    cotangent,
    expert_ids,
    route_weight,
    replaced,
    gate_weight,
    up_weight,
    down_weight,
    backup,
):
    ranks = lax.axis_size("expert")
    grid = nx, ny, nz = GRID[ranks]
    nxz = nx * nz
    along_y = [
        [(x * ny + y) * nz + z for y in range(ny)] for x in range(nx) for z in range(nz)
    ]
    along_xz = [
        [(x * ny + y) * nz + z for x in range(nx) for z in range(nz)] for y in range(ny)
    ]

    def exchange(v, groups):
        flat = v.reshape(-1, v.shape[-1])
        flat = lax.all_to_all(flat, "expert", 0, 0, axis_index_groups=groups, tiled=True)
        return flat.reshape(v.shape)

    def rank(x, y, z):
        return ((x % nx) * ny + y) * nz + z % nz

    def step(v, dx, dz):
        pairs = [
            (rank(x, y, z), rank(x + dx, y, z + dz))
            for x in range(nx) for y in range(ny) for z in range(nz)
        ]
        return lax.ppermute(v, "expert", pairs)

    tok, topk = expert_ids.shape
    feat = tokens.shape[1]
    ff = gate_weight.shape[2]
    ffr = ff // ranks
    capacity = min(tok, 5 * tok * topk // (2 * ranks))
    chunk = ranks * capacity // 8
    mid = chunk // 2
    me, expert = lax.axis_index("dp"), lax.axis_index("expert")
    who = jnp.stack(
        [
            (expert == replaced[0]).astype(jnp.int32),
            me // 2,
            me % 2,
            expert // (ny * nz),
            expert % nz,
        ]
    ).astype(jnp.int32)

    saved = jnp.transpose(backup, (0, 2, 1))
    pair = jnp.concatenate([saved[0], saved[1]], axis=1)
    pair = jnp.concatenate([pair, step(pair, 0, 1)], axis=0)
    (first,) = call(functools.partial(pack_kernel, grid), [(ny, tok, LANES)], operands=5)(
        expert_ids, route_weight, tokens, cotangent, saved[2]
    )
    pair, first = lax.optimization_barrier((pair, first))
    first = exchange(first, along_y)

    line = jnp.concatenate([pair] + [step(pair, k, 0) for k in range(1, nx)], axis=0)
    line, first = lax.optimization_barrier((line, first))
    saved_gate_up = lax.all_gather(
        line, "expert", axis=0, axis_index_groups=along_y, tiled=True
    )

    out_rows, seen = ny * capacity, ny * tok
    row, col = np.arange(out_rows)[:, None], np.arange(seen)[None, :]
    want = np.where(row // capacity == col // tok, row % capacity, -2).astype(np.float32)
    table = (nxz * out_rows, seen)
    send, pick, pick_hi, pick_lo = call(
        select_kernel, [(nxz, ny * ffr, 768), table, table, table], operands=2
    )(first, want)
    recv_grads = exchange(send, along_xz)
    (send,) = call(pick_kernel, [(nxz, out_rows, feat)], operands=2)(first, pick)
    recv_rows = exchange(send, along_xz)

    def sum_parts(far, rest, far_out, rest_out):
        far = add(far, core_swap(far_out))
        rest_in = core_swap(rest_out)
        from_left, from_right = shift(far[:mid], 1), shift(far[mid:], -1)
        sides = add(rest[chunk:], rest_in[chunk:])
        right, left = sides[:chunk], sides[chunk:]
        right = jnp.concatenate([add(right[:mid], from_left), right[mid:]], axis=0)
        left = jnp.concatenate([left[:mid], add(left[mid:], from_right)], axis=0)
        return rest, rest_in, shift(right, 1), shift(left, -1)

    def parts_of(width):
        return [(chunk, width), (3 * chunk, width)] * 2

    w_gate, w_up, w_down = gate_weight[0], up_weight[0], jnp.transpose(down_weight[0])
    *parts, restored_down = call(
        functools.partial(down_kernel, grid),
        parts_of(ff) + [(ff, feat)],
        scratch=[pltpu.VMEM((8 * chunk, feat), BF)],
        scalars=1,
        operands=2,
    )(who, recv_grads, w_down)
    grad_parts = sum_parts(*parts)
    rows, *parts, restored = call(
        functools.partial(gate_up_kernel, grid),
        [(8 * chunk, feat)] + parts_of(2 * ff) + [(2, ff, feat)],
        scalars=1,
        operands=4,
    )(who, recv_rows, saved_gate_up, w_gate, w_up)
    (own,) = call(activate_kernel, [(chunk, 3 * ff)], operands=8)(*sum_parts(*parts), *grad_parts)

    left, right, own_other = lax.optimization_barrier((shift(own, 1), shift(own, -1), core_swap(own)))
    far = (shift(left[:mid], 1), shift(right[mid:], -1))
    low, high, right_other, left_other = lax.optimization_barrier(
        (*far, core_swap(right), core_swap(left))
    )
    far = jnp.concatenate([low, high], axis=0)
    mine = (far, own, right, left)
    other = (core_swap(far), own_other, right_other, left_other)

    out, grads = call(
        back_kernel,
        [(8, chunk, 2 * feat), (8 * chunk, 2 * ff)],
        scratch=[
            pltpu.VMEM((8 * chunk, ff), BF),
            pltpu.VMEM((8 * chunk, feat), BF),
            pltpu.VMEM((8 * chunk, feat), BF),
        ],
        scalars=1,
        operands=13,
        megabytes=40,
    )(who, *mine, *other, w_gate, w_up, w_down, restored, restored_down)

    out = exchange(out.reshape(nxz, out_rows, 2 * feat), along_xz)
    gate_grad = dot(rows, grads[:, :ff], TN).astype(BF)
    up_grad = dot(rows, grads[:, ff:], TN).astype(BF)
    (part,) = call(combine_kernel, [(seen, 2 * feat)], operands=4)(out, pick, pick_hi, pick_lo)
    part = exchange(part.reshape(ny, tok, 2 * feat), along_y)
    combined, token_grad = call(finish_kernel, [(tok, feat), (tok, feat)], operands=1)(part)
    return (combined, token_grad, gate_grad[None], up_grad[None])


def solution(mesh):
    placed = (
        P("expert", "dp"),
        P("expert", "dp"),
        P("expert", None),
        P("expert", None),
        P(),
        P("expert", "dp", None),
        P("expert", "dp", None),
        P("expert", None, "dp"),
        P(None, "dp", "expert"),
    )
    return jax.shard_map(
        body,
        mesh=mesh,
        in_specs=placed,
        out_specs=(
            P("expert", "dp"),
            P("expert", "dp"),
            P("expert", "dp", None),
            P("expert", "dp", None),
        ),
        check_vma=False,
    )
```

```python
import functools

import jax
import jax.numpy as jnp
import numpy as np
from jax import lax
from jax.experimental import pallas as pl
from jax.experimental.pallas import tpu as pltpu
from jax.sharding import PartitionSpec as P

BF = jnp.bfloat16
F32 = jnp.float32
GRID = {64: (4, 8, 2), 8: (2, 2, 2)}
NN = (((1,), (0,)), ((), ()))
NT = (((1,), (1,)), ((), ()))
TN = (((0,), (0,)), ((), ()))
LANES = 1024
TILE = 256


def dot(a, b, dims=NN):
    return lax.dot_general(a, b, dims, preferred_element_type=F32)


def call(kernel, outs, scratch=(), scalars=0, operands=0, megabytes=32):
    def of(shape, dtype=BF):
        return jax.ShapeDtypeStruct(shape, dtype)

    specs = [pl.BlockSpec(memory_space=pltpu.SMEM)] * scalars
    specs += [pl.BlockSpec(memory_space=pltpu.VMEM)] * operands
    return pl.pallas_call(
        kernel,
        out_shape=[of(*s) if isinstance(s[0], tuple) else of(s) for s in outs],
        in_specs=specs,
        out_specs=[pl.BlockSpec(memory_space=pltpu.VMEM)] * len(outs),
        scratch_shapes=list(scratch),
        compiler_params=pltpu.CompilerParams(vmem_limit_bytes=megabytes << 20),
    )


def pack_kernel(grid, ids_ref, weight_ref, tok_ref, cot_ref, out_ref):
    nx, ny, nz = grid
    nxz, ranks = nx * nz, nx * ny * nz
    tok, topk = ids_ref.shape
    ids = ids_ref[...]
    x, y, z = lax.div(ids, ny * nz), lax.rem(lax.div(ids, nz), ny), lax.rem(ids, nz)
    column = (x * nz + z) * ny + y
    lane = lax.broadcasted_iota(jnp.int32, (tok, ranks), 1)
    member = jnp.zeros((tok, ranks), F32)
    share = jnp.zeros((tok, ranks), F32)
    for k in range(topk):
        same = column[:, k : k + 1] == lane
        member = member + jnp.where(same, 1.0, 0.0)
        share = share + jnp.where(same, weight_ref[:, k : k + 1], 0.0)
    row = lax.broadcasted_iota(jnp.int32, (tok, tok), 0)
    col = lax.broadcasted_iota(jnp.int32, (tok, tok), 1)
    before = dot(jnp.where(col <= row, 1.0, 0.0).astype(BF), member.astype(BF))
    place = jnp.where(member > 0.5, before - 1.0, -1.0).astype(BF)
    hi = share.astype(BF)
    lo = (share - hi.astype(F32)).astype(BF)
    source = lax.broadcasted_iota(jnp.int32, (ranks, nxz * 128), 0)
    target = lax.broadcasted_iota(jnp.int32, (ranks, nxz * 128), 1)
    base = lax.div(source, ny) * 128 + lax.rem(source, ny) + 64
    meta = jnp.zeros((tok, nxz * 128), F32)
    for k, part in enumerate((place, hi, lo)):
        meta = meta + dot(part, jnp.where(target == base + k * ny, 1.0, 0.0).astype(BF))
    feat = tok_ref.shape[1]
    assert feat == 448
    last = jnp.concatenate([tok_ref[:, 384:448].astype(F32), jnp.zeros((tok, 64), F32)], axis=1)
    for i in range(nxz):
        out_ref[i, :, 0:384] = tok_ref[:, 0:384]
        out_ref[i, :, 384:512] = (meta[:, i * 128 : (i + 1) * 128] + last).astype(BF)
        out_ref[i, :, 512 : 512 + feat] = cot_ref[...]


def select_kernel(first_ref, want_ref, out_ref, pick_ref, hi_ref, lo_ref):
    ny, rows, width = out_ref.shape
    feat = width // 2
    nxz, tok, _ = first_ref.shape
    seen = nxz * tok
    tokens = first_ref[:, :, 0:feat].reshape(seen, feat)
    cots = first_ref[:, :, 512 : 512 + feat].reshape(seen, feat)
    meta = jnp.transpose(first_ref[:, :, 384:512].reshape(seen, 128).astype(F32))
    want = want_ref[...]
    both = jnp.concatenate([cots, cots], axis=0)
    for q in range(ny):
        hit = meta[64 + q : 65 + q] == want
        pick = jnp.where(hit, 1.0, 0.0).astype(BF)
        hi = jnp.where(hit, meta[64 + ny + q : 65 + ny + q], 0.0).astype(BF)
        lo = jnp.where(hit, meta[64 + 2 * ny + q : 65 + 2 * ny + q], 0.0).astype(BF)
        span = pl.ds(q * rows, rows)
        pick_ref[span, :] = pick
        hi_ref[span, :] = hi
        lo_ref[span, :] = lo
        out_ref[q, :, 0:feat] = dot(pick, tokens).astype(BF)
        out_ref[q, :, feat:width] = dot(jnp.concatenate([hi, lo], axis=1), both).astype(BF)


def chunk_at(h, c, p):
    half = c if p < 4 else 1 - c
    return half * 4 + lax.rem(h + (2, 0, 1, 3)[p % 4], 4)


def block_of(ref, g, chunk):
    per = ref.shape[1] // chunk
    if per == 1:
        return ref.at[g]
    return ref.at[lax.div(g, per), pl.ds(lax.rem(g, per) * chunk, chunk)]


def products_kernel(
    grid, who_ref, recv_ref, s0, s1, s2a, s2b, s3, gate_ref, up_ref, down_ref,
    rows_ref, far_ref, rest_ref, far_out_ref, rest_out_ref, restored_ref, grads_ref,
):
    nx, ny, nz = grid
    feat, ff = gate_ref.shape
    chunk = far_ref.shape[0]
    target, h, c, my_x, my_z = (who_ref[i] for i in range(5))
    for p in range(8):
        block = block_of(recv_ref, chunk_at(h, c, p), chunk)
        rows_ref[p * chunk : (p + 1) * chunk, :] = block[:, 0:feat]
        grads_ref[p * chunk : (p + 1) * chunk, :] = block[:, feat : 2 * feat]

    def store(k, j, value):
        at = pl.ds(pl.multiple_of(k * ff + j * TILE, TILE), TILE)
        value = value.astype(BF)
        far_ref[:, at] = value[0:chunk]
        rest_ref[:, at] = value[chunk : 4 * chunk]
        far_out_ref[:, at] = value[4 * chunk : 5 * chunk]
        rest_out_ref[:, at] = value[5 * chunk :]

    tiles = ff // TILE

    @pl.when(target == 0)
    def _():
        @pl.loop(0, tiles)
        def _(j):
            at = pl.ds(pl.multiple_of(j * TILE, TILE), TILE)
            store(0, j, dot(rows_ref[...], gate_ref[:, at]))
            store(1, j, dot(rows_ref[...], up_ref[:, at]))
            store(2, j, dot(grads_ref[...], down_ref[:, at]))

    @pl.when(target == 1)
    def _():
        n = s0.shape[0] // (nz * ny)
        half = ny * n
        for k in range(nx):
            for other in range(nz):
                x = lax.rem(my_x - k + nx, nx)
                z = 1 - my_z if other else my_z
                source = ((s0, s0), (s1, s1), (s2a, s2b), (s3, s3))[k][other]
                start = 0 if k == 2 else other * half
                for y in range(ny):
                    to = pl.ds(pl.multiple_of(((x * ny + y) * nz + z) * n, n), n)
                    r = start + y * n
                    for m in range(3):
                        restored_ref[m, to, :] = source[r : r + n, m * feat : (m + 1) * feat]

        @pl.loop(0, tiles)
        def _(j):
            at = pl.ds(pl.multiple_of(j * TILE, TILE), TILE)
            store(0, j, dot(rows_ref[...], restored_ref[0, at, :], NT))
            store(1, j, dot(rows_ref[...], restored_ref[1, at, :], NT))
            store(2, j, dot(grads_ref[...], restored_ref[2, at, :], NT))


def activate_kernel(own_ref, other_ref, left_ref, right_ref, out_ref):
    ff = out_ref.shape[1] // 3
    rows = out_ref.shape[0]

    @pl.loop(0, ff // TILE)
    def _(j):
        def total(k):
            at = pl.ds(pl.multiple_of(k * ff + j * TILE, TILE), TILE)
            near = own_ref[0:rows, at].astype(F32) + other_ref[0:rows, at].astype(F32)
            return near + (left_ref[:, at].astype(F32) + right_ref[:, at].astype(F32))

        gate, up, dh = total(0), total(1), total(2)
        sig = jax.nn.sigmoid(gate)
        values = (
            gate * sig * up,
            dh * up * sig * (1.0 + gate * (1.0 - sig)),
            dh * gate * sig,
        )
        for k, value in enumerate(values):
            at = pl.ds(pl.multiple_of(k * ff + j * TILE, TILE), TILE)
            out_ref[:, at] = value.astype(BF)


def back_kernel(*refs):
    who_ref, parts = refs[0], refs[1:9]
    gate_ref, up_ref, down_ref, restored_ref, out_ref, grads_ref, hidden_ref, y_ref, dx_ref = refs[9:]
    feat, ff = gate_ref.shape
    chunk = parts[0].shape[0]
    target, h, c = who_ref[0], who_ref[1], who_ref[2]
    for p in range(8):
        span = slice(p * chunk, (p + 1) * chunk)
        hidden_ref[span, :] = parts[p][:, 0:ff]
        grads_ref[span, :] = parts[p][:, ff : 3 * ff]

    @pl.when(target == 0)
    def _():
        y_ref[...] = dot(hidden_ref[...], down_ref[...], NT).astype(BF)
        dx_ref[...] = (
            dot(grads_ref[:, 0:ff], gate_ref[...], NT) + dot(grads_ref[:, ff : 2 * ff], up_ref[...], NT)
        ).astype(BF)

    @pl.when(target == 1)
    def _():
        y_ref[...] = dot(hidden_ref[...], restored_ref[2]).astype(BF)
        dx_ref[...] = (
            dot(grads_ref[:, 0:ff], restored_ref[0]) + dot(grads_ref[:, ff : 2 * ff], restored_ref[1])
        ).astype(BF)

    for p in range(8):
        block = block_of(out_ref, chunk_at(h, c, p), chunk)
        span = slice(p * chunk, (p + 1) * chunk)
        block[:, 0:feat] = y_ref[span, :]
        block[:, feat : 2 * feat] = dx_ref[span, :]


def combine_kernel(recv_ref, pick_ref, hi_ref, lo_ref, out_ref):
    blocks, out_rows, width = recv_ref.shape
    feat = width // 2
    rows = recv_ref[...].reshape(blocks * out_rows, width)
    y = dot(hi_ref[...], rows[:, 0:feat], TN) + dot(lo_ref[...], rows[:, 0:feat], TN)
    out_ref[:, 0:feat] = y.astype(BF)
    out_ref[:, feat:width] = dot(pick_ref[...], rows[:, feat:width], TN).astype(BF)


def finish_kernel(recv_ref, out_ref, grad_ref):
    feat = out_ref.shape[1]
    total = jnp.sum(recv_ref[...].astype(F32), axis=0)
    out_ref[...] = total[:, 0:feat].astype(BF)
    grad_ref[...] = total[:, feat : 2 * feat].astype(BF)


def core_swap(x):
    return lax.ppermute(x, "dp", [(i, i ^ 1) for i in range(8)])


def shift(x, k):
    return lax.ppermute(
        x, "dp", [(2 * h + c, 2 * ((h + k) % 4) + c) for h in range(4) for c in range(2)]
    )


def add(a, b):
    return (a.astype(F32) + b.astype(F32)).astype(BF)


def body(
    tokens,
    cotangent,
    expert_ids,
    route_weight,
    replaced,
    gate_weight,
    up_weight,
    down_weight,
    backup,
):
    ranks = lax.axis_size("expert")
    grid = nx, ny, nz = GRID[ranks]
    nxz = nx * nz
    along_y = [
        [(x * ny + y) * nz + z for y in range(ny)] for x in range(nx) for z in range(nz)
    ]
    along_xz = [
        [(x * ny + y) * nz + z for x in range(nx) for z in range(nz)] for y in range(ny)
    ]

    def exchange(v, groups):
        flat = v.reshape(-1, v.shape[-1])
        flat = lax.all_to_all(flat, "expert", 0, 0, axis_index_groups=groups, tiled=True)
        return flat.reshape(v.shape)

    def rank(x, y, z):
        return ((x % nx) * ny + y) * nz + z % nz

    def step(v, dx, dz):
        pairs = [
            (rank(x, y, z), rank(x + dx, y, z + dz))
            for x in range(nx) for y in range(ny) for z in range(nz)
        ]
        return lax.ppermute(v, "expert", pairs)

    tok, topk = expert_ids.shape
    feat = tokens.shape[1]
    ff = gate_weight.shape[2]
    ffr = ff // ranks
    capacity = min(tok, 5 * tok * topk // (2 * ranks))
    chunk = ranks * capacity // 8
    me, expert = lax.axis_index("dp"), lax.axis_index("expert")
    who = jnp.stack(
        [
            (expert == replaced[0]).astype(jnp.int32),
            me // 2,
            me % 2,
            expert // (ny * nz),
            expert % nz,
        ]
    ).astype(jnp.int32)

    saved = jnp.transpose(backup, (2, 0, 1)).reshape(ffr, 3 * feat)
    saved = exchange(jnp.broadcast_to(saved, (ny, ffr, 3 * feat)), along_y)
    saved = saved.reshape(ny * ffr, 3 * feat)
    both_z = jnp.concatenate([saved, step(saved, 0, 1)], axis=0)

    (first,) = call(functools.partial(pack_kernel, grid), [(nxz, tok, LANES)], operands=4)(
        expert_ids, route_weight, tokens, cotangent
    )
    first, saved = lax.optimization_barrier((first, saved))
    first = exchange(first, along_xz)

    out_rows, seen = nxz * capacity, nxz * tok
    row, col = np.arange(out_rows)[:, None], np.arange(seen)[None, :]
    want = np.where(row // capacity == col // tok, row % capacity, -2).astype(np.float32)
    table = (ny * out_rows, seen)
    send, pick, pick_hi, pick_lo = call(
        select_kernel, [(ny, out_rows, 2 * feat), table, table, table], operands=2
    )(first, want)
    recv = exchange(send, along_y)
    before, after = step(both_z, 1, 0), step(both_z, -1, 0)
    two_before = step(before[: ny * ffr], 1, 0), step(after[ny * ffr :], -1, 0)

    w_gate, w_up, w_down = gate_weight[0], up_weight[0], jnp.transpose(down_weight[0])
    wide = 3 * ff
    rows, far, rest, far_out, rest_out, restored = call(
        functools.partial(products_kernel, grid),
        [
            (8 * chunk, feat), (chunk, wide), (3 * chunk, wide),
            (chunk, wide), (3 * chunk, wide), (3, ff, feat),
        ],
        scratch=[pltpu.VMEM((8 * chunk, feat), BF)],
        scalars=1,
        operands=9,
        megabytes=40,
    )(who, recv, both_z, before, *two_before, after, w_gate, w_up, w_down)

    mid = chunk // 2
    far = add(far, core_swap(far_out))
    rest_in = core_swap(rest_out)
    from_left, from_right = shift(far[:mid], 1), shift(far[mid:], -1)
    sides = add(rest[chunk:], rest_in[chunk:])
    right, left = sides[:chunk], sides[chunk:]
    right = jnp.concatenate([add(right[:mid], from_left), right[mid:]], axis=0)
    left = jnp.concatenate([left[:mid], add(left[mid:], from_right)], axis=0)
    from_left, from_right = shift(right, 1), shift(left, -1)
    (own,) = call(activate_kernel, [(chunk, wide)], operands=4)(
        rest, rest_in, from_left, from_right
    )

    left, right, own_other = lax.optimization_barrier((shift(own, 1), shift(own, -1), core_swap(own)))
    far = (shift(left[:mid], 1), shift(right[mid:], -1))
    low, high, right_other, left_other = lax.optimization_barrier(
        (*far, core_swap(right), core_swap(left))
    )
    far = jnp.concatenate([low, high], axis=0)
    mine = (far, own, right, left)
    other = (core_swap(far), own_other, right_other, left_other)

    out, grads = call(
        back_kernel,
        [(ny, out_rows, 2 * feat), (8 * chunk, 2 * ff)],
        scratch=[
            pltpu.VMEM((8 * chunk, ff), BF),
            pltpu.VMEM((8 * chunk, feat), BF),
            pltpu.VMEM((8 * chunk, feat), BF),
        ],
        scalars=1,
        operands=12,
        megabytes=40,
    )(who, *mine, *other, w_gate, w_up, w_down, restored)

    out = exchange(out, along_y)
    gate_grad = dot(rows, grads[:, :ff], TN).astype(BF)
    up_grad = dot(rows, grads[:, ff:], TN).astype(BF)
    (part,) = call(combine_kernel, [(seen, 2 * feat)], operands=4)(out, pick, pick_hi, pick_lo)
    part = exchange(part.reshape(nxz, tok, 2 * feat), along_xz)
    combined, token_grad = call(finish_kernel, [(tok, feat), (tok, feat)], operands=1)(part)
    return (combined, token_grad, gate_grad[None], up_grad[None])


def solution(mesh):
    placed = (
        P("expert", "dp"),
        P("expert", "dp"),
        P("expert", None),
        P("expert", None),
        P(),
        P("expert", "dp", None),
        P("expert", "dp", None),
        P("expert", None, "dp"),
        P(None, "dp", "expert"),
    )
    return jax.shard_map(
        body,
        mesh=mesh,
        in_specs=placed,
        out_specs=(
            P("expert", "dp"),
            P("expert", "dp"),
            P("expert", "dp", None),
            P("expert", "dp", None),
        ),
        check_vma=False,
    )
```

```python
import functools

import jax
import jax.numpy as jnp
import numpy as np
from jax import lax
from jax.experimental import pallas as pl
from jax.experimental.pallas import tpu as pltpu
from jax.sharding import PartitionSpec as P

BF = jnp.bfloat16
F32 = jnp.float32
GRID = {64: (4, 8, 2), 8: (2, 2, 2)}
NN = (((1,), (0,)), ((), ()))
NT = (((1,), (1,)), ((), ()))
TN = (((0,), (0,)), ((), ()))
LANES = 1024
TILE = 256


def dot(a, b, dims=NN):
    return lax.dot_general(a, b, dims, preferred_element_type=F32)


def call(kernel, outs, scratch=(), scalars=0, operands=0, megabytes=32):
    def of(shape, dtype=BF):
        return jax.ShapeDtypeStruct(shape, dtype)

    specs = [pl.BlockSpec(memory_space=pltpu.SMEM)] * scalars
    specs += [pl.BlockSpec(memory_space=pltpu.VMEM)] * operands
    return pl.pallas_call(
        kernel,
        out_shape=[of(*s) if isinstance(s[0], tuple) else of(s) for s in outs],
        in_specs=specs,
        out_specs=[pl.BlockSpec(memory_space=pltpu.VMEM)] * len(outs),
        scratch_shapes=list(scratch),
        compiler_params=pltpu.CompilerParams(vmem_limit_bytes=megabytes << 20),
    )


def pack_kernel(grid, ids_ref, weight_ref, tok_ref, cot_ref, out_ref):
    nx, ny, nz = grid
    nxz, ranks = nx * nz, nx * ny * nz
    tok, topk = ids_ref.shape
    ids = ids_ref[...]
    x, y, z = lax.div(ids, ny * nz), lax.rem(lax.div(ids, nz), ny), lax.rem(ids, nz)
    column = y * nxz + x * nz + z
    lane = lax.broadcasted_iota(jnp.int32, (tok, ranks), 1)
    member = jnp.zeros((tok, ranks), F32)
    share = jnp.zeros((tok, ranks), F32)
    for k in range(topk):
        same = column[:, k : k + 1] == lane
        member = member + jnp.where(same, 1.0, 0.0)
        share = share + jnp.where(same, weight_ref[:, k : k + 1], 0.0)
    row = lax.broadcasted_iota(jnp.int32, (tok, tok), 0)
    col = lax.broadcasted_iota(jnp.int32, (tok, tok), 1)
    before = dot(jnp.where(col <= row, 1.0, 0.0).astype(BF), member.astype(BF))
    place = jnp.where(member > 0.5, before - 1.0, -1.0).astype(BF)
    hi = share.astype(BF)
    lo = (share - hi.astype(F32)).astype(BF)
    source = lax.broadcasted_iota(jnp.int32, (ranks, ny * 128), 0)
    target = lax.broadcasted_iota(jnp.int32, (ranks, ny * 128), 1)
    base = lax.div(source, nxz) * 128 + lax.rem(source, nxz) + 64
    meta = jnp.zeros((tok, ny * 128), F32)
    for k, part in enumerate((place, hi, lo)):
        meta = meta + dot(part, jnp.where(target == base + k * nxz, 1.0, 0.0).astype(BF))
    feat = tok_ref.shape[1]
    assert feat == 448
    last = jnp.concatenate([tok_ref[:, 384:448].astype(F32), jnp.zeros((tok, 64), F32)], axis=1)
    for i in range(ny):
        out_ref[i, :, 0:384] = tok_ref[:, 0:384]
        out_ref[i, :, 384:512] = (meta[:, i * 128 : (i + 1) * 128] + last).astype(BF)
        out_ref[i, :, 512 : 512 + feat] = cot_ref[...]


def tables(meta_ref, want, q, count):
    hit = meta_ref[q : q + 1, :] == want
    hi = jnp.where(hit, meta_ref[count + q : count + q + 1, :], 0.0).astype(BF)
    lo = jnp.where(hit, meta_ref[2 * count + q : 2 * count + q + 1, :], 0.0).astype(BF)
    return jnp.where(hit, 1.0, 0.0).astype(BF), hi, lo


def select_kernel(first_ref, want_ref, out_ref, meta_ref):
    nxz, rows, width = out_ref.shape
    feat = width // 2
    ny, tok, _ = first_ref.shape
    seen = ny * tok
    tokens = first_ref[:, :, 0:feat].reshape(seen, feat)
    cots = first_ref[:, :, 512 : 512 + feat].reshape(seen, feat)
    meta = jnp.transpose(first_ref[:, :, 384:512].reshape(seen, 128).astype(F32))
    meta_ref[...] = meta[64:128]
    want = want_ref[...]
    both = jnp.concatenate([cots, cots], axis=0)
    for q in range(nxz):
        pick, hi, lo = tables(meta_ref, want, q, nxz)
        out_ref[q, :, 0:feat] = dot(pick, tokens).astype(BF)
        out_ref[q, :, feat:width] = dot(jnp.concatenate([hi, lo], axis=1), both).astype(BF)


def chunk_at(h, c, p):
    half = c if p < 4 else 1 - c
    return half * 4 + lax.rem(h + (2, 0, 1, 3)[p % 4], 4)


def products_kernel(
    grid, who_ref, recv_ref, s0, t0, s1, t1, s2, t2, s3, t3, gate_ref, up_ref, down_ref,
    rows_ref, far_ref, rest_ref, far_out_ref, rest_out_ref, restored_ref, grads_ref,
):
    nx, ny, nz = grid
    feat, ff = gate_ref.shape
    chunk = far_ref.shape[0]
    target, h, c, my_x, my_z = (who_ref[i] for i in range(5))
    for p in range(8):
        g = chunk_at(h, c, p)
        rows_ref[p * chunk : (p + 1) * chunk, :] = recv_ref[g, :, 0:feat]
        grads_ref[p * chunk : (p + 1) * chunk, :] = recv_ref[g, :, feat : 2 * feat]

    def store(k, j, value):
        at = pl.ds(pl.multiple_of(k * ff + j * TILE, TILE), TILE)
        value = value.astype(BF)
        far_ref[:, at] = value[0:chunk]
        rest_ref[:, at] = value[chunk : 4 * chunk]
        far_out_ref[:, at] = value[4 * chunk : 5 * chunk]
        rest_out_ref[:, at] = value[5 * chunk :]

    tiles = ff // TILE

    @pl.when(target == 0)
    def _():
        @pl.loop(0, tiles)
        def _(j):
            at = pl.ds(pl.multiple_of(j * TILE, TILE), TILE)
            store(0, j, dot(rows_ref[...], gate_ref[:, at]))
            store(1, j, dot(rows_ref[...], up_ref[:, at]))
            store(2, j, dot(grads_ref[...], down_ref[:, at]))

    @pl.when(target == 1)
    def _():
        n = s0.shape[0] // ny
        for k, sources in enumerate(((s0, t0), (s1, t1), (s2, t2), (s3, t3))):
            for other in range(nz):
                x = lax.rem(my_x - k + nx, nx)
                z = 1 - my_z if other else my_z
                for y in range(ny):
                    to = pl.ds(pl.multiple_of(((x * ny + y) * nz + z) * n, n), n)
                    for m in range(3):
                        restored_ref[m, to, :] = sources[other][y * n : (y + 1) * n, m * feat : (m + 1) * feat]

        @pl.loop(0, tiles)
        def _(j):
            at = pl.ds(pl.multiple_of(j * TILE, TILE), TILE)
            store(0, j, dot(rows_ref[...], restored_ref[0, at, :], NT))
            store(1, j, dot(rows_ref[...], restored_ref[1, at, :], NT))
            store(2, j, dot(grads_ref[...], restored_ref[2, at, :], NT))


def activate_kernel(own_ref, other_ref, left_ref, right_ref, out_ref):
    ff = out_ref.shape[1] // 3
    rows = out_ref.shape[0]

    @pl.loop(0, ff // TILE)
    def _(j):
        def total(k):
            at = pl.ds(pl.multiple_of(k * ff + j * TILE, TILE), TILE)
            near = own_ref[0:rows, at].astype(F32) + other_ref[0:rows, at].astype(F32)
            return near + (left_ref[:, at].astype(F32) + right_ref[:, at].astype(F32))

        gate, up, dh = total(0), total(1), total(2)
        sig = jax.nn.sigmoid(gate)
        values = (
            gate * sig * up,
            dh * up * sig * (1.0 + gate * (1.0 - sig)),
            dh * gate * sig,
        )
        for k, value in enumerate(values):
            at = pl.ds(pl.multiple_of(k * ff + j * TILE, TILE), TILE)
            out_ref[:, at] = value.astype(BF)


def back_kernel(*refs):
    who_ref, parts = refs[0], refs[1:9]
    gate_ref, up_ref, down_ref, restored_ref, out_ref, grads_ref, hidden_ref, y_ref, dx_ref = refs[9:]
    feat, ff = gate_ref.shape
    chunk = out_ref.shape[1]
    target, h, c = who_ref[0], who_ref[1], who_ref[2]
    for p in range(8):
        span = slice(p * chunk, (p + 1) * chunk)
        hidden_ref[span, :] = parts[p][:, 0:ff]
        grads_ref[span, :] = parts[p][:, ff : 3 * ff]

    @pl.when(target == 0)
    def _():
        y_ref[...] = dot(hidden_ref[...], down_ref[...], NT).astype(BF)
        dx_ref[...] = (
            dot(grads_ref[:, 0:ff], gate_ref[...], NT) + dot(grads_ref[:, ff : 2 * ff], up_ref[...], NT)
        ).astype(BF)

    @pl.when(target == 1)
    def _():
        y_ref[...] = dot(hidden_ref[...], restored_ref[2]).astype(BF)
        dx_ref[...] = (
            dot(grads_ref[:, 0:ff], restored_ref[0]) + dot(grads_ref[:, ff : 2 * ff], restored_ref[1])
        ).astype(BF)

    for p in range(8):
        g = chunk_at(h, c, p)
        span = slice(p * chunk, (p + 1) * chunk)
        out_ref[g, :, 0:feat] = y_ref[span, :]
        out_ref[g, :, feat : 2 * feat] = dx_ref[span, :]


def combine_kernel(recv_ref, meta_ref, want_ref, out_ref, pick_ref, share_ref):
    nxz, out_rows, width = recv_ref.shape
    feat = width // 2
    total = nxz * out_rows
    for q in range(nxz):
        span = pl.ds(q * out_rows, out_rows)
        pick_ref[span, :], share_ref[0, span, :], share_ref[1, span, :] = tables(
            meta_ref, want_ref[...], q, nxz
        )
    rows = recv_ref[...].reshape(total, width)
    y = dot(share_ref[0], rows[:, 0:feat], TN) + dot(share_ref[1], rows[:, 0:feat], TN)
    out_ref[:, 0:feat] = y.astype(BF)
    out_ref[:, feat:width] = dot(pick_ref[...], rows[:, feat:width], TN).astype(BF)


def finish_kernel(recv_ref, out_ref, grad_ref):
    feat = out_ref.shape[1]
    total = jnp.sum(recv_ref[...].astype(F32), axis=0)
    out_ref[...] = total[:, 0:feat].astype(BF)
    grad_ref[...] = total[:, feat : 2 * feat].astype(BF)


def core_swap(x):
    return lax.ppermute(x, "dp", [(i, i ^ 1) for i in range(8)])


def shift(x, k):
    return lax.ppermute(
        x, "dp", [(2 * h + c, 2 * ((h + k) % 4) + c) for h in range(4) for c in range(2)]
    )


def add(a, b):
    return (a.astype(F32) + b.astype(F32)).astype(BF)


def body(
    tokens,
    cotangent,
    expert_ids,
    route_weight,
    replaced,
    gate_weight,
    up_weight,
    down_weight,
    backup,
):
    ranks = lax.axis_size("expert")
    grid = nx, ny, nz = GRID[ranks]
    nxz = nx * nz
    along_y = [
        [(x * ny + y) * nz + z for y in range(ny)] for x in range(nx) for z in range(nz)
    ]
    along_xz = [
        [(x * ny + y) * nz + z for x in range(nx) for z in range(nz)] for y in range(ny)
    ]

    def exchange(v, groups):
        flat = v.reshape(-1, v.shape[-1])
        flat = lax.all_to_all(flat, "expert", 0, 0, axis_index_groups=groups, tiled=True)
        return flat.reshape(v.shape)

    def rank(x, y, z):
        return ((x % nx) * ny + y) * nz + z % nz

    def step(v, dx, dz):
        pairs = [
            (rank(x, y, z), rank(x + dx, y, z + dz))
            for x in range(nx) for y in range(ny) for z in range(nz)
        ]
        return lax.ppermute(v, "expert", pairs)

    tok, topk = expert_ids.shape
    feat = tokens.shape[1]
    ff = gate_weight.shape[2]
    ffr = ff // ranks
    capacity = min(tok, 5 * tok * topk // (2 * ranks))
    chunk = ranks * capacity // 8
    me, expert = lax.axis_index("dp"), lax.axis_index("expert")
    who = jnp.stack(
        [
            (expert == replaced[0]).astype(jnp.int32),
            me // 2,
            me % 2,
            expert // (ny * nz),
            expert % nz,
        ]
    ).astype(jnp.int32)

    saved = jnp.transpose(backup, (2, 0, 1)).reshape(ffr, 3 * feat)
    saved = jnp.pad(saved, ((0, 0), (0, -3 * feat % 128)))
    saved = exchange(jnp.broadcast_to(saved, (ny, *saved.shape)), along_y)
    saved = saved.reshape(ny * ffr, -1)
    (first,) = call(functools.partial(pack_kernel, grid), [(ny, tok, LANES)], operands=4)(
        expert_ids, route_weight, tokens, cotangent
    )
    first, saved = lax.optimization_barrier((first, saved))
    other_z = step(saved, 0, 1)
    before, after = step(saved, 1, 0), step(saved, -1, 0)
    first = exchange(first, along_y)
    first, other_z, before, after = lax.optimization_barrier((first, other_z, before, after))
    before_z, after_z = step(other_z, 1, 0), step(other_z, -1, 0)
    blocks = (
        saved, other_z, before, before_z, step(before, 1, 0), step(after_z, -1, 0), after, after_z,
    )

    out_rows, seen = ny * capacity, ny * tok
    row, col = np.arange(out_rows)[:, None], np.arange(seen)[None, :]
    want = np.where(row // capacity == col // tok, row % capacity, -2).astype(np.float32)
    send, meta = call(
        select_kernel, [(nxz, out_rows, 2 * feat), ((64, seen), F32)], operands=2
    )(first, want)
    recv = exchange(send, along_xz)

    w_gate, w_up, w_down = gate_weight[0], up_weight[0], jnp.transpose(down_weight[0])
    wide = 3 * ff
    rows, far, rest, far_out, rest_out, restored = call(
        functools.partial(products_kernel, grid),
        [
            (8 * chunk, feat), (chunk, wide), (3 * chunk, wide),
            (chunk, wide), (3 * chunk, wide), (3, ff, feat),
        ],
        scratch=[pltpu.VMEM((8 * chunk, feat), BF)],
        scalars=1,
        operands=12,
        megabytes=40,
    )(who, recv, *blocks, w_gate, w_up, w_down)

    mid = chunk // 2
    far = add(far, core_swap(far_out))
    rest_in = core_swap(rest_out)
    from_left, from_right = shift(far[:mid], 1), shift(far[mid:], -1)
    sides = add(rest[chunk:], rest_in[chunk:])
    right, left = sides[:chunk], sides[chunk:]
    right = jnp.concatenate([add(right[:mid], from_left), right[mid:]], axis=0)
    left = jnp.concatenate([left[:mid], add(left[mid:], from_right)], axis=0)
    from_left, from_right = shift(right, 1), shift(left, -1)
    (own,) = call(activate_kernel, [(chunk, wide)], operands=4)(
        rest, rest_in, from_left, from_right
    )

    left, right = shift(own, 1), shift(own, -1)
    far = jnp.concatenate([shift(left[:mid], 1), shift(right[mid:], -1)], axis=0)
    mine = (far, own, right, left)
    other = tuple(core_swap(v) for v in mine)

    out, grads = call(
        back_kernel,
        [(8, chunk, 2 * feat), (8 * chunk, 2 * ff)],
        scratch=[
            pltpu.VMEM((8 * chunk, ff), BF),
            pltpu.VMEM((8 * chunk, feat), BF),
            pltpu.VMEM((8 * chunk, feat), BF),
        ],
        scalars=1,
        operands=12,
        megabytes=40,
    )(who, *mine, *other, w_gate, w_up, w_down, restored)

    out = exchange(out.reshape(nxz, out_rows, 2 * feat), along_xz)
    gate_grad = dot(rows, grads[:, :ff], TN).astype(BF)
    up_grad = dot(rows, grads[:, ff:], TN).astype(BF)
    (part,) = call(
        combine_kernel,
        [(seen, 2 * feat)],
        scratch=[
            pltpu.VMEM((nxz * out_rows, seen), BF),
            pltpu.VMEM((2, nxz * out_rows, seen), BF),
        ],
        operands=3,
    )(out, meta, want)
    part = exchange(part.reshape(ny, tok, 2 * feat), along_y)
    combined, token_grad = call(finish_kernel, [(tok, feat), (tok, feat)], operands=1)(part)
    return (combined, token_grad, gate_grad[None], up_grad[None])


def solution(mesh):
    placed = (
        P("expert", "dp"),
        P("expert", "dp"),
        P("expert", None),
        P("expert", None),
        P(),
        P("expert", "dp", None),
        P("expert", "dp", None),
        P("expert", None, "dp"),
        P(None, "dp", "expert"),
    )
    return jax.shard_map(
        body,
        mesh=mesh,
        in_specs=placed,
        out_specs=(
            P("expert", "dp"),
            P("expert", "dp"),
            P("expert", "dp", None),
            P("expert", "dp", None),
        ),
        check_vma=False,
    )
```

```python
import functools

import jax
import jax.numpy as jnp
import numpy as np
from jax import lax
from jax.experimental import pallas as pl
from jax.experimental.pallas import tpu as pltpu
from jax.sharding import PartitionSpec as P

BF = jnp.bfloat16
F32 = jnp.float32
GRID = {64: (4, 8, 2), 8: (2, 2, 2)}
NN = (((1,), (0,)), ((), ()))
NT = (((1,), (1,)), ((), ()))
TN = (((0,), (0,)), ((), ()))
LANES = 1024
TILE = 256


def dot(a, b, dims=NN):
    return lax.dot_general(a, b, dims, preferred_element_type=F32)


def call(kernel, outs, scratch=(), scalars=0, left=0, operands=0, megabytes=12):
    def of(shape, dtype=BF):
        return jax.ShapeDtypeStruct(shape, dtype)

    specs = [pl.BlockSpec(memory_space=pltpu.SMEM)] * scalars
    specs += [pl.BlockSpec(memory_space=pltpu.HBM)] * left
    specs += [pl.BlockSpec(memory_space=pltpu.VMEM)] * operands
    return pl.pallas_call(
        kernel,
        out_shape=[of(*s) if isinstance(s[0], tuple) else of(s) for s in outs],
        in_specs=specs,
        out_specs=[pl.BlockSpec(memory_space=pltpu.VMEM)] * len(outs),
        scratch_shapes=list(scratch),
        compiler_params=pltpu.CompilerParams(vmem_limit_bytes=megabytes << 20),
    )


def pack_kernel(grid, ids_ref, weight_ref, tok_ref, cot_ref, out_ref):
    nx, ny, nz = grid
    nxz, ranks = nx * nz, nx * ny * nz
    tok, topk = ids_ref.shape
    ids = ids_ref[...]
    x, y, z = lax.div(ids, ny * nz), lax.rem(lax.div(ids, nz), ny), lax.rem(ids, nz)
    column = y * nxz + x * nz + z
    lane = lax.broadcasted_iota(jnp.int32, (tok, ranks), 1)
    member = jnp.zeros((tok, ranks), F32)
    share = jnp.zeros((tok, ranks), F32)
    for k in range(topk):
        same = column[:, k : k + 1] == lane
        member = member + jnp.where(same, 1.0, 0.0)
        share = share + jnp.where(same, weight_ref[:, k : k + 1], 0.0)
    row = lax.broadcasted_iota(jnp.int32, (tok, tok), 0)
    col = lax.broadcasted_iota(jnp.int32, (tok, tok), 1)
    before = dot(jnp.where(col <= row, 1.0, 0.0).astype(BF), member.astype(BF))
    place = jnp.where(member > 0.5, before - 1.0, -1.0).astype(BF)
    hi = share.astype(BF)
    lo = (share - hi.astype(F32)).astype(BF)
    source = lax.broadcasted_iota(jnp.int32, (ranks, ny * 128), 0)
    target = lax.broadcasted_iota(jnp.int32, (ranks, ny * 128), 1)
    base = lax.div(source, nxz) * 128 + lax.rem(source, nxz) + 64
    meta = jnp.zeros((tok, ny * 128), F32)
    for k, part in enumerate((place, hi, lo)):
        meta = meta + dot(part, jnp.where(target == base + k * nxz, 1.0, 0.0).astype(BF))
    feat = tok_ref.shape[1]
    assert feat == 448
    last = jnp.concatenate([tok_ref[:, 384:448].astype(F32), jnp.zeros((tok, 64), F32)], axis=1)
    for i in range(ny):
        out_ref[i, :, 0:384] = tok_ref[:, 0:384]
        out_ref[i, :, 384:512] = (meta[:, i * 128 : (i + 1) * 128] + last).astype(BF)
        out_ref[i, :, 512 : 512 + feat] = cot_ref[...]


def tables(meta_ref, want, q, count):
    hit = meta_ref[q : q + 1, :] == want
    hi = jnp.where(hit, meta_ref[count + q : count + q + 1, :], 0.0).astype(BF)
    lo = jnp.where(hit, meta_ref[2 * count + q : 2 * count + q + 1, :], 0.0).astype(BF)
    return jnp.where(hit, 1.0, 0.0).astype(BF), hi, lo


def select_kernel(first_ref, want_ref, out_ref, meta_ref):
    nxz, rows, width = out_ref.shape
    feat = width // 2
    ny, tok, _ = first_ref.shape
    seen = ny * tok
    tokens = first_ref[:, :, 0:feat].reshape(seen, feat)
    cots = first_ref[:, :, 512 : 512 + feat].reshape(seen, feat)
    meta = jnp.transpose(first_ref[:, :, 384:512].reshape(seen, 128).astype(F32))
    meta_ref[...] = meta[64:128]
    want = want_ref[...]
    both = jnp.concatenate([cots, cots], axis=0)
    for q in range(nxz):
        pick, hi, lo = tables(meta_ref, want, q, nxz)
        out_ref[q, :, 0:feat] = dot(pick, tokens).astype(BF)
        out_ref[q, :, feat:width] = dot(jnp.concatenate([hi, lo], axis=1), both).astype(BF)


def chunk_at(h, c, p):
    half = c if p < 4 else 1 - c
    return half * 4 + lax.rem(h + (2, 0, 1, 3)[p % 4], 4)


def restore_kernel(grid, who_ref, *refs):
    nx, ny, nz = grid
    *blocks, restored_ref, saved_ref, sems = refs
    feat = restored_ref.shape[2]
    n = saved_ref.shape[1] // ny

    @pl.when(who_ref[0] == 1)
    def _():
        my_x, my_z = who_ref[3], who_ref[4]
        copies = [pltpu.make_async_copy(b, saved_ref.at[i], sems.at[i]) for i, b in enumerate(blocks)]
        for copy in copies:
            copy.start()
        for i, copy in enumerate(copies):
            copy.wait()
            x = lax.rem(my_x - i % nx + nx, nx)
            z = my_z if i < nx else 1 - my_z
            for y in range(ny):
                to = pl.ds(pl.multiple_of(((x * ny + y) * nz + z) * n, n), n)
                for m in range(3):
                    restored_ref[m, to, :] = saved_ref[i, y * n : (y + 1) * n, m * feat : (m + 1) * feat]


def products_kernel(
    who_ref, recv_ref, restored_ref, gate_ref, up_ref, down_ref,
    rows_ref, far_ref, rest_ref, far_out_ref, rest_out_ref, grads_ref,
):
    feat, ff = gate_ref.shape
    chunk = far_ref.shape[0]
    target, h, c = who_ref[0], who_ref[1], who_ref[2]
    for p in range(8):
        g = chunk_at(h, c, p)
        rows_ref[p * chunk : (p + 1) * chunk, :] = recv_ref[g, :, 0:feat]
        grads_ref[p * chunk : (p + 1) * chunk, :] = recv_ref[g, :, feat : 2 * feat]

    def store(k, j, value):
        at = pl.ds(pl.multiple_of(k * ff + j * TILE, TILE), TILE)
        value = value.astype(BF)
        far_ref[:, at] = value[0:chunk]
        rest_ref[:, at] = value[chunk : 4 * chunk]
        far_out_ref[:, at] = value[4 * chunk : 5 * chunk]
        rest_out_ref[:, at] = value[5 * chunk :]

    tiles = ff // TILE

    @pl.when(target == 0)
    def _():
        @pl.loop(0, tiles)
        def _(j):
            at = pl.ds(pl.multiple_of(j * TILE, TILE), TILE)
            store(0, j, dot(rows_ref[...], gate_ref[:, at]))
            store(1, j, dot(rows_ref[...], up_ref[:, at]))
            store(2, j, dot(grads_ref[...], down_ref[:, at]))

    @pl.when(target == 1)
    def _():
        @pl.loop(0, tiles)
        def _(j):
            at = pl.ds(pl.multiple_of(j * TILE, TILE), TILE)
            store(0, j, dot(rows_ref[...], restored_ref[0, at, :], NT))
            store(1, j, dot(rows_ref[...], restored_ref[1, at, :], NT))
            store(2, j, dot(grads_ref[...], restored_ref[2, at, :], NT))


def activate_kernel(own_ref, other_ref, left_ref, right_ref, out_ref):
    ff = out_ref.shape[1] // 3
    rows = out_ref.shape[0]

    @pl.loop(0, ff // TILE)
    def _(j):
        def total(k):
            at = pl.ds(pl.multiple_of(k * ff + j * TILE, TILE), TILE)
            near = own_ref[0:rows, at].astype(F32) + other_ref[0:rows, at].astype(F32)
            return near + (left_ref[:, at].astype(F32) + right_ref[:, at].astype(F32))

        gate, up, dh = total(0), total(1), total(2)
        sig = jax.nn.sigmoid(gate)
        values = (
            gate * sig * up,
            dh * up * sig * (1.0 + gate * (1.0 - sig)),
            dh * gate * sig,
        )
        for k, value in enumerate(values):
            at = pl.ds(pl.multiple_of(k * ff + j * TILE, TILE), TILE)
            out_ref[:, at] = value.astype(BF)


def back_kernel(*refs):
    who_ref, parts = refs[0], refs[1:9]
    gate_ref, up_ref, down_ref, restored_ref, out_ref, grads_ref, hidden_ref, y_ref, dx_ref = refs[9:]
    feat, ff = gate_ref.shape
    chunk = out_ref.shape[1]
    target, h, c = who_ref[0], who_ref[1], who_ref[2]
    for p in range(8):
        span = slice(p * chunk, (p + 1) * chunk)
        hidden_ref[span, :] = parts[p][:, 0:ff]
        grads_ref[span, :] = parts[p][:, ff : 3 * ff]

    @pl.when(target == 0)
    def _():
        y_ref[...] = dot(hidden_ref[...], down_ref[...], NT).astype(BF)
        dx_ref[...] = (
            dot(grads_ref[:, 0:ff], gate_ref[...], NT) + dot(grads_ref[:, ff : 2 * ff], up_ref[...], NT)
        ).astype(BF)

    @pl.when(target == 1)
    def _():
        y_ref[...] = dot(hidden_ref[...], restored_ref[2]).astype(BF)
        dx_ref[...] = (
            dot(grads_ref[:, 0:ff], restored_ref[0]) + dot(grads_ref[:, ff : 2 * ff], restored_ref[1])
        ).astype(BF)

    for p in range(8):
        g = chunk_at(h, c, p)
        span = slice(p * chunk, (p + 1) * chunk)
        out_ref[g, :, 0:feat] = y_ref[span, :]
        out_ref[g, :, feat : 2 * feat] = dx_ref[span, :]


def combine_kernel(recv_ref, meta_ref, want_ref, out_ref, pick_ref, share_ref):
    nxz, out_rows, width = recv_ref.shape
    feat = width // 2
    total = nxz * out_rows
    for q in range(nxz):
        span = pl.ds(q * out_rows, out_rows)
        pick_ref[span, :], share_ref[0, span, :], share_ref[1, span, :] = tables(
            meta_ref, want_ref[...], q, nxz
        )
    rows = recv_ref[...].reshape(total, width)
    y = dot(share_ref[0], rows[:, 0:feat], TN) + dot(share_ref[1], rows[:, 0:feat], TN)
    out_ref[:, 0:feat] = y.astype(BF)
    out_ref[:, feat:width] = dot(pick_ref[...], rows[:, feat:width], TN).astype(BF)


def finish_kernel(recv_ref, out_ref, grad_ref):
    feat = out_ref.shape[1]
    total = jnp.sum(recv_ref[...].astype(F32), axis=0)
    out_ref[...] = total[:, 0:feat].astype(BF)
    grad_ref[...] = total[:, feat : 2 * feat].astype(BF)


def core_swap(x):
    return lax.ppermute(x, "dp", [(i, i ^ 1) for i in range(8)])


def shift(x, k):
    return lax.ppermute(
        x, "dp", [(2 * h + c, 2 * ((h + k) % 4) + c) for h in range(4) for c in range(2)]
    )


def add(a, b):
    return (a.astype(F32) + b.astype(F32)).astype(BF)


def body(
    tokens,
    cotangent,
    expert_ids,
    route_weight,
    replaced,
    gate_weight,
    up_weight,
    down_weight,
    backup,
):
    ranks = lax.axis_size("expert")
    grid = nx, ny, nz = GRID[ranks]
    nxz = nx * nz
    along_y = [
        [(x * ny + y) * nz + z for y in range(ny)] for x in range(nx) for z in range(nz)
    ]
    along_xz = [
        [(x * ny + y) * nz + z for x in range(nx) for z in range(nz)] for y in range(ny)
    ]

    def exchange(v, groups):
        flat = v.reshape(-1, v.shape[-1])
        flat = lax.all_to_all(flat, "expert", 0, 0, axis_index_groups=groups, tiled=True)
        return flat.reshape(v.shape)

    def rank(x, y, z):
        return ((x % nx) * ny + y) * nz + z % nz

    def step(v, dx, dz):
        pairs = [
            (rank(x, y, z), rank(x + dx, y, z + dz))
            for x in range(nx) for y in range(ny) for z in range(nz)
        ]
        return lax.ppermute(v, "expert", pairs)

    tok, topk = expert_ids.shape
    feat = tokens.shape[1]
    ff = gate_weight.shape[2]
    ffr = ff // ranks
    capacity = min(tok, 5 * tok * topk // (2 * ranks))
    chunk = ranks * capacity // 8
    me, expert = lax.axis_index("dp"), lax.axis_index("expert")
    who = jnp.stack(
        [
            (expert == replaced[0]).astype(jnp.int32),
            me // 2,
            me % 2,
            expert // (ny * nz),
            expert % nz,
        ]
    ).astype(jnp.int32)

    saved = jnp.transpose(backup, (2, 0, 1)).reshape(ffr, 3 * feat)
    saved = jnp.pad(saved, ((0, 0), (0, -3 * feat % 128)))
    saved = exchange(jnp.broadcast_to(saved, (ny, *saved.shape)), along_y)
    saved = saved.reshape(ny * ffr, -1)
    (first,) = call(functools.partial(pack_kernel, grid), [(ny, tok, LANES)], operands=4)(
        expert_ids, route_weight, tokens, cotangent
    )
    first, saved = lax.optimization_barrier((first, saved))
    other_z = step(saved, 0, 1)
    along_x = [step(saved, k, 0) for k in range(1, nx)]
    first = exchange(first, along_y)
    first, other_z, along_x = lax.optimization_barrier((first, other_z, along_x))
    blocks = [saved, *along_x, other_z, step(other_z, 1, 0), step(along_x[1], 0, 1), step(other_z, 3, 0)]

    out_rows, seen = ny * capacity, ny * tok
    row, col = np.arange(out_rows)[:, None], np.arange(seen)[None, :]
    want = np.where(row // capacity == col // tok, row % capacity, -2).astype(np.float32)
    send, meta = call(
        select_kernel, [(nxz, out_rows, 2 * feat), ((64, seen), F32)], operands=2
    )(first, want)
    recv = exchange(send, along_xz)

    w_gate, w_up, w_down = gate_weight[0], up_weight[0], jnp.transpose(down_weight[0])
    wide = 3 * ff
    (restored,) = call(
        functools.partial(restore_kernel, grid),
        [(3, ff, feat)],
        scratch=[pltpu.VMEM((8, *saved.shape), BF), pltpu.SemaphoreType.DMA((8,))],
        scalars=1,
        left=8,
        megabytes=52,
    )(who, *blocks)
    rows, far, rest, far_out, rest_out = call(
        products_kernel,
        [
            (8 * chunk, feat), (chunk, wide), (3 * chunk, wide),
            (chunk, wide), (3 * chunk, wide),
        ],
        scratch=[pltpu.VMEM((8 * chunk, feat), BF)],
        scalars=1,
        operands=5,
        megabytes=14,
    )(who, recv, restored, w_gate, w_up, w_down)

    mid = chunk // 2
    far = add(far, core_swap(far_out))
    rest_in = core_swap(rest_out)
    from_left, from_right = shift(far[:mid], 1), shift(far[mid:], -1)
    sides = add(rest[chunk:], rest_in[chunk:])
    right, left = sides[:chunk], sides[chunk:]
    right = jnp.concatenate([add(right[:mid], from_left), right[mid:]], axis=0)
    left = jnp.concatenate([left[:mid], add(left[mid:], from_right)], axis=0)
    from_left, from_right = shift(right, 1), shift(left, -1)
    (own,) = call(activate_kernel, [(chunk, wide)], operands=4)(
        rest, rest_in, from_left, from_right
    )

    left, right = shift(own, 1), shift(own, -1)
    far = jnp.concatenate([shift(left[:mid], 1), shift(right[mid:], -1)], axis=0)
    mine = (far, own, right, left)
    other = tuple(core_swap(v) for v in mine)

    out, grads = call(
        back_kernel,
        [(8, chunk, 2 * feat), (8 * chunk, 2 * ff)],
        scratch=[
            pltpu.VMEM((8 * chunk, ff), BF),
            pltpu.VMEM((8 * chunk, feat), BF),
            pltpu.VMEM((8 * chunk, feat), BF),
        ],
        scalars=1,
        operands=12,
        megabytes=14,
    )(who, *mine, *other, w_gate, w_up, w_down, restored)

    out = exchange(out.reshape(nxz, out_rows, 2 * feat), along_xz)
    gate_grad = dot(rows, grads[:, :ff], TN).astype(BF)
    up_grad = dot(rows, grads[:, ff:], TN).astype(BF)
    (part,) = call(
        combine_kernel,
        [(seen, 2 * feat)],
        scratch=[
            pltpu.VMEM((nxz * out_rows, seen), BF),
            pltpu.VMEM((2, nxz * out_rows, seen), BF),
        ],
        operands=3,
    )(out, meta, want)
    part = exchange(part.reshape(ny, tok, 2 * feat), along_y)
    combined, token_grad = call(finish_kernel, [(tok, feat), (tok, feat)], operands=1)(part)
    return (combined, token_grad, gate_grad[None], up_grad[None])


def solution(mesh):
    placed = (
        P("expert", "dp"),
        P("expert", "dp"),
        P("expert", None),
        P("expert", None),
        P(),
        P("expert", "dp", None),
        P("expert", "dp", None),
        P("expert", None, "dp"),
        P(None, "dp", "expert"),
    )
    return jax.shard_map(
        body,
        mesh=mesh,
        in_specs=placed,
        out_specs=(
            P("expert", "dp"),
            P("expert", "dp"),
            P("expert", "dp", None),
            P("expert", "dp", None),
        ),
        check_vma=False,
    )
```

```python
import functools

import jax
import jax.numpy as jnp
import numpy as np
from jax import lax
from jax.experimental import pallas as pl
from jax.experimental.pallas import tpu as pltpu
from jax.sharding import PartitionSpec as P

BF = jnp.bfloat16
F32 = jnp.float32
GRID = {64: (4, 8, 2), 8: (2, 2, 2)}
NN = (((1,), (0,)), ((), ()))
NT = (((1,), (1,)), ((), ()))
TN = (((0,), (0,)), ((), ()))
LANES = 1024
TILE = 256


def dot(a, b, dims=NN):
    return lax.dot_general(a, b, dims, preferred_element_type=F32)


def call(kernel, outs, scratch=(), scalars=0, left=0, operands=0, megabytes=12):
    def of(shape, dtype=BF):
        return jax.ShapeDtypeStruct(shape, dtype)

    specs = [pl.BlockSpec(memory_space=pltpu.SMEM)] * scalars
    specs += [pl.BlockSpec(memory_space=pltpu.HBM)] * left
    specs += [pl.BlockSpec(memory_space=pltpu.VMEM)] * operands
    return pl.pallas_call(
        kernel,
        out_shape=[of(*s) if isinstance(s[0], tuple) else of(s) for s in outs],
        in_specs=specs,
        out_specs=[pl.BlockSpec(memory_space=pltpu.VMEM)] * len(outs),
        scratch_shapes=list(scratch),
        compiler_params=pltpu.CompilerParams(vmem_limit_bytes=megabytes << 20),
    )


def pack_kernel(grid, ids_ref, weight_ref, tok_ref, cot_ref, out_ref):
    nx, ny, nz = grid
    nxz, ranks = nx * nz, nx * ny * nz
    tok, topk = ids_ref.shape
    ids = ids_ref[...]
    x, y, z = lax.div(ids, ny * nz), lax.rem(lax.div(ids, nz), ny), lax.rem(ids, nz)
    column = y * nxz + x * nz + z
    lane = lax.broadcasted_iota(jnp.int32, (tok, ranks), 1)
    member = jnp.zeros((tok, ranks), F32)
    share = jnp.zeros((tok, ranks), F32)
    for k in range(topk):
        same = column[:, k : k + 1] == lane
        member = member + jnp.where(same, 1.0, 0.0)
        share = share + jnp.where(same, weight_ref[:, k : k + 1], 0.0)
    row = lax.broadcasted_iota(jnp.int32, (tok, tok), 0)
    col = lax.broadcasted_iota(jnp.int32, (tok, tok), 1)
    before = dot(jnp.where(col <= row, 1.0, 0.0).astype(BF), member.astype(BF))
    place = jnp.where(member > 0.5, before - 1.0, -1.0).astype(BF)
    hi = share.astype(BF)
    lo = (share - hi.astype(F32)).astype(BF)
    source = lax.broadcasted_iota(jnp.int32, (ranks, ny * 128), 0)
    target = lax.broadcasted_iota(jnp.int32, (ranks, ny * 128), 1)
    base = lax.div(source, nxz) * 128 + lax.rem(source, nxz) + 64
    meta = jnp.zeros((tok, ny * 128), F32)
    for k, part in enumerate((place, hi, lo)):
        meta = meta + dot(part, jnp.where(target == base + k * nxz, 1.0, 0.0).astype(BF))
    feat = tok_ref.shape[1]
    assert feat == 448
    last = jnp.concatenate([tok_ref[:, 384:448].astype(F32), jnp.zeros((tok, 64), F32)], axis=1)
    for i in range(ny):
        out_ref[i, :, 0:384] = tok_ref[:, 0:384]
        out_ref[i, :, 384:512] = (meta[:, i * 128 : (i + 1) * 128] + last).astype(BF)
        out_ref[i, :, 512 : 512 + feat] = cot_ref[...]


def tables(meta_ref, want, q, count):
    hit = meta_ref[q : q + 1, :] == want
    hi = jnp.where(hit, meta_ref[count + q : count + q + 1, :], 0.0).astype(BF)
    lo = jnp.where(hit, meta_ref[2 * count + q : 2 * count + q + 1, :], 0.0).astype(BF)
    return jnp.where(hit, 1.0, 0.0).astype(BF), hi, lo


def select_kernel(first_ref, want_ref, rows_ref, grads_ref, meta_ref):
    nxz, rows, feat = rows_ref.shape
    ny, tok, _ = first_ref.shape
    seen = ny * tok
    tokens = first_ref[:, :, 0:feat].reshape(seen, feat)
    cots = first_ref[:, :, 512 : 512 + feat].reshape(seen, feat)
    meta = jnp.transpose(first_ref[:, :, 384:512].reshape(seen, 128).astype(F32))
    meta_ref[...] = meta[64:128]
    want = want_ref[...]
    both = jnp.concatenate([cots, cots], axis=0)
    for q in range(nxz):
        pick, hi, lo = tables(meta_ref, want, q, nxz)
        rows_ref[q] = dot(pick, tokens).astype(BF)
        grads_ref[q] = dot(jnp.concatenate([hi, lo], axis=1), both).astype(BF)


def chunk_at(h, c, p):
    half = c if p < 4 else 1 - c
    return half * 4 + lax.rem(h + (2, 0, 1, 3)[p % 4], 4)


def products_kernel(grid, count, who_ref, recv_ref, *refs):
    nx, ny, nz = grid
    blocks, weights, outs = refs[:nx], refs[nx : nx + count], refs[nx + count :]
    rows_ref, far_ref, rest_ref, far_out_ref, rest_out_ref, restored_ref = outs
    feat, ff = weights[0].shape
    chunk = far_ref.shape[0]
    target, h, c, my_x, my_z = (who_ref[i] for i in range(5))
    for p in range(8):
        rows_ref[p * chunk : (p + 1) * chunk, :] = recv_ref[chunk_at(h, c, p)]

    def store(k, j, value):
        at = pl.ds(pl.multiple_of(k * ff + j * TILE, TILE), TILE)
        value = value.astype(BF)
        far_ref[:, at] = value[0:chunk]
        rest_ref[:, at] = value[chunk : 4 * chunk]
        far_out_ref[:, at] = value[4 * chunk : 5 * chunk]
        rest_out_ref[:, at] = value[5 * chunk :]

    @pl.when(target == 0)
    def _():
        @pl.loop(0, ff // TILE)
        def _(j):
            at = pl.ds(pl.multiple_of(j * TILE, TILE), TILE)
            for k in range(count):
                store(k, j, dot(rows_ref[...], weights[k][:, at]))

    @pl.when(target == 1)
    def _():
        n = blocks[0].shape[0] // (nz * ny)
        for i, block in enumerate(blocks):
            x = lax.rem(my_x - i + nx, nx)
            for other in range(nz):
                z = 1 - my_z if other else my_z
                for y in range(ny):
                    to = pl.ds(pl.multiple_of(((x * ny + y) * nz + z) * n, n), n)
                    r = (other * ny + y) * n
                    for k in range(count):
                        restored_ref[k, to, :] = block[r : r + n, k * feat : (k + 1) * feat]

        @pl.loop(0, ff // TILE)
        def _(j):
            at = pl.ds(pl.multiple_of(j * TILE, TILE), TILE)
            for k in range(count):
                store(k, j, dot(rows_ref[...], restored_ref[k, at, :], NT))


def activate_kernel(*refs):
    gate_up, grads, out_ref = refs[0:4], refs[4:8], refs[8]
    ff = out_ref.shape[1] // 3
    rows = out_ref.shape[0]

    @pl.loop(0, ff // TILE)
    def _(j):
        def total(parts, k):
            at = pl.ds(pl.multiple_of(k * ff + j * TILE, TILE), TILE)
            near = parts[0][0:rows, at].astype(F32) + parts[1][0:rows, at].astype(F32)
            return near + (parts[2][:, at].astype(F32) + parts[3][:, at].astype(F32))

        gate, up, dh = total(gate_up, 0), total(gate_up, 1), total(grads, 0)
        sig = jax.nn.sigmoid(gate)
        values = (
            gate * sig * up,
            dh * up * sig * (1.0 + gate * (1.0 - sig)),
            dh * gate * sig,
        )
        for k, value in enumerate(values):
            at = pl.ds(pl.multiple_of(k * ff + j * TILE, TILE), TILE)
            out_ref[:, at] = value.astype(BF)


def back_kernel(*refs):
    who_ref, parts = refs[0], refs[1:9]
    gate_ref, up_ref, down_ref, restored_ref, restored_down_ref = refs[9:14]
    out_ref, grads_ref, hidden_ref, y_ref, dx_ref = refs[14:]
    feat, ff = gate_ref.shape
    chunk = out_ref.shape[1]
    target, h, c = who_ref[0], who_ref[1], who_ref[2]
    for p in range(8):
        span = slice(p * chunk, (p + 1) * chunk)
        hidden_ref[span, :] = parts[p][:, 0:ff]
        grads_ref[span, :] = parts[p][:, ff : 3 * ff]

    @pl.when(target == 0)
    def _():
        y_ref[...] = dot(hidden_ref[...], down_ref[...], NT).astype(BF)
        dx_ref[...] = (
            dot(grads_ref[:, 0:ff], gate_ref[...], NT) + dot(grads_ref[:, ff : 2 * ff], up_ref[...], NT)
        ).astype(BF)

    @pl.when(target == 1)
    def _():
        y_ref[...] = dot(hidden_ref[...], restored_down_ref[0]).astype(BF)
        dx_ref[...] = (
            dot(grads_ref[:, 0:ff], restored_ref[0]) + dot(grads_ref[:, ff : 2 * ff], restored_ref[1])
        ).astype(BF)

    for p in range(8):
        g = chunk_at(h, c, p)
        span = slice(p * chunk, (p + 1) * chunk)
        out_ref[g, :, 0:feat] = y_ref[span, :]
        out_ref[g, :, feat : 2 * feat] = dx_ref[span, :]


def combine_kernel(recv_ref, meta_ref, want_ref, out_ref, pick_ref, share_ref):
    nxz, out_rows, width = recv_ref.shape
    feat = width // 2
    total = nxz * out_rows
    for q in range(nxz):
        span = pl.ds(q * out_rows, out_rows)
        pick_ref[span, :], share_ref[0, span, :], share_ref[1, span, :] = tables(
            meta_ref, want_ref[...], q, nxz
        )
    rows = recv_ref[...].reshape(total, width)
    y = dot(share_ref[0], rows[:, 0:feat], TN) + dot(share_ref[1], rows[:, 0:feat], TN)
    out_ref[:, 0:feat] = y.astype(BF)
    out_ref[:, feat:width] = dot(pick_ref[...], rows[:, feat:width], TN).astype(BF)


def finish_kernel(recv_ref, out_ref, grad_ref):
    feat = out_ref.shape[1]
    total = jnp.sum(recv_ref[...].astype(F32), axis=0)
    out_ref[...] = total[:, 0:feat].astype(BF)
    grad_ref[...] = total[:, feat : 2 * feat].astype(BF)


def core_swap(x):
    return lax.ppermute(x, "dp", [(i, i ^ 1) for i in range(8)])


def shift(x, k):
    return lax.ppermute(
        x, "dp", [(2 * h + c, 2 * ((h + k) % 4) + c) for h in range(4) for c in range(2)]
    )


def add(a, b):
    return (a.astype(F32) + b.astype(F32)).astype(BF)


def body(
    tokens,
    cotangent,
    expert_ids,
    route_weight,
    replaced,
    gate_weight,
    up_weight,
    down_weight,
    backup,
):
    ranks = lax.axis_size("expert")
    grid = nx, ny, nz = GRID[ranks]
    nxz = nx * nz
    along_y = [
        [(x * ny + y) * nz + z for y in range(ny)] for x in range(nx) for z in range(nz)
    ]
    along_xz = [
        [(x * ny + y) * nz + z for x in range(nx) for z in range(nz)] for y in range(ny)
    ]

    def exchange(v, groups):
        flat = v.reshape(-1, v.shape[-1])
        flat = lax.all_to_all(flat, "expert", 0, 0, axis_index_groups=groups, tiled=True)
        return flat.reshape(v.shape)

    def rank(x, y, z):
        return ((x % nx) * ny + y) * nz + z % nz

    def step(v, dx, dz):
        pairs = [
            (rank(x, y, z), rank(x + dx, y, z + dz))
            for x in range(nx) for y in range(ny) for z in range(nz)
        ]
        return lax.ppermute(v, "expert", pairs)

    tok, topk = expert_ids.shape
    feat = tokens.shape[1]
    ff = gate_weight.shape[2]
    ffr = ff // ranks
    capacity = min(tok, 5 * tok * topk // (2 * ranks))
    chunk = ranks * capacity // 8
    me, expert = lax.axis_index("dp"), lax.axis_index("expert")
    who = jnp.stack(
        [
            (expert == replaced[0]).astype(jnp.int32),
            me // 2,
            me % 2,
            expert // (ny * nz),
            expert % nz,
        ]
    ).astype(jnp.int32)

    saved = jnp.transpose(backup, (2, 0, 1)).reshape(ffr, 3 * feat)
    saved = jnp.pad(saved, ((0, 0), (0, -3 * feat % 128)))
    saved = exchange(jnp.broadcast_to(saved, (ny, *saved.shape)), along_y)
    saved = saved.reshape(ny * ffr, -1)
    (first,) = call(functools.partial(pack_kernel, grid), [(ny, tok, LANES)], operands=4)(
        expert_ids, route_weight, tokens, cotangent
    )
    first, saved = lax.optimization_barrier((first, saved))
    saved_down, saved_gate_up = saved[:, 2 * feat :], saved[:, : 2 * feat]
    down_z, gate_up_z = (
        jnp.concatenate([v, step(v, 0, 1)], axis=0) for v in (saved_down, saved_gate_up)
    )
    down_blocks = [down_z] + [step(down_z, k, 0) for k in range(1, nx)]
    first = exchange(first, along_y)
    first, gate_up_z, down_blocks = lax.optimization_barrier((first, gate_up_z, down_blocks))
    gate_up_blocks = [gate_up_z] + [step(gate_up_z, k, 0) for k in range(1, nx)]

    out_rows, seen = ny * capacity, ny * tok
    row, col = np.arange(out_rows)[:, None], np.arange(seen)[None, :]
    want = np.where(row // capacity == col // tok, row % capacity, -2).astype(np.float32)
    picked = (nxz, out_rows, feat)
    send_rows, send_grads, meta = call(
        select_kernel, [picked, picked, ((64, seen), F32)], operands=2
    )(first, want)
    recv_grads = exchange(send_grads, along_xz)
    recv_grads, *sides = lax.optimization_barrier((recv_grads, gate_up_blocks[1], gate_up_blocks[3]))
    gate_up_blocks[1], gate_up_blocks[3] = sides
    recv_rows = exchange(send_rows, along_xz)

    mid = chunk // 2

    def products(recv, blocks, *weights):
        count = len(weights)
        parts = [(chunk, count * ff), (3 * chunk, count * ff)]
        return call(
            functools.partial(products_kernel, grid, count),
            [(8 * chunk, feat), *parts, *parts, (count, ff, feat)],
            scalars=1,
            operands=1 + nx + count,
            megabytes=14,
        )(who, recv, *blocks, *weights)

    def sum_parts(far, rest, far_out, rest_out):
        far = add(far, core_swap(far_out))
        rest_in = core_swap(rest_out)
        from_left, from_right = shift(far[:mid], 1), shift(far[mid:], -1)
        sides = add(rest[chunk:], rest_in[chunk:])
        right, left = sides[:chunk], sides[chunk:]
        right = jnp.concatenate([add(right[:mid], from_left), right[mid:]], axis=0)
        left = jnp.concatenate([left[:mid], add(left[mid:], from_right)], axis=0)
        return rest, rest_in, shift(right, 1), shift(left, -1)

    w_gate, w_up, w_down = gate_weight[0], up_weight[0], jnp.transpose(down_weight[0])
    _, *parts, restored_down = products(recv_grads, down_blocks, w_down)
    grad_parts = sum_parts(*parts)
    recv_rows, grad_parts = lax.optimization_barrier((recv_rows, grad_parts))
    rows, *parts, restored = products(recv_rows, gate_up_blocks, w_gate, w_up)
    wide = 3 * ff
    (own,) = call(activate_kernel, [(chunk, wide)], operands=8)(*sum_parts(*parts), *grad_parts)

    left, right = shift(own, 1), shift(own, -1)
    far = jnp.concatenate([shift(left[:mid], 1), shift(right[mid:], -1)], axis=0)
    mine = (far, own, right, left)
    other = tuple(core_swap(v) for v in mine)

    out, grads = call(
        back_kernel,
        [(8, chunk, 2 * feat), (8 * chunk, 2 * ff)],
        scratch=[
            pltpu.VMEM((8 * chunk, ff), BF),
            pltpu.VMEM((8 * chunk, feat), BF),
            pltpu.VMEM((8 * chunk, feat), BF),
        ],
        scalars=1,
        operands=13,
        megabytes=14,
    )(who, *mine, *other, w_gate, w_up, w_down, restored, restored_down)

    out = exchange(out.reshape(nxz, out_rows, 2 * feat), along_xz)
    gate_grad = dot(rows, grads[:, :ff], TN).astype(BF)
    up_grad = dot(rows, grads[:, ff:], TN).astype(BF)
    (part,) = call(
        combine_kernel,
        [(seen, 2 * feat)],
        scratch=[
            pltpu.VMEM((nxz * out_rows, seen), BF),
            pltpu.VMEM((2, nxz * out_rows, seen), BF),
        ],
        operands=3,
    )(out, meta, want)
    part = exchange(part.reshape(ny, tok, 2 * feat), along_y)
    combined, token_grad = call(finish_kernel, [(tok, feat), (tok, feat)], operands=1)(part)
    return (combined, token_grad, gate_grad[None], up_grad[None])


def solution(mesh):
    placed = (
        P("expert", "dp"),
        P("expert", "dp"),
        P("expert", None),
        P("expert", None),
        P(),
        P("expert", "dp", None),
        P("expert", "dp", None),
        P("expert", None, "dp"),
        P(None, "dp", "expert"),
    )
    return jax.shard_map(
        body,
        mesh=mesh,
        in_specs=placed,
        out_specs=(
            P("expert", "dp"),
            P("expert", "dp"),
            P("expert", "dp", None),
            P("expert", "dp", None),
        ),
        check_vma=False,
    )
```

```python
import functools

import jax
import jax.numpy as jnp
import numpy as np
from jax import lax
from jax.experimental import pallas as pl
from jax.experimental.pallas import tpu as pltpu
from jax.sharding import PartitionSpec as P

BF = jnp.bfloat16
F32 = jnp.float32
GRID = {64: (4, 8, 2), 8: (2, 2, 2)}
NN = (((1,), (0,)), ((), ()))
NT = (((1,), (1,)), ((), ()))
TN = (((0,), (0,)), ((), ()))
LANES = 1024
TILE = 256


def dot(a, b, dims=NN):
    return lax.dot_general(a, b, dims, preferred_element_type=F32)


def call(kernel, outs, scratch=(), scalars=0, operands=0, megabytes=32):
    def of(shape, dtype=BF):
        return jax.ShapeDtypeStruct(shape, dtype)

    specs = [pl.BlockSpec(memory_space=pltpu.SMEM)] * scalars
    specs += [pl.BlockSpec(memory_space=pltpu.VMEM)] * operands
    return pl.pallas_call(
        kernel,
        out_shape=[of(*s) if isinstance(s[0], tuple) else of(s) for s in outs],
        in_specs=specs,
        out_specs=[pl.BlockSpec(memory_space=pltpu.VMEM)] * len(outs),
        scratch_shapes=list(scratch),
        compiler_params=pltpu.CompilerParams(vmem_limit_bytes=megabytes << 20),
    )


def pack_kernel(grid, ids_ref, weight_ref, tok_ref, cot_ref, out_ref):
    nx, ny, nz = grid
    nxz, ranks = nx * nz, nx * ny * nz
    tok, topk = ids_ref.shape
    ids = ids_ref[...]
    x, y, z = lax.div(ids, ny * nz), lax.rem(lax.div(ids, nz), ny), lax.rem(ids, nz)
    column = y * nxz + x * nz + z
    lane = lax.broadcasted_iota(jnp.int32, (tok, ranks), 1)
    member = jnp.zeros((tok, ranks), F32)
    share = jnp.zeros((tok, ranks), F32)
    for k in range(topk):
        same = column[:, k : k + 1] == lane
        member = member + jnp.where(same, 1.0, 0.0)
        share = share + jnp.where(same, weight_ref[:, k : k + 1], 0.0)
    row = lax.broadcasted_iota(jnp.int32, (tok, tok), 0)
    col = lax.broadcasted_iota(jnp.int32, (tok, tok), 1)
    before = dot(jnp.where(col <= row, 1.0, 0.0).astype(BF), member.astype(BF))
    place = jnp.where(member > 0.5, before - 1.0, -1.0).astype(BF)
    hi = share.astype(BF)
    lo = (share - hi.astype(F32)).astype(BF)
    source = lax.broadcasted_iota(jnp.int32, (ranks, ny * 128), 0)
    target = lax.broadcasted_iota(jnp.int32, (ranks, ny * 128), 1)
    base = lax.div(source, nxz) * 128 + lax.rem(source, nxz) + 64
    meta = jnp.zeros((tok, ny * 128), F32)
    for k, part in enumerate((place, hi, lo)):
        meta = meta + dot(part, jnp.where(target == base + k * nxz, 1.0, 0.0).astype(BF))
    feat = tok_ref.shape[1]
    assert feat == 448
    last = jnp.concatenate([tok_ref[:, 384:448].astype(F32), jnp.zeros((tok, 64), F32)], axis=1)
    for i in range(ny):
        out_ref[i, :, 0:384] = tok_ref[:, 0:384]
        out_ref[i, :, 384:512] = (meta[:, i * 128 : (i + 1) * 128] + last).astype(BF)
        out_ref[i, :, 512 : 512 + feat] = cot_ref[...]


def tables(meta_ref, want, q, count):
    hit = meta_ref[q : q + 1, :] == want
    hi = jnp.where(hit, meta_ref[count + q : count + q + 1, :], 0.0).astype(BF)
    lo = jnp.where(hit, meta_ref[2 * count + q : 2 * count + q + 1, :], 0.0).astype(BF)
    return jnp.where(hit, 1.0, 0.0).astype(BF), hi, lo


def select_kernel(first_ref, want_ref, out_ref, meta_ref):
    nxz, rows, width = out_ref.shape
    feat = width // 2
    ny, tok, _ = first_ref.shape
    seen = ny * tok
    tokens = first_ref[:, :, 0:feat].reshape(seen, feat)
    cots = first_ref[:, :, 512 : 512 + feat].reshape(seen, feat)
    meta = jnp.transpose(first_ref[:, :, 384:512].reshape(seen, 128).astype(F32))
    meta_ref[...] = meta[64:128]
    want = want_ref[...]
    both = jnp.concatenate([cots, cots], axis=0)
    for q in range(nxz):
        pick, hi, lo = tables(meta_ref, want, q, nxz)
        out_ref[q, :, 0:feat] = dot(pick, tokens).astype(BF)
        out_ref[q, :, feat:width] = dot(jnp.concatenate([hi, lo], axis=1), both).astype(BF)


def chunk_at(h, c, p):
    half = c if p < 4 else 1 - c
    return half * 4 + lax.rem(h + (0, 1, 3, 2)[p % 4], 4)


def products_kernel(
    grid, who_ref, recv_ref, s0, s1, s2a, s2b, s3, gate_ref, up_ref, down_ref,
    rows_ref, far_ref, rest_ref, far_out_ref, rest_out_ref, restored_ref, grads_ref,
):
    nx, ny, nz = grid
    feat, ff = gate_ref.shape
    chunk = far_ref.shape[0]
    target, h, c, my_x, my_z = (who_ref[i] for i in range(5))
    for p in range(8):
        g = chunk_at(h, c, p)
        rows_ref[p * chunk : (p + 1) * chunk, :] = recv_ref[g, :, 0:feat]
        grads_ref[p * chunk : (p + 1) * chunk, :] = recv_ref[g, :, feat : 2 * feat]

    def store(k, j, value):
        at = pl.ds(pl.multiple_of(k * ff + j * TILE, TILE), TILE)
        value = value.astype(BF)
        rest_ref[:, at] = value[0 : 3 * chunk]
        far_ref[:, at] = value[3 * chunk : 4 * chunk]
        rest_out_ref[:, at] = value[4 * chunk : 7 * chunk]
        far_out_ref[:, at] = value[7 * chunk :]

    tiles = ff // TILE

    @pl.when(target == 0)
    def _():
        @pl.loop(0, tiles)
        def _(j):
            at = pl.ds(pl.multiple_of(j * TILE, TILE), TILE)
            store(0, j, dot(rows_ref[...], gate_ref[:, at]))
            store(1, j, dot(rows_ref[...], up_ref[:, at]))
            store(2, j, dot(grads_ref[...], down_ref[:, at]))

    @pl.when(target == 1)
    def _():
        n = s0.shape[0] // (ny * nz)
        half = ny // 2
        for k in range(nx):
            x = lax.rem(my_x - k + nx, nx)
            for y in range(ny):
                source, first = ((s0, 0), (s1, 0), ((s2a, 0), (s2b, half))[y >= half], (s3, 0))[k]
                for other in range(nz):
                    z = 1 - my_z if other else my_z
                    to = pl.ds(pl.multiple_of(((x * ny + y) * nz + z) * n, n), n)
                    r = ((y - first) * nz + other) * n
                    for m in range(3):
                        restored_ref[m, to, :] = source[r : r + n, m * feat : (m + 1) * feat]

        @pl.loop(0, tiles)
        def _(j):
            at = pl.ds(pl.multiple_of(j * TILE, TILE), TILE)
            store(0, j, dot(rows_ref[...], restored_ref[0, at, :], NT))
            store(1, j, dot(rows_ref[...], restored_ref[1, at, :], NT))
            store(2, j, dot(grads_ref[...], restored_ref[2, at, :], NT))


def activate_kernel(own_ref, other_ref, left_ref, right_ref, out_ref):
    ff = out_ref.shape[1] // 3
    rows = out_ref.shape[0]

    @pl.loop(0, ff // TILE)
    def _(j):
        def total(k):
            at = pl.ds(pl.multiple_of(k * ff + j * TILE, TILE), TILE)
            near = own_ref[0:rows, at].astype(F32) + other_ref[0:rows, at].astype(F32)
            return near + (left_ref[:, at].astype(F32) + right_ref[:, at].astype(F32))

        gate, up, dh = total(0), total(1), total(2)
        sig = jax.nn.sigmoid(gate)
        values = (
            gate * sig * up,
            dh * up * sig * (1.0 + gate * (1.0 - sig)),
            dh * gate * sig,
        )
        for k, value in enumerate(values):
            at = pl.ds(pl.multiple_of(k * ff + j * TILE, TILE), TILE)
            out_ref[:, at] = value.astype(BF)


def back_kernel(*refs):
    who_ref, parts = refs[0], refs[1:3]
    gate_ref, up_ref, down_ref, restored_ref, out_ref, grads_ref, hidden_ref, y_ref, dx_ref = refs[3:]
    feat, ff = gate_ref.shape
    chunk = out_ref.shape[1]
    target, h, c = who_ref[0], who_ref[1], who_ref[2]
    for k, part in enumerate(parts):
        span = slice(4 * chunk * k, 4 * chunk * (k + 1))
        hidden_ref[span, :] = part[:, 0:ff]
        grads_ref[span, :] = part[:, ff : 3 * ff]

    @pl.when(target == 0)
    def _():
        y_ref[...] = dot(hidden_ref[...], down_ref[...], NT).astype(BF)
        dx_ref[...] = (
            dot(grads_ref[:, 0:ff], gate_ref[...], NT) + dot(grads_ref[:, ff : 2 * ff], up_ref[...], NT)
        ).astype(BF)

    @pl.when(target == 1)
    def _():
        y_ref[...] = dot(hidden_ref[...], restored_ref[2]).astype(BF)
        dx_ref[...] = (
            dot(grads_ref[:, 0:ff], restored_ref[0]) + dot(grads_ref[:, ff : 2 * ff], restored_ref[1])
        ).astype(BF)

    for p in range(8):
        g = chunk_at(h, c, p)
        span = slice(p * chunk, (p + 1) * chunk)
        out_ref[g, :, 0:feat] = y_ref[span, :]
        out_ref[g, :, feat : 2 * feat] = dx_ref[span, :]


def combine_kernel(recv_ref, meta_ref, want_ref, out_ref, pick_ref, share_ref):
    nxz, out_rows, width = recv_ref.shape
    feat = width // 2
    total = nxz * out_rows
    for q in range(nxz):
        span = pl.ds(q * out_rows, out_rows)
        pick_ref[span, :], share_ref[0, span, :], share_ref[1, span, :] = tables(
            meta_ref, want_ref[...], q, nxz
        )
    rows = recv_ref[...].reshape(total, width)
    y = dot(share_ref[0], rows[:, 0:feat], TN) + dot(share_ref[1], rows[:, 0:feat], TN)
    out_ref[:, 0:feat] = y.astype(BF)
    out_ref[:, feat:width] = dot(pick_ref[...], rows[:, feat:width], TN).astype(BF)


def finish_kernel(recv_ref, out_ref, grad_ref):
    feat = out_ref.shape[1]
    total = jnp.sum(recv_ref[...].astype(F32), axis=0)
    out_ref[...] = total[:, 0:feat].astype(BF)
    grad_ref[...] = total[:, feat : 2 * feat].astype(BF)


def core_swap(x):
    return lax.ppermute(x, "dp", [(i, i ^ 1) for i in range(8)])


def shift(x, k):
    return lax.ppermute(
        x, "dp", [(2 * h + c, 2 * ((h + k) % 4) + c) for h in range(4) for c in range(2)]
    )


def add(a, b):
    return (a.astype(F32) + b.astype(F32)).astype(BF)


def body(
    tokens,
    cotangent,
    expert_ids,
    route_weight,
    replaced,
    gate_weight,
    up_weight,
    down_weight,
    backup,
):
    ranks = lax.axis_size("expert")
    grid = nx, ny, nz = GRID[ranks]
    nxz = nx * nz
    along_y = [
        [(x * ny + y) * nz + z for y in range(ny)] for x in range(nx) for z in range(nz)
    ]
    along_xz = [
        [(x * ny + y) * nz + z for x in range(nx) for z in range(nz)] for y in range(ny)
    ]

    def exchange(v, groups):
        flat = v.reshape(-1, v.shape[-1])
        flat = lax.all_to_all(flat, "expert", 0, 0, axis_index_groups=groups, tiled=True)
        return flat.reshape(v.shape)

    def rank(x, y, z):
        return ((x % nx) * ny + y) * nz + z % nz

    def step(v, dx, dz):
        pairs = [
            (rank(x, y, z), rank(x + dx, y, z + dz))
            for x in range(nx) for y in range(ny) for z in range(nz)
        ]
        return lax.ppermute(v, "expert", pairs)

    tok, topk = expert_ids.shape
    feat = tokens.shape[1]
    ff = gate_weight.shape[2]
    ffr = ff // ranks
    capacity = min(tok, 5 * tok * topk // (2 * ranks))
    chunk = ranks * capacity // 8
    me, expert = lax.axis_index("dp"), lax.axis_index("expert")
    who = jnp.stack(
        [
            (expert == replaced[0]).astype(jnp.int32),
            me // 2,
            me % 2,
            expert // (ny * nz),
            expert % nz,
        ]
    ).astype(jnp.int32)

    saved = jnp.transpose(backup, (2, 0, 1)).reshape(ffr, 3 * feat)
    saved = jnp.pad(saved, ((0, 0), (0, -3 * feat % 128)))
    saved = jnp.concatenate([saved, step(saved, 0, 1)], axis=0)
    saved = exchange(jnp.broadcast_to(saved, (ny, *saved.shape)), along_y)
    saved = saved.reshape(ny * nz * ffr, -1)

    (first,) = call(functools.partial(pack_kernel, grid), [(ny, tok, LANES)], operands=4)(
        expert_ids, route_weight, tokens, cotangent
    )
    first, saved = lax.optimization_barrier((first, saved))
    before, after = step(saved, 1, 0), step(saved, -1, 0)
    first = exchange(first, along_y)
    first, before, after = lax.optimization_barrier((first, before, after))
    half = saved.shape[0] // 2
    blocks = saved, before, step(before[:half], 1, 0), step(after[half:], -1, 0), after

    out_rows, seen = ny * capacity, ny * tok
    row, col = np.arange(out_rows)[:, None], np.arange(seen)[None, :]
    want = np.where(row // capacity == col // tok, row % capacity, -2).astype(np.float32)
    send, meta = call(
        select_kernel, [(nxz, out_rows, 2 * feat), ((64, seen), F32)], operands=2
    )(first, want)
    recv = exchange(send, along_xz)

    w_gate, w_up, w_down = gate_weight[0], up_weight[0], jnp.transpose(down_weight[0])
    wide = 3 * ff
    rows, far, rest, far_out, rest_out, restored = call(
        functools.partial(products_kernel, grid),
        [
            (8 * chunk, feat), (chunk, wide), (3 * chunk, wide),
            (chunk, wide), (3 * chunk, wide), (3, ff, feat),
        ],
        scratch=[pltpu.VMEM((8 * chunk, feat), BF)],
        scalars=1,
        operands=9,
        megabytes=18,
    )(who, recv, *blocks, w_gate, w_up, w_down)

    mid = chunk // 2
    far = add(far, core_swap(far_out))
    rest_in = core_swap(rest_out)
    from_left, from_right = shift(far[:mid], 1), shift(far[mid:], -1)
    sides = add(rest[chunk:], rest_in[chunk:])
    right, left = sides[:chunk], sides[chunk:]
    right = jnp.concatenate([add(right[:mid], from_left), right[mid:]], axis=0)
    left = jnp.concatenate([left[:mid], add(left[mid:], from_right)], axis=0)
    from_left, from_right = shift(right, 1), shift(left, -1)
    (own,) = call(activate_kernel, [(chunk, wide)], operands=4)(
        rest, rest_in, from_left, from_right
    )

    left, right = shift(own, 1), shift(own, -1)
    far = shift(left[:mid], 1), shift(right[mid:], -1)
    mine = jnp.concatenate([own, right, left, *far], axis=0)
    other = core_swap(mine)

    out, grads = call(
        back_kernel,
        [(8, chunk, 2 * feat), (8 * chunk, 2 * ff)],
        scratch=[
            pltpu.VMEM((8 * chunk, ff), BF),
            pltpu.VMEM((8 * chunk, feat), BF),
            pltpu.VMEM((8 * chunk, feat), BF),
        ],
        scalars=1,
        operands=6,
        megabytes=18,
    )(who, mine, other, w_gate, w_up, w_down, restored)

    out = exchange(out.reshape(nxz, out_rows, 2 * feat), along_xz)
    gate_grad = dot(rows, grads[:, :ff], TN).astype(BF)
    up_grad = dot(rows, grads[:, ff:], TN).astype(BF)
    (part,) = call(
        combine_kernel,
        [(seen, 2 * feat)],
        scratch=[
            pltpu.VMEM((nxz * out_rows, seen), BF),
            pltpu.VMEM((2, nxz * out_rows, seen), BF),
        ],
        operands=3,
    )(out, meta, want)
    part = exchange(part.reshape(ny, tok, 2 * feat), along_y)
    combined, token_grad = call(finish_kernel, [(tok, feat), (tok, feat)], operands=1)(part)
    return (combined, token_grad, gate_grad[None], up_grad[None])


def solution(mesh):
    placed = (
        P("expert", "dp"),
        P("expert", "dp"),
        P("expert", None),
        P("expert", None),
        P(),
        P("expert", "dp", None),
        P("expert", "dp", None),
        P("expert", None, "dp"),
        P(None, "dp", "expert"),
    )
    return jax.shard_map(
        body,
        mesh=mesh,
        in_specs=placed,
        out_specs=(
            P("expert", "dp"),
            P("expert", "dp"),
            P("expert", "dp", None),
            P("expert", "dp", None),
        ),
        check_vma=False,
    )
```

```python
import functools

import jax
import jax.numpy as jnp
import numpy as np
from jax import lax
from jax.experimental import pallas as pl
from jax.experimental.pallas import tpu as pltpu
from jax.sharding import PartitionSpec as P

BF = jnp.bfloat16
F32 = jnp.float32
GRID = {64: (4, 8, 2), 8: (2, 2, 2)}
NN = (((1,), (0,)), ((), ()))
NT = (((1,), (1,)), ((), ()))
TN = (((0,), (0,)), ((), ()))
LANES = 1024
TILE = 256


def dot(a, b, dims=NN):
    return lax.dot_general(a, b, dims, preferred_element_type=F32)


def call(kernel, outs, scratch=(), scalars=0, operands=0, megabytes=32):
    def of(shape, dtype=BF):
        return jax.ShapeDtypeStruct(shape, dtype)

    specs = [pl.BlockSpec(memory_space=pltpu.SMEM)] * scalars
    specs += [pl.BlockSpec(memory_space=pltpu.VMEM)] * operands
    return pl.pallas_call(
        kernel,
        out_shape=[of(*s) if isinstance(s[0], tuple) else of(s) for s in outs],
        in_specs=specs,
        out_specs=[pl.BlockSpec(memory_space=pltpu.VMEM)] * len(outs),
        scratch_shapes=list(scratch),
        compiler_params=pltpu.CompilerParams(vmem_limit_bytes=megabytes << 20),
    )


def pack_kernel(grid, ids_ref, weight_ref, tok_ref, cot_ref, out_ref):
    nx, ny, nz = grid
    nxz, ranks = nx * nz, nx * ny * nz
    tok, topk = ids_ref.shape
    ids = ids_ref[...]
    x, y, z = lax.div(ids, ny * nz), lax.rem(lax.div(ids, nz), ny), lax.rem(ids, nz)
    column = y * nxz + x * nz + z
    lane = lax.broadcasted_iota(jnp.int32, (tok, ranks), 1)
    member = jnp.zeros((tok, ranks), F32)
    share = jnp.zeros((tok, ranks), F32)
    for k in range(topk):
        same = column[:, k : k + 1] == lane
        member = member + jnp.where(same, 1.0, 0.0)
        share = share + jnp.where(same, weight_ref[:, k : k + 1], 0.0)
    row = lax.broadcasted_iota(jnp.int32, (tok, tok), 0)
    col = lax.broadcasted_iota(jnp.int32, (tok, tok), 1)
    before = dot(jnp.where(col <= row, 1.0, 0.0).astype(BF), member.astype(BF))
    place = jnp.where(member > 0.5, before - 1.0, -1.0).astype(BF)
    hi = share.astype(BF)
    lo = (share - hi.astype(F32)).astype(BF)
    source = lax.broadcasted_iota(jnp.int32, (ranks, ny * 128), 0)
    target = lax.broadcasted_iota(jnp.int32, (ranks, ny * 128), 1)
    base = lax.div(source, nxz) * 128 + lax.rem(source, nxz) + 64
    meta = jnp.zeros((tok, ny * 128), F32)
    for k, part in enumerate((place, hi, lo)):
        meta = meta + dot(part, jnp.where(target == base + k * nxz, 1.0, 0.0).astype(BF))
    feat = tok_ref.shape[1]
    assert feat == 448
    last = jnp.concatenate([tok_ref[:, 384:448].astype(F32), jnp.zeros((tok, 64), F32)], axis=1)
    for i in range(ny):
        out_ref[i, :, 0:384] = tok_ref[:, 0:384]
        out_ref[i, :, 384:512] = (meta[:, i * 128 : (i + 1) * 128] + last).astype(BF)
        out_ref[i, :, 512 : 512 + feat] = cot_ref[...]


def tables(meta_ref, want, q, count):
    hit = meta_ref[q : q + 1, :] == want
    hi = jnp.where(hit, meta_ref[count + q : count + q + 1, :], 0.0).astype(BF)
    lo = jnp.where(hit, meta_ref[2 * count + q : 2 * count + q + 1, :], 0.0).astype(BF)
    return jnp.where(hit, 1.0, 0.0).astype(BF), hi, lo


def select_kernel(first_ref, want_ref, out_ref, meta_ref):
    nxz, rows, width = out_ref.shape
    feat = width // 2
    ny, tok, _ = first_ref.shape
    seen = ny * tok
    tokens = first_ref[:, :, 0:feat].reshape(seen, feat)
    cots = first_ref[:, :, 512 : 512 + feat].reshape(seen, feat)
    meta = jnp.transpose(first_ref[:, :, 384:512].reshape(seen, 128).astype(F32))
    meta_ref[...] = meta[64:128]
    want = want_ref[...]
    both = jnp.concatenate([cots, cots], axis=0)
    for q in range(nxz):
        pick, hi, lo = tables(meta_ref, want, q, nxz)
        out_ref[q, :, 0:feat] = dot(pick, tokens).astype(BF)
        out_ref[q, :, feat:width] = dot(jnp.concatenate([hi, lo], axis=1), both).astype(BF)


def chunk_at(h, c, p):
    half = c if p < 4 else 1 - c
    return half * 4 + lax.rem(h + (0, 1, 3, 2)[p % 4], 4)


def products_kernel(
    grid, who_ref, recv_ref, s0, t0, s1, t1, s2, t2, s3, t3, gate_ref, up_ref, down_ref,
    rows_ref, far_ref, rest_ref, far_out_ref, rest_out_ref, restored_ref, grads_ref,
):
    nx, ny, nz = grid
    feat, ff = gate_ref.shape
    chunk = far_ref.shape[0]
    target, h, c, my_x, my_z = (who_ref[i] for i in range(5))
    for p in range(8):
        g = chunk_at(h, c, p)
        rows_ref[p * chunk : (p + 1) * chunk, :] = recv_ref[g, :, 0:feat]
        grads_ref[p * chunk : (p + 1) * chunk, :] = recv_ref[g, :, feat : 2 * feat]

    def store(k, j, value):
        at = pl.ds(pl.multiple_of(k * ff + j * TILE, TILE), TILE)
        value = value.astype(BF)
        rest_ref[:, at] = value[0 : 3 * chunk]
        far_ref[:, at] = value[3 * chunk : 4 * chunk]
        rest_out_ref[:, at] = value[4 * chunk : 7 * chunk]
        far_out_ref[:, at] = value[7 * chunk :]

    tiles = ff // TILE

    @pl.when(target == 0)
    def _():
        @pl.loop(0, tiles)
        def _(j):
            at = pl.ds(pl.multiple_of(j * TILE, TILE), TILE)
            store(0, j, dot(rows_ref[...], gate_ref[:, at]))
            store(1, j, dot(rows_ref[...], up_ref[:, at]))
            store(2, j, dot(grads_ref[...], down_ref[:, at]))

    @pl.when(target == 1)
    def _():
        n = s0.shape[0] // ny
        for k, sources in enumerate(((s0, t0), (s1, t1), (s2, t2), (s3, t3))):
            for other in range(nz):
                x = lax.rem(my_x - k + nx, nx)
                z = 1 - my_z if other else my_z
                for y in range(ny):
                    to = pl.ds(pl.multiple_of(((x * ny + y) * nz + z) * n, n), n)
                    for m in range(3):
                        restored_ref[m, to, :] = sources[other][y * n : (y + 1) * n, m * feat : (m + 1) * feat]

        @pl.loop(0, tiles)
        def _(j):
            at = pl.ds(pl.multiple_of(j * TILE, TILE), TILE)
            store(0, j, dot(rows_ref[...], restored_ref[0, at, :], NT))
            store(1, j, dot(rows_ref[...], restored_ref[1, at, :], NT))
            store(2, j, dot(grads_ref[...], restored_ref[2, at, :], NT))


def activate_kernel(own_ref, other_ref, left_ref, right_ref, out_ref):
    ff = out_ref.shape[1] // 3
    rows = out_ref.shape[0]

    @pl.loop(0, ff // TILE)
    def _(j):
        def total(k):
            at = pl.ds(pl.multiple_of(k * ff + j * TILE, TILE), TILE)
            near = own_ref[0:rows, at].astype(F32) + other_ref[0:rows, at].astype(F32)
            return near + (left_ref[:, at].astype(F32) + right_ref[:, at].astype(F32))

        gate, up, dh = total(0), total(1), total(2)
        sig = jax.nn.sigmoid(gate)
        values = (
            gate * sig * up,
            dh * up * sig * (1.0 + gate * (1.0 - sig)),
            dh * gate * sig,
        )
        for k, value in enumerate(values):
            at = pl.ds(pl.multiple_of(k * ff + j * TILE, TILE), TILE)
            out_ref[:, at] = value.astype(BF)


def back_kernel(*refs):
    who_ref, parts = refs[0], refs[1:3]
    gate_ref, up_ref, down_ref, restored_ref, out_ref, grads_ref, hidden_ref, y_ref, dx_ref = refs[3:]
    feat, ff = gate_ref.shape
    chunk = out_ref.shape[1]
    target, h, c = who_ref[0], who_ref[1], who_ref[2]
    for k, part in enumerate(parts):
        span = slice(4 * chunk * k, 4 * chunk * (k + 1))
        hidden_ref[span, :] = part[:, 0:ff]
        grads_ref[span, :] = part[:, ff : 3 * ff]

    @pl.when(target == 0)
    def _():
        y_ref[...] = dot(hidden_ref[...], down_ref[...], NT).astype(BF)
        dx_ref[...] = (
            dot(grads_ref[:, 0:ff], gate_ref[...], NT) + dot(grads_ref[:, ff : 2 * ff], up_ref[...], NT)
        ).astype(BF)

    @pl.when(target == 1)
    def _():
        y_ref[...] = dot(hidden_ref[...], restored_ref[2]).astype(BF)
        dx_ref[...] = (
            dot(grads_ref[:, 0:ff], restored_ref[0]) + dot(grads_ref[:, ff : 2 * ff], restored_ref[1])
        ).astype(BF)

    for p in range(8):
        g = chunk_at(h, c, p)
        span = slice(p * chunk, (p + 1) * chunk)
        out_ref[g, :, 0:feat] = y_ref[span, :]
        out_ref[g, :, feat : 2 * feat] = dx_ref[span, :]


def combine_kernel(recv_ref, meta_ref, want_ref, out_ref, pick_ref, share_ref):
    nxz, out_rows, width = recv_ref.shape
    feat = width // 2
    total = nxz * out_rows
    for q in range(nxz):
        span = pl.ds(q * out_rows, out_rows)
        pick_ref[span, :], share_ref[0, span, :], share_ref[1, span, :] = tables(
            meta_ref, want_ref[...], q, nxz
        )
    rows = recv_ref[...].reshape(total, width)
    y = dot(share_ref[0], rows[:, 0:feat], TN) + dot(share_ref[1], rows[:, 0:feat], TN)
    out_ref[:, 0:feat] = y.astype(BF)
    out_ref[:, feat:width] = dot(pick_ref[...], rows[:, feat:width], TN).astype(BF)


def finish_kernel(recv_ref, out_ref, grad_ref):
    feat = out_ref.shape[1]
    total = jnp.sum(recv_ref[...].astype(F32), axis=0)
    out_ref[...] = total[:, 0:feat].astype(BF)
    grad_ref[...] = total[:, feat : 2 * feat].astype(BF)


def core_swap(x):
    return lax.ppermute(x, "dp", [(i, i ^ 1) for i in range(8)])


def shift(x, k):
    return lax.ppermute(
        x, "dp", [(2 * h + c, 2 * ((h + k) % 4) + c) for h in range(4) for c in range(2)]
    )


def add(a, b):
    return (a.astype(F32) + b.astype(F32)).astype(BF)


def body(
    tokens,
    cotangent,
    expert_ids,
    route_weight,
    replaced,
    gate_weight,
    up_weight,
    down_weight,
    backup,
):
    ranks = lax.axis_size("expert")
    grid = nx, ny, nz = GRID[ranks]
    nxz = nx * nz
    along_y = [
        [(x * ny + y) * nz + z for y in range(ny)] for x in range(nx) for z in range(nz)
    ]
    along_xz = [
        [(x * ny + y) * nz + z for x in range(nx) for z in range(nz)] for y in range(ny)
    ]

    def exchange(v, groups):
        flat = v.reshape(-1, v.shape[-1])
        flat = lax.all_to_all(flat, "expert", 0, 0, axis_index_groups=groups, tiled=True)
        return flat.reshape(v.shape)

    def rank(x, y, z):
        return ((x % nx) * ny + y) * nz + z % nz

    def step(v, dx, dz):
        pairs = [
            (rank(x, y, z), rank(x + dx, y, z + dz))
            for x in range(nx) for y in range(ny) for z in range(nz)
        ]
        return lax.ppermute(v, "expert", pairs)

    tok, topk = expert_ids.shape
    feat = tokens.shape[1]
    ff = gate_weight.shape[2]
    ffr = ff // ranks
    capacity = min(tok, 5 * tok * topk // (2 * ranks))
    chunk = ranks * capacity // 8
    me, expert = lax.axis_index("dp"), lax.axis_index("expert")
    who = jnp.stack(
        [
            (expert == replaced[0]).astype(jnp.int32),
            me // 2,
            me % 2,
            expert // (ny * nz),
            expert % nz,
        ]
    ).astype(jnp.int32)

    saved = jnp.transpose(backup, (2, 0, 1)).reshape(ffr, 3 * feat)
    saved = jnp.pad(saved, ((0, 0), (0, -3 * feat % 128)))
    saved = exchange(jnp.broadcast_to(saved, (ny, *saved.shape)), along_y)
    saved = saved.reshape(ny * ffr, -1)
    (first,) = call(functools.partial(pack_kernel, grid), [(ny, tok, LANES)], operands=4)(
        expert_ids, route_weight, tokens, cotangent
    )
    first, saved = lax.optimization_barrier((first, saved))
    other_z = step(saved, 0, 1)
    before, after = step(saved, 1, 0), step(saved, -1, 0)
    first = exchange(first, along_y)
    first, other_z, before, after = lax.optimization_barrier((first, other_z, before, after))
    before_z, after_z = step(other_z, 1, 0), step(other_z, -1, 0)
    blocks = (
        saved, other_z, before, before_z, step(before, 1, 0), step(after_z, -1, 0), after, after_z,
    )

    out_rows, seen = ny * capacity, ny * tok
    row, col = np.arange(out_rows)[:, None], np.arange(seen)[None, :]
    want = np.where(row // capacity == col // tok, row % capacity, -2).astype(np.float32)
    send, meta = call(
        select_kernel, [(nxz, out_rows, 2 * feat), ((64, seen), F32)], operands=2
    )(first, want)
    recv = exchange(send, along_xz)

    w_gate, w_up, w_down = gate_weight[0], up_weight[0], jnp.transpose(down_weight[0])
    wide = 3 * ff
    rows, far, rest, far_out, rest_out, restored = call(
        functools.partial(products_kernel, grid),
        [
            (8 * chunk, feat), (chunk, wide), (3 * chunk, wide),
            (chunk, wide), (3 * chunk, wide), (3, ff, feat),
        ],
        scratch=[pltpu.VMEM((8 * chunk, feat), BF)],
        scalars=1,
        operands=12,
        megabytes=18,
    )(who, recv, *blocks, w_gate, w_up, w_down)

    mid = chunk // 2
    far = add(far, core_swap(far_out))
    rest_in = core_swap(rest_out)
    from_left, from_right = shift(far[:mid], 1), shift(far[mid:], -1)
    sides = add(rest[chunk:], rest_in[chunk:])
    right, left = sides[:chunk], sides[chunk:]
    right = jnp.concatenate([add(right[:mid], from_left), right[mid:]], axis=0)
    left = jnp.concatenate([left[:mid], add(left[mid:], from_right)], axis=0)
    from_left, from_right = shift(right, 1), shift(left, -1)
    (own,) = call(activate_kernel, [(chunk, wide)], operands=4)(
        rest, rest_in, from_left, from_right
    )

    left, right = shift(own, 1), shift(own, -1)
    far = shift(left[:mid], 1), shift(right[mid:], -1)
    mine = jnp.concatenate([own, right, left, *far], axis=0)
    other = core_swap(mine)

    out, grads = call(
        back_kernel,
        [(8, chunk, 2 * feat), (8 * chunk, 2 * ff)],
        scratch=[
            pltpu.VMEM((8 * chunk, ff), BF),
            pltpu.VMEM((8 * chunk, feat), BF),
            pltpu.VMEM((8 * chunk, feat), BF),
        ],
        scalars=1,
        operands=6,
        megabytes=18,
    )(who, mine, other, w_gate, w_up, w_down, restored)

    out = exchange(out.reshape(nxz, out_rows, 2 * feat), along_xz)
    gate_grad = dot(rows, grads[:, :ff], TN).astype(BF)
    up_grad = dot(rows, grads[:, ff:], TN).astype(BF)
    (part,) = call(
        combine_kernel,
        [(seen, 2 * feat)],
        scratch=[
            pltpu.VMEM((nxz * out_rows, seen), BF),
            pltpu.VMEM((2, nxz * out_rows, seen), BF),
        ],
        operands=3,
    )(out, meta, want)
    part = exchange(part.reshape(ny, tok, 2 * feat), along_y)
    combined, token_grad = call(finish_kernel, [(tok, feat), (tok, feat)], operands=1)(part)
    return (combined, token_grad, gate_grad[None], up_grad[None])


def solution(mesh):
    placed = (
        P("expert", "dp"),
        P("expert", "dp"),
        P("expert", None),
        P("expert", None),
        P(),
        P("expert", "dp", None),
        P("expert", "dp", None),
        P("expert", None, "dp"),
        P(None, "dp", "expert"),
    )
    return jax.shard_map(
        body,
        mesh=mesh,
        in_specs=placed,
        out_specs=(
            P("expert", "dp"),
            P("expert", "dp"),
            P("expert", "dp", None),
            P("expert", "dp", None),
        ),
        check_vma=False,
    )
```

```python
import functools

import jax
import jax.numpy as jnp
import numpy as np
from jax import lax
from jax.experimental import pallas as pl
from jax.experimental.pallas import tpu as pltpu
from jax.sharding import PartitionSpec as P

BF = jnp.bfloat16
F32 = jnp.float32
GRID = {64: (4, 8, 2), 8: (2, 2, 2)}
NN = (((1,), (0,)), ((), ()))
NT = (((1,), (1,)), ((), ()))
TN = (((0,), (0,)), ((), ()))
LANES = 1024
TILE = 256


def dot(a, b, dims=NN):
    return lax.dot_general(a, b, dims, preferred_element_type=F32)


def call(kernel, outs, scratch=(), scalars=0, operands=0, megabytes=32):
    def of(shape, dtype=BF):
        return jax.ShapeDtypeStruct(shape, dtype)

    specs = [pl.BlockSpec(memory_space=pltpu.SMEM)] * scalars
    specs += [pl.BlockSpec(memory_space=pltpu.VMEM)] * operands
    return pl.pallas_call(
        kernel,
        out_shape=[of(*s) if isinstance(s[0], tuple) else of(s) for s in outs],
        in_specs=specs,
        out_specs=[pl.BlockSpec(memory_space=pltpu.VMEM)] * len(outs),
        scratch_shapes=list(scratch),
        compiler_params=pltpu.CompilerParams(vmem_limit_bytes=megabytes << 20),
    )


def pack_kernel(grid, ids_ref, weight_ref, tok_ref, cot_ref, out_ref):
    nx, ny, nz = grid
    nxz, ranks = nx * nz, nx * ny * nz
    tok, topk = ids_ref.shape
    ids = ids_ref[...]
    x, y, z = lax.div(ids, ny * nz), lax.rem(lax.div(ids, nz), ny), lax.rem(ids, nz)
    column = y * nxz + x * nz + z
    lane = lax.broadcasted_iota(jnp.int32, (tok, ranks), 1)
    member = jnp.zeros((tok, ranks), F32)
    share = jnp.zeros((tok, ranks), F32)
    for k in range(topk):
        same = column[:, k : k + 1] == lane
        member = member + jnp.where(same, 1.0, 0.0)
        share = share + jnp.where(same, weight_ref[:, k : k + 1], 0.0)
    row = lax.broadcasted_iota(jnp.int32, (tok, tok), 0)
    col = lax.broadcasted_iota(jnp.int32, (tok, tok), 1)
    before = dot(jnp.where(col <= row, 1.0, 0.0).astype(BF), member.astype(BF))
    place = jnp.where(member > 0.5, before - 1.0, -1.0).astype(BF)
    hi = share.astype(BF)
    lo = (share - hi.astype(F32)).astype(BF)
    source = lax.broadcasted_iota(jnp.int32, (ranks, ny * 128), 0)
    target = lax.broadcasted_iota(jnp.int32, (ranks, ny * 128), 1)
    base = lax.div(source, nxz) * 128 + lax.rem(source, nxz) + 64
    meta = jnp.zeros((tok, ny * 128), F32)
    for k, part in enumerate((place, hi, lo)):
        meta = meta + dot(part, jnp.where(target == base + k * nxz, 1.0, 0.0).astype(BF))
    feat = tok_ref.shape[1]
    assert feat == 448
    last = jnp.concatenate([tok_ref[:, 384:448].astype(F32), jnp.zeros((tok, 64), F32)], axis=1)
    for i in range(ny):
        out_ref[i, :, 0:384] = tok_ref[:, 0:384]
        out_ref[i, :, 384:512] = (meta[:, i * 128 : (i + 1) * 128] + last).astype(BF)
        out_ref[i, :, 512 : 512 + feat] = cot_ref[...]


def tables(meta_ref, want, q, count):
    hit = meta_ref[q : q + 1, :] == want
    hi = jnp.where(hit, meta_ref[count + q : count + q + 1, :], 0.0).astype(BF)
    lo = jnp.where(hit, meta_ref[2 * count + q : 2 * count + q + 1, :], 0.0).astype(BF)
    return jnp.where(hit, 1.0, 0.0).astype(BF), hi, lo


def select_kernel(first_ref, want_ref, out_ref, meta_ref):
    nxz, rows, width = out_ref.shape
    feat = width // 2
    ny, tok, _ = first_ref.shape
    seen = ny * tok
    tokens = first_ref[:, :, 0:feat].reshape(seen, feat)
    cots = first_ref[:, :, 512 : 512 + feat].reshape(seen, feat)
    meta = jnp.transpose(first_ref[:, :, 384:512].reshape(seen, 128).astype(F32))
    meta_ref[...] = meta[64:128]
    want = want_ref[...]
    both = jnp.concatenate([cots, cots], axis=0)
    for q in range(nxz):
        pick, hi, lo = tables(meta_ref, want, q, nxz)
        out_ref[q, :, 0:feat] = dot(pick, tokens).astype(BF)
        out_ref[q, :, feat:width] = dot(jnp.concatenate([hi, lo], axis=1), both).astype(BF)


def chunk_at(h, c, p):
    half = c if p < 4 else 1 - c
    return half * 4 + lax.rem(h + (0, 1, 3, 2)[p % 4], 4)


def products_kernel(
    grid, who_ref, recv_ref, s0, t0, s1, t1, s2, t2, s3, t3, gate_ref, up_ref, down_ref,
    rows_ref, far_ref, rest_ref, far_out_ref, rest_out_ref, restored_ref, grads_ref,
):
    nx, ny, nz = grid
    feat, ff = gate_ref.shape
    chunk = far_ref.shape[0]
    target, h, c, my_x, my_z = (who_ref[i] for i in range(5))
    for p in range(8):
        g = chunk_at(h, c, p)
        rows_ref[p * chunk : (p + 1) * chunk, :] = recv_ref[g, :, 0:feat]
        grads_ref[p * chunk : (p + 1) * chunk, :] = recv_ref[g, :, feat : 2 * feat]

    def store(k, j, value):
        at = pl.ds(pl.multiple_of(k * ff + j * TILE, TILE), TILE)
        value = value.astype(BF)
        rest_ref[:, at] = value[0 : 3 * chunk]
        far_ref[:, at] = value[3 * chunk : 4 * chunk]
        rest_out_ref[:, at] = value[4 * chunk : 7 * chunk]
        far_out_ref[:, at] = value[7 * chunk :]

    tiles = ff // TILE

    @pl.when(target == 0)
    def _():
        @pl.loop(0, tiles)
        def _(j):
            at = pl.ds(pl.multiple_of(j * TILE, TILE), TILE)
            store(0, j, dot(rows_ref[...], gate_ref[:, at]))
            store(1, j, dot(rows_ref[...], up_ref[:, at]))
            store(2, j, dot(grads_ref[...], down_ref[:, at]))

    @pl.when(target == 1)
    def _():
        n = s0.shape[0] // ny
        for k, sources in enumerate(((s0, t0), (s1, t1), (s2, t2), (s3, t3))):
            for other in range(nz):
                x = lax.rem(my_x - k + nx, nx)
                z = 1 - my_z if other else my_z
                for y in range(ny):
                    to = pl.ds(pl.multiple_of(((x * ny + y) * nz + z) * n, n), n)
                    for m in range(3):
                        restored_ref[m, to, :] = sources[other][y * n : (y + 1) * n, m * feat : (m + 1) * feat]

        @pl.loop(0, tiles)
        def _(j):
            at = pl.ds(pl.multiple_of(j * TILE, TILE), TILE)
            store(0, j, dot(rows_ref[...], restored_ref[0, at, :], NT))
            store(1, j, dot(rows_ref[...], restored_ref[1, at, :], NT))
            store(2, j, dot(grads_ref[...], restored_ref[2, at, :], NT))


def activate_kernel(own_ref, other_ref, left_ref, right_ref, out_ref):
    ff = out_ref.shape[1] // 3
    rows = out_ref.shape[0]

    @pl.loop(0, ff // TILE)
    def _(j):
        def total(k):
            at = pl.ds(pl.multiple_of(k * ff + j * TILE, TILE), TILE)
            near = own_ref[0:rows, at].astype(F32) + other_ref[0:rows, at].astype(F32)
            return near + (left_ref[:, at].astype(F32) + right_ref[:, at].astype(F32))

        gate, up, dh = total(0), total(1), total(2)
        sig = jax.nn.sigmoid(gate)
        values = (
            gate * sig * up,
            dh * up * sig * (1.0 + gate * (1.0 - sig)),
            dh * gate * sig,
        )
        for k, value in enumerate(values):
            at = pl.ds(pl.multiple_of(k * ff + j * TILE, TILE), TILE)
            out_ref[:, at] = value.astype(BF)


def back_kernel(*refs):
    who_ref, parts = refs[0], refs[1:3]
    gate_ref, up_ref, down_ref, restored_ref, out_ref, grads_ref, hidden_ref, y_ref, dx_ref = refs[3:]
    feat, ff = gate_ref.shape
    chunk = out_ref.shape[1]
    target, h, c = who_ref[0], who_ref[1], who_ref[2]
    for k, part in enumerate(parts):
        span = slice(4 * chunk * k, 4 * chunk * (k + 1))
        hidden_ref[span, :] = part[:, 0:ff]
        grads_ref[span, :] = part[:, ff : 3 * ff]

    @pl.when(target == 0)
    def _():
        y_ref[...] = dot(hidden_ref[...], down_ref[...], NT).astype(BF)
        dx_ref[...] = (
            dot(grads_ref[:, 0:ff], gate_ref[...], NT) + dot(grads_ref[:, ff : 2 * ff], up_ref[...], NT)
        ).astype(BF)

    @pl.when(target == 1)
    def _():
        y_ref[...] = dot(hidden_ref[...], restored_ref[2]).astype(BF)
        dx_ref[...] = (
            dot(grads_ref[:, 0:ff], restored_ref[0]) + dot(grads_ref[:, ff : 2 * ff], restored_ref[1])
        ).astype(BF)

    for p in range(8):
        g = chunk_at(h, c, p)
        span = slice(p * chunk, (p + 1) * chunk)
        out_ref[g, :, 0:feat] = y_ref[span, :]
        out_ref[g, :, feat : 2 * feat] = dx_ref[span, :]


def combine_kernel(recv_ref, meta_ref, want_ref, out_ref, pick_ref, share_ref):
    nxz, out_rows, width = recv_ref.shape
    feat = width // 2
    total = nxz * out_rows
    for q in range(nxz):
        span = pl.ds(q * out_rows, out_rows)
        pick_ref[span, :], share_ref[0, span, :], share_ref[1, span, :] = tables(
            meta_ref, want_ref[...], q, nxz
        )
    rows = recv_ref[...].reshape(total, width)
    y = dot(share_ref[0], rows[:, 0:feat], TN) + dot(share_ref[1], rows[:, 0:feat], TN)
    out_ref[:, 0:feat] = y.astype(BF)
    out_ref[:, feat:width] = dot(pick_ref[...], rows[:, feat:width], TN).astype(BF)


def finish_kernel(recv_ref, out_ref, grad_ref):
    feat = out_ref.shape[1]
    total = jnp.sum(recv_ref[...].astype(F32), axis=0)
    out_ref[...] = total[:, 0:feat].astype(BF)
    grad_ref[...] = total[:, feat : 2 * feat].astype(BF)


def core_swap(x):
    return lax.ppermute(x, "dp", [(i, i ^ 1) for i in range(8)])


def shift(x, k):
    return lax.ppermute(
        x, "dp", [(2 * h + c, 2 * ((h + k) % 4) + c) for h in range(4) for c in range(2)]
    )


def add(a, b):
    return (a.astype(F32) + b.astype(F32)).astype(BF)


def body(
    tokens,
    cotangent,
    expert_ids,
    route_weight,
    replaced,
    gate_weight,
    up_weight,
    down_weight,
    backup,
):
    ranks = lax.axis_size("expert")
    grid = nx, ny, nz = GRID[ranks]
    nxz = nx * nz
    along_y = [
        [(x * ny + y) * nz + z for y in range(ny)] for x in range(nx) for z in range(nz)
    ]
    along_xz = [
        [(x * ny + y) * nz + z for x in range(nx) for z in range(nz)] for y in range(ny)
    ]

    def exchange(v, groups):
        flat = v.reshape(-1, v.shape[-1])
        flat = lax.all_to_all(flat, "expert", 0, 0, axis_index_groups=groups, tiled=True)
        return flat.reshape(v.shape)

    def rank(x, y, z):
        return ((x % nx) * ny + y) * nz + z % nz

    def step(v, dx, dz):
        pairs = [
            (rank(x, y, z), rank(x + dx, y, z + dz))
            for x in range(nx) for y in range(ny) for z in range(nz)
        ]
        return lax.ppermute(v, "expert", pairs)

    tok, topk = expert_ids.shape
    feat = tokens.shape[1]
    ff = gate_weight.shape[2]
    ffr = ff // ranks
    capacity = min(tok, 5 * tok * topk // (2 * ranks))
    chunk = ranks * capacity // 8
    me, expert = lax.axis_index("dp"), lax.axis_index("expert")
    who = jnp.stack(
        [
            (expert == replaced[0]).astype(jnp.int32),
            me // 2,
            me % 2,
            expert // (ny * nz),
            expert % nz,
        ]
    ).astype(jnp.int32)

    saved = jnp.transpose(backup, (2, 0, 1)).reshape(ffr, 3 * feat)
    saved = jnp.pad(saved, ((0, 0), (0, -3 * feat % 128)))
    saved = exchange(jnp.broadcast_to(saved, (ny, *saved.shape)), along_y)
    saved = saved.reshape(ny * ffr, -1)
    (first,) = call(functools.partial(pack_kernel, grid), [(ny, tok, LANES)], operands=4)(
        expert_ids, route_weight, tokens, cotangent
    )
    first, saved = lax.optimization_barrier((first, saved))
    other_z = step(saved, 0, 1)
    before, after = step(saved, 1, 0), step(saved, -1, 0)
    first = exchange(first, along_y)
    first, other_z, before, after = lax.optimization_barrier((first, other_z, before, after))
    half = saved.shape[0] // 2
    two_before = jnp.concatenate([step(before[:half], 1, 0), step(after[half:], -1, 0)], axis=0)
    before_z, after_z = step(other_z, 1, 0), step(other_z, -1, 0)
    blocks = saved, other_z, before, before_z, two_before, step(two_before, 0, 1), after, after_z

    out_rows, seen = ny * capacity, ny * tok
    row, col = np.arange(out_rows)[:, None], np.arange(seen)[None, :]
    want = np.where(row // capacity == col // tok, row % capacity, -2).astype(np.float32)
    send, meta = call(
        select_kernel, [(nxz, out_rows, 2 * feat), ((64, seen), F32)], operands=2
    )(first, want)
    recv = exchange(send, along_xz)

    w_gate, w_up, w_down = gate_weight[0], up_weight[0], jnp.transpose(down_weight[0])
    wide = 3 * ff
    rows, far, rest, far_out, rest_out, restored = call(
        functools.partial(products_kernel, grid),
        [
            (8 * chunk, feat), (chunk, wide), (3 * chunk, wide),
            (chunk, wide), (3 * chunk, wide), (3, ff, feat),
        ],
        scratch=[pltpu.VMEM((8 * chunk, feat), BF)],
        scalars=1,
        operands=12,
        megabytes=18,
    )(who, recv, *blocks, w_gate, w_up, w_down)

    mid = chunk // 2
    far = add(far, core_swap(far_out))
    rest_in = core_swap(rest_out)
    from_left, from_right = shift(far[:mid], 1), shift(far[mid:], -1)
    sides = add(rest[chunk:], rest_in[chunk:])
    right, left = sides[:chunk], sides[chunk:]
    right = jnp.concatenate([add(right[:mid], from_left), right[mid:]], axis=0)
    left = jnp.concatenate([left[:mid], add(left[mid:], from_right)], axis=0)
    from_left, from_right = shift(right, 1), shift(left, -1)
    (own,) = call(activate_kernel, [(chunk, wide)], operands=4)(
        rest, rest_in, from_left, from_right
    )

    left, right = shift(own, 1), shift(own, -1)
    far = shift(left[:mid], 1), shift(right[mid:], -1)
    mine = jnp.concatenate([own, right, left, *far], axis=0)
    other = core_swap(mine)

    out, grads = call(
        back_kernel,
        [(8, chunk, 2 * feat), (8 * chunk, 2 * ff)],
        scratch=[
            pltpu.VMEM((8 * chunk, ff), BF),
            pltpu.VMEM((8 * chunk, feat), BF),
            pltpu.VMEM((8 * chunk, feat), BF),
        ],
        scalars=1,
        operands=6,
        megabytes=18,
    )(who, mine, other, w_gate, w_up, w_down, restored)

    out = exchange(out.reshape(nxz, out_rows, 2 * feat), along_xz)
    gate_grad = dot(rows, grads[:, :ff], TN).astype(BF)
    up_grad = dot(rows, grads[:, ff:], TN).astype(BF)
    (part,) = call(
        combine_kernel,
        [(seen, 2 * feat)],
        scratch=[
            pltpu.VMEM((nxz * out_rows, seen), BF),
            pltpu.VMEM((2, nxz * out_rows, seen), BF),
        ],
        operands=3,
    )(out, meta, want)
    part = exchange(part.reshape(ny, tok, 2 * feat), along_y)
    combined, token_grad = call(finish_kernel, [(tok, feat), (tok, feat)], operands=1)(part)
    return (combined, token_grad, gate_grad[None], up_grad[None])


def solution(mesh):
    placed = (
        P("expert", "dp"),
        P("expert", "dp"),
        P("expert", None),
        P("expert", None),
        P(),
        P("expert", "dp", None),
        P("expert", "dp", None),
        P("expert", None, "dp"),
        P(None, "dp", "expert"),
    )
    return jax.shard_map(
        body,
        mesh=mesh,
        in_specs=placed,
        out_specs=(
            P("expert", "dp"),
            P("expert", "dp"),
            P("expert", "dp", None),
            P("expert", "dp", None),
        ),
        check_vma=False,
    )
```

```python
import functools

import jax
import jax.numpy as jnp
import numpy as np
from jax import lax
from jax.experimental import pallas as pl
from jax.experimental.pallas import tpu as pltpu
from jax.sharding import PartitionSpec as P

BF = jnp.bfloat16
F32 = jnp.float32
GRID = {64: (4, 8, 2), 8: (2, 2, 2)}
NN = (((1,), (0,)), ((), ()))
NT = (((1,), (1,)), ((), ()))
TN = (((0,), (0,)), ((), ()))
LANES = 1024
TILE = 256


def dot(a, b, dims=NN):
    return lax.dot_general(a, b, dims, preferred_element_type=F32)


def call(kernel, outs, scratch=(), scalars=0, operands=0, megabytes=18, left_out=0):
    def of(shape, dtype=BF):
        return jax.ShapeDtypeStruct(shape, dtype)

    specs = [pl.BlockSpec(memory_space=pltpu.SMEM)] * scalars
    specs += [pl.BlockSpec(memory_space=pltpu.VMEM)] * operands
    return pl.pallas_call(
        kernel,
        out_shape=[of(*s) if isinstance(s[0], tuple) else of(s) for s in outs],
        in_specs=specs,
        out_specs=[pl.BlockSpec(memory_space=pltpu.VMEM)] * (len(outs) - left_out)
        + [pl.BlockSpec(memory_space=pltpu.HBM)] * left_out,
        scratch_shapes=list(scratch),
        compiler_params=pltpu.CompilerParams(vmem_limit_bytes=megabytes << 20),
    )


def pack_kernel(grid, ids_ref, weight_ref, tok_ref, cot_ref, out_ref):
    nx, ny, nz = grid
    nxz, ranks = nx * nz, nx * ny * nz
    tok, topk = ids_ref.shape
    ids = ids_ref[...]
    x, y, z = lax.div(ids, ny * nz), lax.rem(lax.div(ids, nz), ny), lax.rem(ids, nz)
    column = y * nxz + x * nz + z
    lane = lax.broadcasted_iota(jnp.int32, (tok, ranks), 1)
    member = jnp.zeros((tok, ranks), F32)
    share = jnp.zeros((tok, ranks), F32)
    for k in range(topk):
        same = column[:, k : k + 1] == lane
        member = member + jnp.where(same, 1.0, 0.0)
        share = share + jnp.where(same, weight_ref[:, k : k + 1], 0.0)
    row = lax.broadcasted_iota(jnp.int32, (tok, tok), 0)
    col = lax.broadcasted_iota(jnp.int32, (tok, tok), 1)
    before = dot(jnp.where(col <= row, 1.0, 0.0).astype(BF), member.astype(BF))
    place = jnp.where(member > 0.5, before - 1.0, -1.0).astype(BF)
    hi = share.astype(BF)
    lo = (share - hi.astype(F32)).astype(BF)
    source = lax.broadcasted_iota(jnp.int32, (ranks, ny * 128), 0)
    target = lax.broadcasted_iota(jnp.int32, (ranks, ny * 128), 1)
    base = lax.div(source, nxz) * 128 + lax.rem(source, nxz) + 64
    meta = jnp.zeros((tok, ny * 128), F32)
    for k, part in enumerate((place, hi, lo)):
        meta = meta + dot(part, jnp.where(target == base + k * nxz, 1.0, 0.0).astype(BF))
    feat = tok_ref.shape[1]
    assert feat == 448
    last = jnp.concatenate([tok_ref[:, 384:448].astype(F32), jnp.zeros((tok, 64), F32)], axis=1)
    for i in range(ny):
        out_ref[i, :, 0:384] = tok_ref[:, 0:384]
        out_ref[i, :, 384:512] = (meta[:, i * 128 : (i + 1) * 128] + last).astype(BF)
        out_ref[i, :, 512 : 512 + feat] = cot_ref[...]


def tables(meta_ref, want, q, count):
    hit = meta_ref[q : q + 1, :] == want
    hi = jnp.where(hit, meta_ref[count + q : count + q + 1, :], 0.0).astype(BF)
    lo = jnp.where(hit, meta_ref[2 * count + q : 2 * count + q + 1, :], 0.0).astype(BF)
    return jnp.where(hit, 1.0, 0.0).astype(BF), hi, lo


def select_kernel(first_ref, want_ref, out_ref, meta_ref):
    nxz, rows, width = out_ref.shape
    feat = width // 2
    ny, tok, _ = first_ref.shape
    seen = ny * tok
    tokens = first_ref[:, :, 0:feat].reshape(seen, feat)
    cots = first_ref[:, :, 512 : 512 + feat].reshape(seen, feat)
    meta = jnp.transpose(first_ref[:, :, 384:512].reshape(seen, 128).astype(F32))
    meta_ref[...] = meta[64:128]
    want = want_ref[...]
    both = jnp.concatenate([cots, cots], axis=0)
    for q in range(nxz):
        pick, hi, lo = tables(meta_ref, want, q, nxz)
        out_ref[q, :, 0:feat] = dot(pick, tokens).astype(BF)
        out_ref[q, :, feat:width] = dot(jnp.concatenate([hi, lo], axis=1), both).astype(BF)


def chunk_at(h, c, p):
    half = c if p < 4 else 1 - c
    return half * 4 + lax.rem(h + (0, 1, 3, 2)[p % 4], 4)


def products_kernel(
    grid, who_ref, recv_ref, s0, t0, s1, t1, s2, t2, s3, t3, gate_ref, up_ref, down_ref,
    rows_ref, far_ref, rest_ref, far_out_ref, rest_out_ref, restored_ref, grads_ref,
):
    nx, ny, nz = grid
    feat, ff = gate_ref.shape
    chunk = far_ref.shape[0]
    target, h, c, my_x, my_z = (who_ref[i] for i in range(5))
    for p in range(8):
        g = chunk_at(h, c, p)
        rows_ref[p * chunk : (p + 1) * chunk, :] = recv_ref[g, :, 0:feat]
        grads_ref[p * chunk : (p + 1) * chunk, :] = recv_ref[g, :, feat : 2 * feat]

    def store(k, j, value):
        at = pl.ds(pl.multiple_of(k * ff + j * TILE, TILE), TILE)
        value = value.astype(BF)
        rest_ref[:, at] = value[0 : 3 * chunk]
        far_ref[:, at] = value[3 * chunk : 4 * chunk]
        rest_out_ref[:, at] = value[4 * chunk : 7 * chunk]
        far_out_ref[:, at] = value[7 * chunk :]

    tiles = ff // TILE

    @pl.when(target == 0)
    def _():
        @pl.loop(0, tiles)
        def _(j):
            at = pl.ds(pl.multiple_of(j * TILE, TILE), TILE)
            store(0, j, dot(rows_ref[...], gate_ref[:, at]))
            store(1, j, dot(rows_ref[...], up_ref[:, at]))
            store(2, j, dot(grads_ref[...], down_ref[:, at]))

    @pl.when(target == 1)
    def _():
        n = s0.shape[0] // ny
        for k, sources in enumerate(((s0, t0), (s1, t1), (s2, t2), (s3, t3))):
            for other in range(nz):
                x = lax.rem(my_x - k + nx, nx)
                z = 1 - my_z if other else my_z
                for y in range(ny):
                    to = pl.ds(pl.multiple_of(((x * ny + y) * nz + z) * n, n), n)
                    for m in range(3):
                        restored_ref[m, to, :] = sources[other][y * n : (y + 1) * n, m * feat : (m + 1) * feat]

        @pl.loop(0, tiles)
        def _(j):
            at = pl.ds(pl.multiple_of(j * TILE, TILE), TILE)
            store(0, j, dot(rows_ref[...], restored_ref[0, at, :], NT))
            store(1, j, dot(rows_ref[...], restored_ref[1, at, :], NT))
            store(2, j, dot(grads_ref[...], restored_ref[2, at, :], NT))


def merge_kernel(at, low, own_ref, other_ref, arrived_ref, out_ref):
    rows, width = out_ref.shape
    mid = arrived_ref.shape[0]

    @pl.loop(0, width // TILE)
    def _(j):
        lanes = pl.ds(pl.multiple_of(j * TILE, TILE), TILE)
        value = own_ref[at : at + rows, lanes].astype(F32) + other_ref[at : at + rows, lanes].astype(F32)
        more = arrived_ref[:, lanes].astype(F32)
        none = jnp.zeros((rows - mid, TILE), F32)
        value = value + jnp.concatenate([more, none] if low else [none, more], axis=0)
        out_ref[:, lanes] = value.astype(BF)


def activate_kernel(own_ref, other_ref, left_ref, right_ref, out_ref):
    ff = out_ref.shape[1] // 3
    rows = out_ref.shape[0]

    @pl.loop(0, ff // TILE)
    def _(j):
        def total(k):
            at = pl.ds(pl.multiple_of(k * ff + j * TILE, TILE), TILE)
            near = own_ref[0:rows, at].astype(F32) + other_ref[0:rows, at].astype(F32)
            return near + (left_ref[:, at].astype(F32) + right_ref[:, at].astype(F32))

        gate, up, dh = total(0), total(1), total(2)
        sig = jax.nn.sigmoid(gate)
        values = (
            gate * sig * up,
            dh * up * sig * (1.0 + gate * (1.0 - sig)),
            dh * gate * sig,
        )
        for k, value in enumerate(values):
            at = pl.ds(pl.multiple_of(k * ff + j * TILE, TILE), TILE)
            out_ref[:, at] = value.astype(BF)


def back_kernel(
    who_ref, mine_ref, other_ref, gate_ref, up_ref, down_ref, restored_ref,
    out_ref, grads_ref, y_ref, dx_ref, sems,
):
    feat, ff = gate_ref.shape
    chunk = out_ref.shape[1]
    target, h, c = who_ref[0], who_ref[1], who_ref[2]
    copies = [
        pltpu.make_async_copy(ref.at[:, ff : 3 * ff], grads_ref.at[k], sems.at[k])
        for k, ref in enumerate((mine_ref, other_ref))
    ]
    for copy in copies:
        copy.start()
    for k, ref in enumerate((mine_ref, other_ref)):
        span = slice(4 * chunk * k, 4 * chunk * (k + 1))

        @pl.when(target == 0)
        def _():
            y_ref[span, :] = dot(ref[:, 0:ff], down_ref[...], NT).astype(BF)
            dx = dot(ref[:, ff : 2 * ff], gate_ref[...], NT)
            dx_ref[span, :] = (dx + dot(ref[:, 2 * ff : 3 * ff], up_ref[...], NT)).astype(BF)

        @pl.when(target == 1)
        def _():
            y_ref[span, :] = dot(ref[:, 0:ff], restored_ref[2]).astype(BF)
            dx = dot(ref[:, ff : 2 * ff], restored_ref[0])
            dx_ref[span, :] = (dx + dot(ref[:, 2 * ff : 3 * ff], restored_ref[1])).astype(BF)

    for p in range(8):
        g = chunk_at(h, c, p)
        span = slice(p * chunk, (p + 1) * chunk)
        out_ref[g, :, 0:feat] = y_ref[span, :]
        out_ref[g, :, feat : 2 * feat] = dx_ref[span, :]
    for copy in copies:
        copy.wait()


def combine_kernel(recv_ref, meta_ref, want_ref, out_ref, pick_ref, share_ref):
    nxz, out_rows, width = recv_ref.shape
    feat = width // 2
    total = nxz * out_rows
    for q in range(nxz):
        span = pl.ds(q * out_rows, out_rows)
        pick_ref[span, :], share_ref[0, span, :], share_ref[1, span, :] = tables(
            meta_ref, want_ref[...], q, nxz
        )
    rows = recv_ref[...].reshape(total, width)
    y = dot(share_ref[0], rows[:, 0:feat], TN) + dot(share_ref[1], rows[:, 0:feat], TN)
    out_ref[:, 0:feat] = y.astype(BF)
    out_ref[:, feat:width] = dot(pick_ref[...], rows[:, feat:width], TN).astype(BF)


def finish_kernel(recv_ref, out_ref, grad_ref):
    feat = out_ref.shape[1]
    total = jnp.sum(recv_ref[...].astype(F32), axis=0)
    out_ref[...] = total[:, 0:feat].astype(BF)
    grad_ref[...] = total[:, feat : 2 * feat].astype(BF)


def core_swap(x):
    return lax.ppermute(x, "dp", [(i, i ^ 1) for i in range(8)])


def shift(x, k):
    return lax.ppermute(
        x, "dp", [(2 * h + c, 2 * ((h + k) % 4) + c) for h in range(4) for c in range(2)]
    )


def add(a, b):
    return (a.astype(F32) + b.astype(F32)).astype(BF)


def body(
    tokens,
    cotangent,
    expert_ids,
    route_weight,
    replaced,
    gate_weight,
    up_weight,
    down_weight,
    backup,
):
    ranks = lax.axis_size("expert")
    grid = nx, ny, nz = GRID[ranks]
    nxz = nx * nz
    along_y = [
        [(x * ny + y) * nz + z for y in range(ny)] for x in range(nx) for z in range(nz)
    ]
    along_xz = [
        [(x * ny + y) * nz + z for x in range(nx) for z in range(nz)] for y in range(ny)
    ]

    def exchange(v, groups):
        flat = v.reshape(-1, v.shape[-1])
        flat = lax.all_to_all(flat, "expert", 0, 0, axis_index_groups=groups, tiled=True)
        return flat.reshape(v.shape)

    def rank(x, y, z):
        return ((x % nx) * ny + y) * nz + z % nz

    def step(v, dx, dz):
        pairs = [
            (rank(x, y, z), rank(x + dx, y, z + dz))
            for x in range(nx) for y in range(ny) for z in range(nz)
        ]
        return lax.ppermute(v, "expert", pairs)

    tok, topk = expert_ids.shape
    feat = tokens.shape[1]
    ff = gate_weight.shape[2]
    ffr = ff // ranks
    capacity = min(tok, 5 * tok * topk // (2 * ranks))
    chunk = ranks * capacity // 8
    me, expert = lax.axis_index("dp"), lax.axis_index("expert")
    who = jnp.stack(
        [
            (expert == replaced[0]).astype(jnp.int32),
            me // 2,
            me % 2,
            expert // (ny * nz),
            expert % nz,
        ]
    ).astype(jnp.int32)

    saved = jnp.transpose(backup, (2, 0, 1)).reshape(ffr, 3 * feat)
    saved = jnp.pad(saved, ((0, 0), (0, -3 * feat % 128)))
    saved = exchange(jnp.broadcast_to(saved, (ny, *saved.shape)), along_y)
    saved = saved.reshape(ny * ffr, -1)
    (first,) = call(functools.partial(pack_kernel, grid), [(ny, tok, LANES)], operands=4)(
        expert_ids, route_weight, tokens, cotangent
    )
    first, saved = lax.optimization_barrier((first, saved))
    other_z = step(saved, 0, 1)
    before, after = step(saved, 1, 0), step(saved, -1, 0)
    first = exchange(first, along_y)
    first, other_z, before, after = lax.optimization_barrier((first, other_z, before, after))
    before_z, after_z = step(other_z, 1, 0), step(other_z, -1, 0)
    blocks = (
        saved, other_z, before, before_z, step(before, 1, 0), step(after_z, -1, 0), after, after_z,
    )

    out_rows, seen = ny * capacity, ny * tok
    row, col = np.arange(out_rows)[:, None], np.arange(seen)[None, :]
    want = np.where(row // capacity == col // tok, row % capacity, -2).astype(np.float32)
    send, meta = call(
        select_kernel, [(nxz, out_rows, 2 * feat), ((64, seen), F32)], operands=2
    )(first, want)
    recv = exchange(send, along_xz)

    w_gate, w_up, w_down = gate_weight[0], up_weight[0], jnp.transpose(down_weight[0])
    wide = 3 * ff
    rows, far, rest, far_out, rest_out, restored = call(
        functools.partial(products_kernel, grid),
        [
            (8 * chunk, feat), (chunk, wide), (3 * chunk, wide),
            (chunk, wide), (3 * chunk, wide), (3, ff, feat),
        ],
        scratch=[pltpu.VMEM((8 * chunk, feat), BF)],
        scalars=1,
        operands=12,
        megabytes=18,
    )(who, recv, *blocks, w_gate, w_up, w_down)

    mid = chunk // 2
    far = add(far, core_swap(far_out))
    rest_in = core_swap(rest_out)
    from_left, from_right = shift(far[:mid], 1), shift(far[mid:], -1)
    def merged(at, low, arrived):
        kernel = functools.partial(merge_kernel, at, low)
        return call(kernel, [(chunk, wide)], operands=3)(rest, rest_in, arrived)[0]

    from_left = shift(merged(chunk, True, from_left), 1)
    from_right = shift(merged(2 * chunk, False, from_right), -1)
    (own,) = call(activate_kernel, [(chunk, wide)], operands=4)(
        rest, rest_in, from_left, from_right
    )

    left, right = shift(own, 1), shift(own, -1)
    far = shift(left[:mid], 1), shift(right[mid:], -1)
    mine = jnp.concatenate([own, right, left, *far], axis=0)
    other = core_swap(mine)

    out, grads = call(
        back_kernel,
        [(8, chunk, 2 * feat), (2, 4 * chunk, 2 * ff)],
        scratch=[
            pltpu.VMEM((8 * chunk, feat), BF),
            pltpu.VMEM((8 * chunk, feat), BF),
            pltpu.SemaphoreType.DMA((2,)),
        ],
        scalars=1,
        operands=6,
        megabytes=18,
        left_out=1,
    )(who, mine, other, w_gate, w_up, w_down, restored)
    grads = grads.reshape(8 * chunk, 2 * ff)

    out = exchange(out.reshape(nxz, out_rows, 2 * feat), along_xz)
    gate_grad = dot(rows, grads[:, :ff], TN).astype(BF)
    up_grad = dot(rows, grads[:, ff:], TN).astype(BF)
    out, gate_grad = lax.optimization_barrier((out, gate_grad))
    (part,) = call(
        combine_kernel,
        [(seen, 2 * feat)],
        scratch=[
            pltpu.VMEM((nxz * out_rows, seen), BF),
            pltpu.VMEM((2, nxz * out_rows, seen), BF),
        ],
        operands=3,
    )(out, meta, want)
    part = exchange(part.reshape(ny, tok, 2 * feat), along_y)
    combined, token_grad = call(finish_kernel, [(tok, feat), (tok, feat)], operands=1)(part)
    return (combined, token_grad, gate_grad[None], up_grad[None])


def solution(mesh):
    placed = (
        P("expert", "dp"),
        P("expert", "dp"),
        P("expert", None),
        P("expert", None),
        P(),
        P("expert", "dp", None),
        P("expert", "dp", None),
        P("expert", None, "dp"),
        P(None, "dp", "expert"),
    )
    return jax.shard_map(
        body,
        mesh=mesh,
        in_specs=placed,
        out_specs=(
            P("expert", "dp"),
            P("expert", "dp"),
            P("expert", "dp", None),
            P("expert", "dp", None),
        ),
        check_vma=False,
    )
```

```python
import functools

import jax
import jax.numpy as jnp
import numpy as np
from jax import lax
from jax.experimental import pallas as pl
from jax.experimental.pallas import tpu as pltpu
from jax.sharding import PartitionSpec as P

BF = jnp.bfloat16
F32 = jnp.float32
GRID = {64: (4, 8, 2), 8: (2, 2, 2)}
NN = (((1,), (0,)), ((), ()))
NT = (((1,), (1,)), ((), ()))
TN = (((0,), (0,)), ((), ()))
LANES = 1024
TILE = 256


def dot(a, b, dims=NN):
    return lax.dot_general(a, b, dims, preferred_element_type=F32)


def call(kernel, outs, scratch=(), scalars=0, operands=0, megabytes=32):
    def of(shape, dtype=BF):
        return jax.ShapeDtypeStruct(shape, dtype)

    specs = [pl.BlockSpec(memory_space=pltpu.SMEM)] * scalars
    specs += [pl.BlockSpec(memory_space=pltpu.VMEM)] * operands
    return pl.pallas_call(
        kernel,
        out_shape=[of(*s) if isinstance(s[0], tuple) else of(s) for s in outs],
        in_specs=specs,
        out_specs=[pl.BlockSpec(memory_space=pltpu.VMEM)] * len(outs),
        scratch_shapes=list(scratch),
        compiler_params=pltpu.CompilerParams(vmem_limit_bytes=megabytes << 20),
    )


def pack_kernel(grid, ids_ref, weight_ref, tok_ref, cot_ref, out_ref):
    nx, ny, nz = grid
    nxz, ranks = nx * nz, nx * ny * nz
    tok, topk = ids_ref.shape
    ids = ids_ref[...]
    x, y, z = lax.div(ids, ny * nz), lax.rem(lax.div(ids, nz), ny), lax.rem(ids, nz)
    column = y * nxz + x * nz + z
    lane = lax.broadcasted_iota(jnp.int32, (tok, ranks), 1)
    member = jnp.zeros((tok, ranks), F32)
    share = jnp.zeros((tok, ranks), F32)
    for k in range(topk):
        same = column[:, k : k + 1] == lane
        member = member + jnp.where(same, 1.0, 0.0)
        share = share + jnp.where(same, weight_ref[:, k : k + 1], 0.0)
    row = lax.broadcasted_iota(jnp.int32, (tok, tok), 0)
    col = lax.broadcasted_iota(jnp.int32, (tok, tok), 1)
    before = dot(jnp.where(col <= row, 1.0, 0.0).astype(BF), member.astype(BF))
    place = jnp.where(member > 0.5, before - 1.0, -1.0).astype(BF)
    hi = share.astype(BF)
    lo = (share - hi.astype(F32)).astype(BF)
    source = lax.broadcasted_iota(jnp.int32, (ranks, ny * 128), 0)
    target = lax.broadcasted_iota(jnp.int32, (ranks, ny * 128), 1)
    base = lax.div(source, nxz) * 128 + lax.rem(source, nxz) + 64
    meta = jnp.zeros((tok, ny * 128), F32)
    for k, part in enumerate((place, hi, lo)):
        meta = meta + dot(part, jnp.where(target == base + k * nxz, 1.0, 0.0).astype(BF))
    feat = tok_ref.shape[1]
    assert feat == 448
    last = jnp.concatenate([tok_ref[:, 384:448].astype(F32), jnp.zeros((tok, 64), F32)], axis=1)
    for i in range(ny):
        out_ref[i, :, 0:384] = tok_ref[:, 0:384]
        out_ref[i, :, 384:512] = (meta[:, i * 128 : (i + 1) * 128] + last).astype(BF)
        out_ref[i, :, 512 : 512 + feat] = cot_ref[...]


def tables(meta_ref, want, q, count):
    hit = meta_ref[q : q + 1, :] == want
    hi = jnp.where(hit, meta_ref[count + q : count + q + 1, :], 0.0).astype(BF)
    lo = jnp.where(hit, meta_ref[2 * count + q : 2 * count + q + 1, :], 0.0).astype(BF)
    return jnp.where(hit, 1.0, 0.0).astype(BF), hi, lo


def select_kernel(first_ref, want_ref, out_ref, meta_ref):
    nxz, rows, width = out_ref.shape
    feat = width // 2
    ny, tok, _ = first_ref.shape
    seen = ny * tok
    tokens = first_ref[:, :, 0:feat].reshape(seen, feat)
    cots = first_ref[:, :, 512 : 512 + feat].reshape(seen, feat)
    meta = jnp.transpose(first_ref[:, :, 384:512].reshape(seen, 128).astype(F32))
    meta_ref[...] = meta[64:128]
    want = want_ref[...]
    both = jnp.concatenate([cots, cots], axis=0)
    for q in range(nxz):
        pick, hi, lo = tables(meta_ref, want, q, nxz)
        out_ref[q, :, 0:feat] = dot(pick, tokens).astype(BF)
        out_ref[q, :, feat:width] = dot(jnp.concatenate([hi, lo], axis=1), both).astype(BF)


def chunk_at(h, c, p):
    half = c if p < 4 else 1 - c
    return half * 4 + lax.rem(h + (0, 1, 3, 2)[p % 4], 4)


def products_kernel(
    grid, who_ref, recv_ref, s0, t0, s1, t1, s2, t2, s3, t3, gate_ref, up_ref, down_ref,
    rows_ref, far_ref, rest_ref, far_out_ref, rest_out_ref, restored_ref, grads_ref,
):
    nx, ny, nz = grid
    feat, ff = gate_ref.shape
    chunk = far_ref.shape[0]
    target, h, c, my_x, my_z = (who_ref[i] for i in range(5))
    for p in range(8):
        g = chunk_at(h, c, p)
        rows_ref[p * chunk : (p + 1) * chunk, :] = recv_ref[g, :, 0:feat]
        grads_ref[p * chunk : (p + 1) * chunk, :] = recv_ref[g, :, feat : 2 * feat]

    def store(k, j, value):
        at = pl.ds(pl.multiple_of(k * ff + j * TILE, TILE), TILE)
        value = value.astype(BF)
        rest_ref[:, at] = value[0 : 3 * chunk]
        far_ref[:, at] = value[3 * chunk : 4 * chunk]
        rest_out_ref[:, at] = value[4 * chunk : 7 * chunk]
        far_out_ref[:, at] = value[7 * chunk :]

    tiles = ff // TILE

    @pl.when(target == 0)
    def _():
        @pl.loop(0, tiles)
        def _(j):
            at = pl.ds(pl.multiple_of(j * TILE, TILE), TILE)
            store(0, j, dot(rows_ref[...], gate_ref[:, at]))
            store(1, j, dot(rows_ref[...], up_ref[:, at]))
            store(2, j, dot(grads_ref[...], down_ref[:, at]))

    @pl.when(target == 1)
    def _():
        n = s0.shape[0] // ny
        for k, sources in enumerate(((s0, t0), (s1, t1), (s2, t2), (s3, t3))):
            for other in range(nz):
                x = lax.rem(my_x - k + nx, nx)
                z = 1 - my_z if other else my_z
                for y in range(ny):
                    to = pl.ds(pl.multiple_of(((x * ny + y) * nz + z) * n, n), n)
                    for m in range(3):
                        restored_ref[m, to, :] = sources[other][y * n : (y + 1) * n, m * feat : (m + 1) * feat]

        @pl.loop(0, tiles)
        def _(j):
            at = pl.ds(pl.multiple_of(j * TILE, TILE), TILE)
            store(0, j, dot(rows_ref[...], restored_ref[0, at, :], NT))
            store(1, j, dot(rows_ref[...], restored_ref[1, at, :], NT))
            store(2, j, dot(grads_ref[...], restored_ref[2, at, :], NT))


def merge_kernel(at, low, own_ref, other_ref, arrived_ref, out_ref):
    rows, width = out_ref.shape
    mid = arrived_ref.shape[0]

    @pl.loop(0, width // TILE)
    def _(j):
        lanes = pl.ds(pl.multiple_of(j * TILE, TILE), TILE)
        value = own_ref[at : at + rows, lanes].astype(F32) + other_ref[at : at + rows, lanes].astype(F32)
        more = arrived_ref[:, lanes].astype(F32)
        none = jnp.zeros((rows - mid, TILE), F32)
        value = value + jnp.concatenate([more, none] if low else [none, more], axis=0)
        out_ref[:, lanes] = value.astype(BF)


def activate_kernel(own_ref, other_ref, left_ref, right_ref, out_ref):
    ff = out_ref.shape[1] // 3
    rows = out_ref.shape[0]

    @pl.loop(0, ff // TILE)
    def _(j):
        def total(k):
            at = pl.ds(pl.multiple_of(k * ff + j * TILE, TILE), TILE)
            near = own_ref[0:rows, at].astype(F32) + other_ref[0:rows, at].astype(F32)
            return near + (left_ref[:, at].astype(F32) + right_ref[:, at].astype(F32))

        gate, up, dh = total(0), total(1), total(2)
        sig = jax.nn.sigmoid(gate)
        values = (
            gate * sig * up,
            dh * up * sig * (1.0 + gate * (1.0 - sig)),
            dh * gate * sig,
        )
        for k, value in enumerate(values):
            at = pl.ds(pl.multiple_of(k * ff + j * TILE, TILE), TILE)
            out_ref[:, at] = value.astype(BF)


def back_kernel(*refs):
    who_ref, parts = refs[0], refs[1:3]
    gate_ref, up_ref, down_ref, restored_ref, out_ref, grads_ref, hidden_ref, y_ref, dx_ref = refs[3:]
    feat, ff = gate_ref.shape
    chunk = out_ref.shape[1]
    target, h, c = who_ref[0], who_ref[1], who_ref[2]
    for k, part in enumerate(parts):
        span = slice(4 * chunk * k, 4 * chunk * (k + 1))
        hidden_ref[span, :] = part[:, 0:ff]
        grads_ref[span, :] = part[:, ff : 3 * ff]

    @pl.when(target == 0)
    def _():
        y_ref[...] = dot(hidden_ref[...], down_ref[...], NT).astype(BF)
        dx_ref[...] = (
            dot(grads_ref[:, 0:ff], gate_ref[...], NT) + dot(grads_ref[:, ff : 2 * ff], up_ref[...], NT)
        ).astype(BF)

    @pl.when(target == 1)
    def _():
        y_ref[...] = dot(hidden_ref[...], restored_ref[2]).astype(BF)
        dx_ref[...] = (
            dot(grads_ref[:, 0:ff], restored_ref[0]) + dot(grads_ref[:, ff : 2 * ff], restored_ref[1])
        ).astype(BF)

    for p in range(8):
        g = chunk_at(h, c, p)
        span = slice(p * chunk, (p + 1) * chunk)
        out_ref[g, :, 0:feat] = y_ref[span, :]
        out_ref[g, :, feat : 2 * feat] = dx_ref[span, :]


def combine_kernel(recv_ref, meta_ref, want_ref, out_ref, pick_ref, share_ref):
    nxz, out_rows, width = recv_ref.shape
    feat = width // 2
    total = nxz * out_rows
    for q in range(nxz):
        span = pl.ds(q * out_rows, out_rows)
        pick_ref[span, :], share_ref[0, span, :], share_ref[1, span, :] = tables(
            meta_ref, want_ref[...], q, nxz
        )
    rows = recv_ref[...].reshape(total, width)
    y = dot(share_ref[0], rows[:, 0:feat], TN) + dot(share_ref[1], rows[:, 0:feat], TN)
    out_ref[:, 0:feat] = y.astype(BF)
    out_ref[:, feat:width] = dot(pick_ref[...], rows[:, feat:width], TN).astype(BF)


def finish_kernel(recv_ref, out_ref, grad_ref):
    feat = out_ref.shape[1]
    total = jnp.sum(recv_ref[...].astype(F32), axis=0)
    out_ref[...] = total[:, 0:feat].astype(BF)
    grad_ref[...] = total[:, feat : 2 * feat].astype(BF)


def core_swap(x):
    return lax.ppermute(x, "dp", [(i, i ^ 1) for i in range(8)])


def shift(x, k):
    return lax.ppermute(
        x, "dp", [(2 * h + c, 2 * ((h + k) % 4) + c) for h in range(4) for c in range(2)]
    )


def add(a, b):
    return (a.astype(F32) + b.astype(F32)).astype(BF)


def body(
    tokens,
    cotangent,
    expert_ids,
    route_weight,
    replaced,
    gate_weight,
    up_weight,
    down_weight,
    backup,
):
    ranks = lax.axis_size("expert")
    grid = nx, ny, nz = GRID[ranks]
    nxz = nx * nz
    along_y = [
        [(x * ny + y) * nz + z for y in range(ny)] for x in range(nx) for z in range(nz)
    ]
    along_xz = [
        [(x * ny + y) * nz + z for x in range(nx) for z in range(nz)] for y in range(ny)
    ]

    def exchange(v, groups):
        flat = v.reshape(-1, v.shape[-1])
        flat = lax.all_to_all(flat, "expert", 0, 0, axis_index_groups=groups, tiled=True)
        return flat.reshape(v.shape)

    def rank(x, y, z):
        return ((x % nx) * ny + y) * nz + z % nz

    def step(v, dx, dz):
        pairs = [
            (rank(x, y, z), rank(x + dx, y, z + dz))
            for x in range(nx) for y in range(ny) for z in range(nz)
        ]
        return lax.ppermute(v, "expert", pairs)

    tok, topk = expert_ids.shape
    feat = tokens.shape[1]
    ff = gate_weight.shape[2]
    ffr = ff // ranks
    capacity = min(tok, 5 * tok * topk // (2 * ranks))
    chunk = ranks * capacity // 8
    me, expert = lax.axis_index("dp"), lax.axis_index("expert")
    who = jnp.stack(
        [
            (expert == replaced[0]).astype(jnp.int32),
            me // 2,
            me % 2,
            expert // (ny * nz),
            expert % nz,
        ]
    ).astype(jnp.int32)

    saved = jnp.transpose(backup, (2, 0, 1)).reshape(ffr, 3 * feat)
    saved = jnp.pad(saved, ((0, 0), (0, -3 * feat % 128)))
    saved = exchange(jnp.broadcast_to(saved, (ny, *saved.shape)), along_y)
    saved = saved.reshape(ny * ffr, -1)
    (first,) = call(functools.partial(pack_kernel, grid), [(ny, tok, LANES)], operands=4)(
        expert_ids, route_weight, tokens, cotangent
    )
    first, saved = lax.optimization_barrier((first, saved))
    other_z = step(saved, 0, 1)
    before, after = step(saved, 1, 0), step(saved, -1, 0)
    first = exchange(first, along_y)
    first, other_z, before, after = lax.optimization_barrier((first, other_z, before, after))
    before_z, after_z = step(other_z, 1, 0), step(other_z, -1, 0)
    blocks = (
        saved, other_z, before, before_z, step(before, 1, 0), step(after_z, -1, 0), after, after_z,
    )

    out_rows, seen = ny * capacity, ny * tok
    row, col = np.arange(out_rows)[:, None], np.arange(seen)[None, :]
    want = np.where(row // capacity == col // tok, row % capacity, -2).astype(np.float32)
    send, meta = call(
        select_kernel, [(nxz, out_rows, 2 * feat), ((64, seen), F32)], operands=2
    )(first, want)
    recv = exchange(send, along_xz)

    w_gate, w_up, w_down = gate_weight[0], up_weight[0], jnp.transpose(down_weight[0])
    wide = 3 * ff
    rows, far, rest, far_out, rest_out, restored = call(
        functools.partial(products_kernel, grid),
        [
            (8 * chunk, feat), (chunk, wide), (3 * chunk, wide),
            (chunk, wide), (3 * chunk, wide), (3, ff, feat),
        ],
        scratch=[pltpu.VMEM((8 * chunk, feat), BF)],
        scalars=1,
        operands=12,
        megabytes=18,
    )(who, recv, *blocks, w_gate, w_up, w_down)

    mid = chunk // 2
    far = add(far, core_swap(far_out))
    rest_in = core_swap(rest_out)
    from_left, from_right = shift(far[:mid], 1), shift(far[mid:], -1)
    def merged(at, low, arrived):
        kernel = functools.partial(merge_kernel, at, low)
        return call(kernel, [(chunk, wide)], operands=3)(rest, rest_in, arrived)[0]

    from_left = shift(merged(chunk, True, from_left), 1)
    from_right = shift(merged(2 * chunk, False, from_right), -1)
    (own,) = call(activate_kernel, [(chunk, wide)], operands=4)(
        rest, rest_in, from_left, from_right
    )

    left, right = shift(own, 1), shift(own, -1)
    far = shift(left[:mid], 1), shift(right[mid:], -1)
    mine = jnp.concatenate([own, right, left, *far], axis=0)
    other = core_swap(mine)

    out, grads = call(
        back_kernel,
        [(8, chunk, 2 * feat), (8 * chunk, 2 * ff)],
        scratch=[
            pltpu.VMEM((8 * chunk, ff), BF),
            pltpu.VMEM((8 * chunk, feat), BF),
            pltpu.VMEM((8 * chunk, feat), BF),
        ],
        scalars=1,
        operands=6,
        megabytes=18,
    )(who, mine, other, w_gate, w_up, w_down, restored)

    out = exchange(out.reshape(nxz, out_rows, 2 * feat), along_xz)
    gate_grad = dot(rows, grads[:, :ff], TN).astype(BF)
    up_grad = dot(rows, grads[:, ff:], TN).astype(BF)
    (part,) = call(
        combine_kernel,
        [(seen, 2 * feat)],
        scratch=[
            pltpu.VMEM((nxz * out_rows, seen), BF),
            pltpu.VMEM((2, nxz * out_rows, seen), BF),
        ],
        operands=3,
    )(out, meta, want)
    part = exchange(part.reshape(ny, tok, 2 * feat), along_y)
    combined, token_grad = call(finish_kernel, [(tok, feat), (tok, feat)], operands=1)(part)
    return (combined, token_grad, gate_grad[None], up_grad[None])


def solution(mesh):
    placed = (
        P("expert", "dp"),
        P("expert", "dp"),
        P("expert", None),
        P("expert", None),
        P(),
        P("expert", "dp", None),
        P("expert", "dp", None),
        P("expert", None, "dp"),
        P(None, "dp", "expert"),
    )
    return jax.shard_map(
        body,
        mesh=mesh,
        in_specs=placed,
        out_specs=(
            P("expert", "dp"),
            P("expert", "dp"),
            P("expert", "dp", None),
            P("expert", "dp", None),
        ),
        check_vma=False,
    )
```

```python
import functools

import jax
import jax.numpy as jnp
import numpy as np
from jax import lax
from jax.experimental import pallas as pl
from jax.experimental.pallas import tpu as pltpu
from jax.sharding import PartitionSpec as P

BF = jnp.bfloat16
F32 = jnp.float32
GRID = {64: (4, 8, 2), 8: (2, 2, 2)}
NN = (((1,), (0,)), ((), ()))
NT = (((1,), (1,)), ((), ()))
TN = (((0,), (0,)), ((), ()))
LANES = 1024
TILE = 256


def dot(a, b, dims=NN):
    return lax.dot_general(a, b, dims, preferred_element_type=F32)


def call(kernel, outs, scratch=(), scalars=0, operands=0, megabytes=32):
    def of(shape, dtype=BF):
        return jax.ShapeDtypeStruct(shape, dtype)

    specs = [pl.BlockSpec(memory_space=pltpu.SMEM)] * scalars
    specs += [pl.BlockSpec(memory_space=pltpu.VMEM)] * operands
    return pl.pallas_call(
        kernel,
        out_shape=[of(*s) if isinstance(s[0], tuple) else of(s) for s in outs],
        in_specs=specs,
        out_specs=[pl.BlockSpec(memory_space=pltpu.VMEM)] * len(outs),
        scratch_shapes=list(scratch),
        compiler_params=pltpu.CompilerParams(vmem_limit_bytes=megabytes << 20),
    )


def pack_kernel(grid, ids_ref, weight_ref, tok_ref, cot_ref, out_ref):
    nx, ny, nz = grid
    nxz, ranks = nx * nz, nx * ny * nz
    tok, topk = ids_ref.shape
    ids = ids_ref[...]
    x, y, z = lax.div(ids, ny * nz), lax.rem(lax.div(ids, nz), ny), lax.rem(ids, nz)
    column = y * nxz + x * nz + z
    lane = lax.broadcasted_iota(jnp.int32, (tok, ranks), 1)
    member = jnp.zeros((tok, ranks), F32)
    share = jnp.zeros((tok, ranks), F32)
    for k in range(topk):
        same = column[:, k : k + 1] == lane
        member = member + jnp.where(same, 1.0, 0.0)
        share = share + jnp.where(same, weight_ref[:, k : k + 1], 0.0)
    row = lax.broadcasted_iota(jnp.int32, (tok, tok), 0)
    col = lax.broadcasted_iota(jnp.int32, (tok, tok), 1)
    before = dot(jnp.where(col <= row, 1.0, 0.0).astype(BF), member.astype(BF))
    place = jnp.where(member > 0.5, before - 1.0, -1.0).astype(BF)
    hi = share.astype(BF)
    lo = (share - hi.astype(F32)).astype(BF)
    source = lax.broadcasted_iota(jnp.int32, (ranks, ny * 128), 0)
    target = lax.broadcasted_iota(jnp.int32, (ranks, ny * 128), 1)
    base = lax.div(source, nxz) * 128 + lax.rem(source, nxz) + 64
    meta = jnp.zeros((tok, ny * 128), F32)
    for k, part in enumerate((place, hi, lo)):
        meta = meta + dot(part, jnp.where(target == base + k * nxz, 1.0, 0.0).astype(BF))
    feat = tok_ref.shape[1]
    assert feat == 448
    last = jnp.concatenate([tok_ref[:, 384:448].astype(F32), jnp.zeros((tok, 64), F32)], axis=1)
    for i in range(ny):
        out_ref[i, :, 0:384] = tok_ref[:, 0:384]
        out_ref[i, :, 384:512] = (meta[:, i * 128 : (i + 1) * 128] + last).astype(BF)
        out_ref[i, :, 512 : 512 + feat] = cot_ref[...]


def tables(meta_ref, want, q, count):
    hit = meta_ref[q : q + 1, :] == want
    hi = jnp.where(hit, meta_ref[count + q : count + q + 1, :], 0.0).astype(BF)
    lo = jnp.where(hit, meta_ref[2 * count + q : 2 * count + q + 1, :], 0.0).astype(BF)
    return jnp.where(hit, 1.0, 0.0).astype(BF), hi, lo


def select_kernel(first_ref, want_ref, out_ref, meta_ref):
    nxz, rows, width = out_ref.shape
    feat = width // 2
    ny, tok, _ = first_ref.shape
    seen = ny * tok
    tokens = first_ref[:, :, 0:feat].reshape(seen, feat)
    cots = first_ref[:, :, 512 : 512 + feat].reshape(seen, feat)
    meta = jnp.transpose(first_ref[:, :, 384:512].reshape(seen, 128).astype(F32))
    meta_ref[...] = meta[64:128]
    want = want_ref[...]
    both = jnp.concatenate([cots, cots], axis=0)
    for q in range(nxz):
        pick, hi, lo = tables(meta_ref, want, q, nxz)
        out_ref[q, :, 0:feat] = dot(pick, tokens).astype(BF)
        out_ref[q, :, feat:width] = dot(jnp.concatenate([hi, lo], axis=1), both).astype(BF)


def chunk_at(h, c, p):
    half = c if p < 4 else 1 - c
    return half * 4 + lax.rem(h + (0, 1, 3, 2)[p % 4], 4)


def products_kernel(
    grid, who_ref, recv_ref, s0, t0, s1, t1, s2, t2, s3, t3, gate_ref, up_ref, down_ref,
    rows_ref, far_ref, rest_ref, far_out_ref, rest_out_ref, restored_ref, grads_ref,
):
    nx, ny, nz = grid
    feat, ff = gate_ref.shape
    chunk = far_ref.shape[0]
    target, h, c, my_x, my_z = (who_ref[i] for i in range(5))
    for p in range(8):
        g = chunk_at(h, c, p)
        rows_ref[p * chunk : (p + 1) * chunk, :] = recv_ref[g, :, 0:feat]
        grads_ref[p * chunk : (p + 1) * chunk, :] = recv_ref[g, :, feat : 2 * feat]

    def store(k, j, value):
        at = pl.ds(pl.multiple_of(k * ff + j * TILE, TILE), TILE)
        value = value.astype(BF)
        rest_ref[:, at] = value[0 : 3 * chunk]
        far_ref[:, at] = value[3 * chunk : 4 * chunk]
        rest_out_ref[:, at] = value[4 * chunk : 7 * chunk]
        far_out_ref[:, at] = value[7 * chunk :]

    tiles = ff // TILE

    @pl.when(target == 0)
    def _():
        @pl.loop(0, tiles)
        def _(j):
            at = pl.ds(pl.multiple_of(j * TILE, TILE), TILE)
            store(0, j, dot(rows_ref[...], gate_ref[:, at]))
            store(1, j, dot(rows_ref[...], up_ref[:, at]))
            store(2, j, dot(grads_ref[...], down_ref[:, at]))

    @pl.when(target == 1)
    def _():
        n = s0.shape[0] // ny
        for k, sources in enumerate(((s0, t0), (s1, t1), (s2, t2), (s3, t3))):
            for other in range(nz):
                x = lax.rem(my_x - k + nx, nx)
                z = 1 - my_z if other else my_z
                for y in range(ny):
                    to = pl.ds(pl.multiple_of(((x * ny + y) * nz + z) * n, n), n)
                    for m in range(3):
                        restored_ref[m, to, :] = sources[other][y * n : (y + 1) * n, m * feat : (m + 1) * feat]

        @pl.loop(0, tiles)
        def _(j):
            at = pl.ds(pl.multiple_of(j * TILE, TILE), TILE)
            store(0, j, dot(rows_ref[...], restored_ref[0, at, :], NT))
            store(1, j, dot(rows_ref[...], restored_ref[1, at, :], NT))
            store(2, j, dot(grads_ref[...], restored_ref[2, at, :], NT))


def activate_kernel(own_ref, other_ref, left_ref, right_ref, out_ref):
    ff = out_ref.shape[1] // 3
    rows = out_ref.shape[0]

    @pl.loop(0, ff // TILE)
    def _(j):
        def total(k):
            at = pl.ds(pl.multiple_of(k * ff + j * TILE, TILE), TILE)
            near = own_ref[0:rows, at].astype(F32) + other_ref[0:rows, at].astype(F32)
            return near + (left_ref[:, at].astype(F32) + right_ref[:, at].astype(F32))

        gate, up, dh = total(0), total(1), total(2)
        sig = jax.nn.sigmoid(gate)
        values = (
            gate * sig * up,
            dh * up * sig * (1.0 + gate * (1.0 - sig)),
            dh * gate * sig,
        )
        for k, value in enumerate(values):
            at = pl.ds(pl.multiple_of(k * ff + j * TILE, TILE), TILE)
            out_ref[:, at] = value.astype(BF)


def back_kernel(who_ref, part_ref, gate_ref, up_ref, down_ref, restored_ref, y_ref, dx_ref):
    ff = gate_ref.shape[1]

    @pl.when(who_ref[0] == 0)
    def _():
        y_ref[...] = dot(part_ref[:, 0:ff], down_ref[...], NT).astype(BF)
        dx = dot(part_ref[:, ff : 2 * ff], gate_ref[...], NT)
        dx_ref[...] = (dx + dot(part_ref[:, 2 * ff : 3 * ff], up_ref[...], NT)).astype(BF)

    @pl.when(who_ref[0] == 1)
    def _():
        y_ref[...] = dot(part_ref[:, 0:ff], restored_ref[2]).astype(BF)
        dx = dot(part_ref[:, ff : 2 * ff], restored_ref[0])
        dx_ref[...] = (dx + dot(part_ref[:, 2 * ff : 3 * ff], restored_ref[1])).astype(BF)


def last_back_kernel(
    who_ref, part_ref, gate_ref, up_ref, down_ref, restored_ref, own_y_ref, own_dx_ref,
    out_ref, y_ref, dx_ref,
):
    feat = gate_ref.shape[0]
    chunk = out_ref.shape[1]
    back_kernel(who_ref, part_ref, gate_ref, up_ref, down_ref, restored_ref, y_ref, dx_ref)
    for p in range(8):
        g = chunk_at(who_ref[1], who_ref[2], p)
        y, dx = (own_y_ref, own_dx_ref) if p < 4 else (y_ref, dx_ref)
        span = slice(p % 4 * chunk, (p % 4 + 1) * chunk)
        out_ref[g, :, 0:feat] = y[span, :]
        out_ref[g, :, feat : 2 * feat] = dx[span, :]


def combine_kernel(recv_ref, meta_ref, want_ref, out_ref, pick_ref, share_ref):
    nxz, out_rows, width = recv_ref.shape
    feat = width // 2
    total = nxz * out_rows
    for q in range(nxz):
        span = pl.ds(q * out_rows, out_rows)
        pick_ref[span, :], share_ref[0, span, :], share_ref[1, span, :] = tables(
            meta_ref, want_ref[...], q, nxz
        )
    rows = recv_ref[...].reshape(total, width)
    y = dot(share_ref[0], rows[:, 0:feat], TN) + dot(share_ref[1], rows[:, 0:feat], TN)
    out_ref[:, 0:feat] = y.astype(BF)
    out_ref[:, feat:width] = dot(pick_ref[...], rows[:, feat:width], TN).astype(BF)


def finish_kernel(recv_ref, out_ref, grad_ref):
    feat = out_ref.shape[1]
    total = jnp.sum(recv_ref[...].astype(F32), axis=0)
    out_ref[...] = total[:, 0:feat].astype(BF)
    grad_ref[...] = total[:, feat : 2 * feat].astype(BF)


def core_swap(x):
    return lax.ppermute(x, "dp", [(i, i ^ 1) for i in range(8)])


def shift(x, k):
    return lax.ppermute(
        x, "dp", [(2 * h + c, 2 * ((h + k) % 4) + c) for h in range(4) for c in range(2)]
    )


def add(a, b):
    return (a.astype(F32) + b.astype(F32)).astype(BF)


def body(
    tokens,
    cotangent,
    expert_ids,
    route_weight,
    replaced,
    gate_weight,
    up_weight,
    down_weight,
    backup,
):
    ranks = lax.axis_size("expert")
    grid = nx, ny, nz = GRID[ranks]
    nxz = nx * nz
    along_y = [
        [(x * ny + y) * nz + z for y in range(ny)] for x in range(nx) for z in range(nz)
    ]
    along_xz = [
        [(x * ny + y) * nz + z for x in range(nx) for z in range(nz)] for y in range(ny)
    ]

    def exchange(v, groups):
        flat = v.reshape(-1, v.shape[-1])
        flat = lax.all_to_all(flat, "expert", 0, 0, axis_index_groups=groups, tiled=True)
        return flat.reshape(v.shape)

    def rank(x, y, z):
        return ((x % nx) * ny + y) * nz + z % nz

    def step(v, dx, dz):
        pairs = [
            (rank(x, y, z), rank(x + dx, y, z + dz))
            for x in range(nx) for y in range(ny) for z in range(nz)
        ]
        return lax.ppermute(v, "expert", pairs)

    tok, topk = expert_ids.shape
    feat = tokens.shape[1]
    ff = gate_weight.shape[2]
    ffr = ff // ranks
    capacity = min(tok, 5 * tok * topk // (2 * ranks))
    chunk = ranks * capacity // 8
    me, expert = lax.axis_index("dp"), lax.axis_index("expert")
    who = jnp.stack(
        [
            (expert == replaced[0]).astype(jnp.int32),
            me // 2,
            me % 2,
            expert // (ny * nz),
            expert % nz,
        ]
    ).astype(jnp.int32)

    saved = jnp.transpose(backup, (2, 0, 1)).reshape(ffr, 3 * feat)
    saved = jnp.pad(saved, ((0, 0), (0, -3 * feat % 128)))
    saved = exchange(jnp.broadcast_to(saved, (ny, *saved.shape)), along_y)
    saved = saved.reshape(ny * ffr, -1)
    (first,) = call(functools.partial(pack_kernel, grid), [(ny, tok, LANES)], operands=4)(
        expert_ids, route_weight, tokens, cotangent
    )
    first, saved = lax.optimization_barrier((first, saved))
    other_z = step(saved, 0, 1)
    before, after = step(saved, 1, 0), step(saved, -1, 0)
    first = exchange(first, along_y)
    first, other_z, before, after = lax.optimization_barrier((first, other_z, before, after))
    before_z, after_z = step(other_z, 1, 0), step(other_z, -1, 0)
    blocks = (
        saved, other_z, before, before_z, step(before, 1, 0), step(after_z, -1, 0), after, after_z,
    )

    out_rows, seen = ny * capacity, ny * tok
    row, col = np.arange(out_rows)[:, None], np.arange(seen)[None, :]
    want = np.where(row // capacity == col // tok, row % capacity, -2).astype(np.float32)
    send, meta = call(
        select_kernel, [(nxz, out_rows, 2 * feat), ((64, seen), F32)], operands=2
    )(first, want)
    recv = exchange(send, along_xz)

    w_gate, w_up, w_down = gate_weight[0], up_weight[0], jnp.transpose(down_weight[0])
    wide = 3 * ff
    rows, far, rest, far_out, rest_out, restored = call(
        functools.partial(products_kernel, grid),
        [
            (8 * chunk, feat), (chunk, wide), (3 * chunk, wide),
            (chunk, wide), (3 * chunk, wide), (3, ff, feat),
        ],
        scratch=[pltpu.VMEM((8 * chunk, feat), BF)],
        scalars=1,
        operands=12,
        megabytes=18,
    )(who, recv, *blocks, w_gate, w_up, w_down)

    mid = chunk // 2
    far = add(far, core_swap(far_out))
    rest_in = core_swap(rest_out)
    from_left, from_right = shift(far[:mid], 1), shift(far[mid:], -1)
    sides = add(rest[chunk:], rest_in[chunk:])
    right, left = sides[:chunk], sides[chunk:]
    right = jnp.concatenate([add(right[:mid], from_left), right[mid:]], axis=0)
    left = jnp.concatenate([left[:mid], add(left[mid:], from_right)], axis=0)
    from_left, from_right = shift(right, 1), shift(left, -1)
    (own,) = call(activate_kernel, [(chunk, wide)], operands=4)(
        rest, rest_in, from_left, from_right
    )

    left, right = shift(own, 1), shift(own, -1)
    far = shift(left[:mid], 1), shift(right[mid:], -1)
    mine = jnp.concatenate([own, right, left, *far], axis=0)
    other = core_swap(mine)

    weights = w_gate, w_up, w_down, restored
    half = (4 * chunk, feat)
    own_back = call(back_kernel, [half, half], scalars=1, operands=5, megabytes=18)(who, mine, *weights)
    (out,) = call(
        last_back_kernel,
        [(8, chunk, 2 * feat)],
        scratch=[pltpu.VMEM(half, BF), pltpu.VMEM(half, BF)],
        scalars=1,
        operands=7,
        megabytes=18,
    )(who, other, *weights, *own_back)

    out = exchange(out.reshape(nxz, out_rows, 2 * feat), along_xz)
    halves = (rows[: 4 * chunk], mine), (rows[4 * chunk :], other)
    gate_grad, up_grad = (
        sum(dot(r, d[:, k : k + ff], TN) for r, d in halves).astype(BF) for k in (ff, 2 * ff)
    )
    (part,) = call(
        combine_kernel,
        [(seen, 2 * feat)],
        scratch=[
            pltpu.VMEM((nxz * out_rows, seen), BF),
            pltpu.VMEM((2, nxz * out_rows, seen), BF),
        ],
        operands=3,
    )(out, meta, want)
    part = exchange(part.reshape(ny, tok, 2 * feat), along_y)
    combined, token_grad = call(finish_kernel, [(tok, feat), (tok, feat)], operands=1)(part)
    return (combined, token_grad, gate_grad[None], up_grad[None])


def solution(mesh):
    placed = (
        P("expert", "dp"),
        P("expert", "dp"),
        P("expert", None),
        P("expert", None),
        P(),
        P("expert", "dp", None),
        P("expert", "dp", None),
        P("expert", None, "dp"),
        P(None, "dp", "expert"),
    )
    return jax.shard_map(
        body,
        mesh=mesh,
        in_specs=placed,
        out_specs=(
            P("expert", "dp"),
            P("expert", "dp"),
            P("expert", "dp", None),
            P("expert", "dp", None),
        ),
        check_vma=False,
    )
```
